512 devices in a mesh: gx: 8 (over y_lo, core), gy: 8 (over z), gz: 8 (over y_hi, x).
Axes of the slice: x: 4, y: 8 (y_hi: 2, y_lo: 4; y = y_hi * 4 + y_lo), z: 8, core: 2. Of those that a mesh axis runs over, the one named last changes fastest.
Arguments:
- tokens: bfloat16 [1024, 8192], P('gx', ('gz', 'gy')), may hold values from -6 to 6
- gate_weight: bfloat16 [14336, 8192], P(('gy', 'gx'), 'gz'), may hold values from -0.0625 to 0.0625
- up_weight: bfloat16 [14336, 8192], P(('gy', 'gx'), 'gz'), may hold values from -0.0625 to 0.0625
- down_weight: bfloat16 [14336, 8192], P(('gy', 'gx'), 'gz'), may hold values from -0.046875 to 0.046875
- reward_head: bfloat16 [8192], P(('gz', 'gy')), may hold values from -0.0625 to 0.0625
- lm_grad: float32 [1024, 8192], P('gx', ('gz', 'gy')), may hold values from -6 to 6
- pair_index: int32 [4, 2], replicated, may hold values from 0 to 7, as said below
Outputs:
- grad_tokens: float32 [1024, 8192], P('gx', ('gz', 'gy'))
- grad_gate: float32 [14336, 8192], P(('gy', 'gx'), 'gz')
- grad_up: float32 [14336, 8192], P(('gy', 'gx'), 'gz')
- grad_down: float32 [14336, 8192], P(('gy', 'gx'), 'gz')
- rewards: float32 [8], replicated
The draws below stay inside these ranges and needn't reach their ends.
Inputs may be any that keep to these rules, and one draw needn't show every extreme that they name: Every sequence number of 0 to 7 stands exactly once in pair_index.
All inputs are finite; a program needn't handle non-finite values.
Results may differ from the reference program's by a relative error of at most 0.008.
Values may be sent and summed in bfloat16 or wider, within the bound.
No kernel may reach another device: no remote copies, remote signals or barrier semaphores. Data moves between devices by JAX's collectives and lax.ppermute only.
A program may use at most 64 MiB of HBM per device.

```python
import jax
import jax.numpy as jnp
from jax import lax

D = 8192
FF = 14336
SEQ_LEN = 128
TOKENS = 1024
SEQS = 8
PAIRS = 4


def draw_pair_index(key, part):
    key = jax.random.fold_in(key, 7)
    order = jax.random.permutation(key, SEQS)
    return order.reshape(PAIRS, 2).astype(jnp.int32)


def levels(stream_key, dims, split, smallest, high):
    def one(axis_at, parts):
        draws = jax.random.uniform(jax.random.fold_in(jax.random.fold_in(stream_key, 6), axis_at), (parts,), jnp.float32, smallest / len(split), high / len(split))
        return jnp.repeat(jnp.exp(draws), dims[axis_at] // parts).reshape((-1,) + (1,) * (len(dims) - axis_at - 1))

    level = one(*split[0])
    for cut in split[1:]:
        level = level * one(*cut)
    return level


def normal_values(key, dims, scale, reach, split=(), held_as=jnp.bfloat16):
    array = jax.random.normal(key, dims, jnp.float32) * scale
    if len(split) > 0:
        array = levels(key, dims, split, -0.22, 0.18) * array
    return jnp.clip(array, min=-reach, max=reach).astype(held_as)


def setup_inputs(seed: int = 0) -> dict:
    streams_of = jax.random.split(jax.random.key(seed), 8)
    return {
        "tokens": normal_values(streams_of[0], (TOKENS, D), 1.0, 6.0, ((0, 8), (1, 64))),
        "gate_weight": normal_values(streams_of[1], (FF, D), D ** -0.5, 0.0625, ((0, 64), (1, 8))),
        "up_weight": normal_values(streams_of[2], (FF, D), D ** -0.5, 0.0625, ((0, 64), (1, 8))),
        "down_weight": normal_values(streams_of[3], (FF, D), FF ** -0.5, 0.046875, ((0, 64), (1, 8))),
        "reward_head": normal_values(streams_of[4], (D,), D ** -0.5, 0.0625, ((0, 64),)),
        "lm_grad": normal_values(streams_of[5], (TOKENS, D), 1.0, 6.0, ((0, 8), (1, 64)), jnp.float32),
        "pair_index": draw_pair_index(jax.random.fold_in(streams_of[7], 71), 0),
    }


reward_weight = 64.0

def reference(tokens, gate_weight, up_weight, down_weight, reward_head, lm_grad, pair_index):
    gate_sum = jnp.dot(tokens, gate_weight.T, preferred_element_type=jnp.float32)
    up_sum = jnp.dot(tokens, up_weight.T, preferred_element_type=jnp.float32)
    gate_sigmoid = jax.nn.sigmoid(gate_sum)
    silu_gate = gate_sum * gate_sigmoid
    hidden = (silu_gate * up_sum).astype(jnp.bfloat16)
    ffn_out = jnp.dot(hidden, down_weight, preferred_element_type=jnp.float32)
    block_out = tokens.astype(jnp.float32) + ffn_out
    head_vec = reward_head.astype(jnp.float32)
    last_rows = block_out.reshape(SEQS, SEQ_LEN, D)[:, SEQ_LEN - 1, :]
    rewards = lax.optimization_barrier(jnp.sum(last_rows * head_vec[None, :], axis=1))
    sequence = jnp.arange(SEQS, dtype=jnp.int32)
    chosen_hot = (pair_index[:, 0:1] == sequence[None, :]).astype(jnp.float32)
    rejected_hot = (pair_index[:, 1:2] == sequence[None, :]).astype(jnp.float32)
    margin = lax.optimization_barrier(jnp.sum(chosen_hot * rewards[None, :], axis=1)) - lax.optimization_barrier(jnp.sum(rejected_hot * rewards[None, :], axis=1))
    pair_weight = jax.nn.sigmoid(-margin)
    pair_coefs = lax.optimization_barrier(jnp.sum((rejected_hot - chosen_hot) * pair_weight[:, None], axis=0))
    head_term = reward_weight * pair_coefs[:, None] * head_vec[None, :]
    grad_out = lm_grad.reshape(SEQS, SEQ_LEN, D).at[:, SEQ_LEN - 1, :].add(head_term).reshape(TOKENS, D)
    grad_low = grad_out.astype(jnp.bfloat16)
    hidden_grad = jnp.dot(grad_low, down_weight.T, preferred_element_type=jnp.float32)
    up_grad = (hidden_grad * silu_gate).astype(jnp.bfloat16)
    gate_grad = (hidden_grad * up_sum * gate_sigmoid * (1.0 + gate_sum * (1.0 - gate_sigmoid))).astype(jnp.bfloat16)
    grad_tokens = grad_out + jnp.dot(gate_grad, gate_weight, preferred_element_type=jnp.float32) + jnp.dot(up_grad, up_weight, preferred_element_type=jnp.float32)
    loss_scale = 1.0 / jnp.sqrt(jnp.float32(TOKENS))
    grad_gate = jnp.dot(gate_grad.T, tokens, preferred_element_type=jnp.float32) * loss_scale
    grad_up = jnp.dot(up_grad.T, tokens, preferred_element_type=jnp.float32) * loss_scale
    grad_down = jnp.dot(hidden.T, grad_low, preferred_element_type=jnp.float32) * loss_scale
    return (grad_tokens, grad_gate, grad_up, grad_down, rewards)
```

```python
import jax
import jax.numpy as jnp
from jax import lax
from jax.sharding import Mesh, PartitionSpec as P

SEQ_LEN = 128
reward_weight = 64.0
EVERY = ("yl", "co", "gy", "yh", "xx")
PLANE = ("yl", "gy")
GZ = ("yh", "xx")
SWAP = [(0, 1), (1, 0)]
f32, bf16 = jnp.float32, jnp.bfloat16


def exchange(pieces, axes):
    return lax.all_to_all(pieces, axes, 0, 0)


def to_all(value, axes, count):
    return exchange(jnp.broadcast_to(value[None], (count,) + value.shape), axes)


def dot(left, right, left_dim, right_dim):
    return lax.dot_general(
        left, right, (((left_dim,), (right_dim,)), ((), ())), preferred_element_type=f32
    )


def body(tokens, gate_weight, up_weight, down_weight, reward_head, lm_grad, pair_index):
    n_yl, n_gy = lax.axis_size("yl"), lax.axis_size("gy")
    n_plane, n_gz = n_yl * n_gy, lax.axis_size(GZ)
    n_all = n_plane * n_gz * lax.axis_size("co")
    rows, cols = tokens.shape
    units, width = gate_weight.shape
    my_seq = lax.axis_index(("yl", "co"))
    core = lax.axis_index("co")

    def chip_block(weight):
        return jnp.concatenate([weight, lax.ppermute(weight, "co", SWAP)], axis=0)

    gate_w, up_w, down_w = chip_block(gate_weight), chip_block(up_weight), chip_block(down_weight)

    head_rows = jnp.pad(reward_head[None, :], ((0, 7), (0, 0)))
    block = jnp.concatenate([tokens, lm_grad.astype(bf16), head_rows], axis=0)
    got = to_all(block, PLANE, n_plane).reshape(n_yl, n_gy, 2 * rows + 8, cols)

    def spread(part):
        return part.transpose(0, 2, 1, 3).reshape(n_yl * rows, width)

    tok_half = spread(got[:, :, :rows])
    low_half = spread(got[:, :, rows : 2 * rows])
    head_vec = got[0, :, 2 * rows].reshape(1, width)
    half = n_yl * rows

    low_head = jnp.concatenate([low_half, jnp.pad(head_vec, ((0, 127), (0, 0)))], axis=0)
    gate_part = dot(gate_w, tok_half, 1, 1).astype(bf16)
    up_part = dot(up_w, tok_half, 1, 1).astype(bf16)
    back_part = dot(down_w, low_head, 1, 1)
    v_part = back_part[:, half : half + 1]
    v_hi = v_part.astype(bf16)
    v_mid = (v_part - v_hi.astype(f32)).astype(bf16)
    v_cols = jnp.pad(jnp.concatenate([v_hi, v_mid], axis=1), ((0, 0), (0, 126)))
    parts = jnp.concatenate([gate_part, up_part, back_part[:, :half].astype(bf16), v_cols], axis=1)
    own = 2 * units // n_gz
    sums = jnp.sum(exchange(parts.reshape(n_gz, own, 3 * half + 128), GZ).astype(f32), axis=0)
    gate_sum, up_sum, hidden_grad = (sums[:, i * half : (i + 1) * half] for i in range(3))
    head_down = sums[:, 3 * half : 3 * half + 1] + sums[:, 3 * half + 1 : 3 * half + 2]

    gate_sigmoid = jax.nn.sigmoid(gate_sum)
    silu_gate = gate_sum * gate_sigmoid
    hidden = (silu_gate * up_sum).astype(bf16)

    last_hidden = hidden.reshape(own, n_yl, rows)[:, :, rows - 1].astype(f32)
    seq_terms = jnp.sum(last_hidden * head_down, axis=0)
    own_term = jnp.sum(tokens[rows - 1].astype(f32) * reward_head.astype(f32))
    sequence = jnp.arange(2 * n_yl, dtype=jnp.int32)
    terms = jnp.where(sequence % 2 == core, jnp.repeat(seq_terms, 2), 0.0)
    terms = terms + jnp.where(sequence == my_seq, own_term, 0.0)
    term_row = jnp.pad(terms, (0, 128 - terms.shape[0]))[None, :]
    rewards = jnp.sum(to_all(term_row, EVERY, n_all), axis=(0, 1))[: 2 * n_yl]

    chosen_hot = (pair_index[:, 0:1] == sequence[None, :]).astype(f32)
    rejected_hot = (pair_index[:, 1:2] == sequence[None, :]).astype(f32)
    margin = jnp.sum((chosen_hot - rejected_hot) * rewards[None, :], axis=1)
    pair_weight = jax.nn.sigmoid(-margin)
    pair_coefs = jnp.sum((rejected_hot - chosen_hot) * pair_weight[:, None], axis=0)
    scaled = reward_weight * pair_coefs
    core_coefs = jnp.sum(
        jnp.where(sequence[:, None] == 2 * jnp.arange(n_yl)[None, :] + core, scaled[:, None], 0.0), axis=0
    )
    sib_coefs = jnp.sum(
        jnp.where(sequence[:, None] == 2 * jnp.arange(n_yl)[None, :] + 1 - core, scaled[:, None], 0.0), axis=0
    )
    my_coef = jnp.sum(jnp.where(sequence == my_seq, scaled, 0.0))

    def last_only(coefs):
        spot = jnp.arange(half)
        return jnp.where(spot % rows == rows - 1, jnp.repeat(coefs, rows), 0.0)

    hidden_grad = hidden_grad + head_down * last_only(core_coefs)[None, :]
    up_grad = (hidden_grad * silu_gate).astype(bf16)
    gate_grad = (
        hidden_grad * up_sum * gate_sigmoid * (1.0 + gate_sum * (1.0 - gate_sigmoid))
    ).astype(bf16)

    mine = jnp.concatenate([gate_grad, up_grad, hidden], axis=0)
    everyone = to_all(mine, GZ, n_gz)
    gate_g, up_g, hid = (
        everyone[:, i * own : (i + 1) * own].reshape(2 * units, half) for i in range(3)
    )

    token_part = dot(gate_g, gate_w, 0, 0) + dot(up_g, up_w, 0, 0)
    token_part = token_part.astype(bf16).reshape(n_yl, rows, n_gy, cols).transpose(0, 2, 1, 3)
    token_sum = jnp.sum(
        exchange(token_part.reshape(n_plane, rows, cols), PLANE).astype(f32), axis=0
    )
    head_own = reward_head.astype(f32)[None, :]
    row = jnp.arange(rows)[:, None]
    grad_out = lm_grad + jnp.where(row == rows - 1, my_coef * head_own, 0.0)
    grad_tokens = grad_out + token_sum

    loss_scale = 1.0 / jnp.sqrt(f32(rows * 2 * n_yl))
    head_full = head_vec.astype(f32)

    def cotangent(low, coefs):
        return (low.astype(f32) + last_only(coefs)[:, None] * head_full).astype(bf16)

    tok_sib = lax.ppermute(tok_half, "co", SWAP)
    low_sib = lax.ppermute(low_half, "co", SWAP)

    def weight_grad(full, own_right, sib_right):
        from_sib = lax.ppermute(full[units:], "co", SWAP)
        return (dot(full[:units], own_right, 1, 0) + dot(from_sib, sib_right, 1, 0)) * loss_scale

    grad_gate = weight_grad(gate_g, tok_half, tok_sib)
    grad_up = weight_grad(up_g, tok_half, tok_sib)
    grad_down = weight_grad(hid, cotangent(low_half, core_coefs), cotangent(low_sib, sib_coefs))
    return grad_tokens, grad_gate, grad_up, grad_down, rewards


def solution(mesh):
    fine = Mesh(mesh.devices.reshape(4, 2, 8, 2, 4), EVERY)
    gx, gz = ("yl", "co"), GZ
    weight = P(("gy",) + gx, gz)
    act = P(gx, gz + ("gy",))
    return jax.shard_map(
        body,
        mesh=fine,
        in_specs=(act, weight, weight, weight, P(gz + ("gy",)), act, P()),
        out_specs=(act, weight, weight, weight, P()),
        check_vma=False,
    )
```

```python
import jax
import jax.numpy as jnp
from jax import lax
from jax.sharding import Mesh, PartitionSpec as P

SEQ_LEN = 128
reward_weight = 64.0
FINE = ("yl", "co", "gy", "yh", "xx")
PLANE = ("yl", "gy")
GZ = ("yh", "xx")
SWAP = [(0, 1), (1, 0)]
f32, bf16 = jnp.float32, jnp.bfloat16


def exchange(pieces, axes):
    return lax.all_to_all(pieces, axes, 0, 0)


def to_all(value, axes, count):
    return exchange(jnp.broadcast_to(value[None], (count,) + value.shape), axes)


def dot(left, right, left_dim, right_dim):
    return lax.dot_general(
        left, right, (((left_dim,), (right_dim,)), ((), ())), preferred_element_type=f32
    )


def pieces(value):
    high = lax.reduce_precision(value, 8, 7)
    middle = lax.reduce_precision(value - high, 8, 7)
    return jnp.stack([high, middle, value - high - middle]).astype(bf16)


def body(tokens, gate_weight, up_weight, down_weight, reward_head, lm_grad, pair_index):
    n_yl, n_gy = lax.axis_size("yl"), lax.axis_size("gy")
    n_plane, n_gz = n_yl * n_gy, lax.axis_size(GZ)
    rows, cols = tokens.shape
    units, width = gate_weight.shape
    my_seq = lax.axis_index(("yl", "co"))
    core = lax.axis_index("co")

    def chip_block(weight):
        return jnp.concatenate([weight, lax.ppermute(weight, "co", SWAP)], axis=0)

    gate_w, up_w, down_w = chip_block(gate_weight), chip_block(up_weight), chip_block(down_weight)

    head_rows = jnp.broadcast_to(reward_head[None, :], (16, cols))
    block = jnp.concatenate([tokens, lm_grad.astype(bf16), head_rows], axis=0)
    block = to_all(block, "yl", n_yl)
    up, down = [block], [block]
    for step in range(n_gy // 2):
        up.append(lax.ppermute(up[-1], "gy", [(k, (k + 1) % n_gy) for k in range(n_gy)]))
        if step < n_gy // 2 - 1:
            down.append(lax.ppermute(down[-1], "gy", [(k, (k - 1) % n_gy) for k in range(n_gy)]))
    got = jnp.roll(jnp.stack(down + up[:0:-1]), lax.axis_index("gy"), axis=0)

    def spread(part):
        return part.transpose(1, 2, 0, 3).reshape(n_yl * rows, width)

    tok_half = spread(got[:, :, :rows])
    low_half = spread(got[:, :, rows : 2 * rows])
    head_vec = got[:, 0, 2 * rows].reshape(1, width)
    half = n_yl * rows

    low_head = jnp.concatenate([low_half, jnp.pad(head_vec, ((0, 127), (0, 0)))], axis=0)
    gate_part = dot(gate_w, tok_half, 1, 1).astype(bf16)
    up_part = dot(up_w, tok_half, 1, 1).astype(bf16)
    back_part = dot(down_w, low_head, 1, 1)
    v_part = back_part[:, half : half + 1]
    v_high = lax.reduce_precision(v_part, 8, 7)
    v_cols = jnp.concatenate([v_high, v_part - v_high], axis=1).astype(bf16)
    v_cols = jnp.pad(v_cols, ((0, 0), (0, 126)))
    parts = jnp.concatenate([gate_part, up_part, back_part[:, :half].astype(bf16), v_cols], axis=1)
    own = 2 * units // n_gz
    sums = jnp.sum(exchange(parts.reshape(n_gz, own, 3 * half + 128), GZ).astype(f32), axis=0)
    gate_sum, up_sum, hidden_grad = (sums[:, i * half : (i + 1) * half] for i in range(3))
    head_down = sums[:, 3 * half : 3 * half + 1] + sums[:, 3 * half + 1 : 3 * half + 2]

    gate_sigmoid = jax.nn.sigmoid(gate_sum)
    silu_gate = gate_sum * gate_sigmoid
    hidden = (silu_gate * up_sum).astype(bf16)

    gate_slope = up_sum * gate_sigmoid * (1.0 + gate_sum * (1.0 - gate_sigmoid))
    up_grad = (hidden_grad * silu_gate).astype(bf16)
    gate_grad = (hidden_grad * gate_slope).astype(bf16)

    def last_cols(value):
        return value.reshape(own, n_yl, rows)[:, :, rows - 1].astype(f32)

    gate_unit = (head_down * last_cols(gate_slope)).astype(bf16).T
    up_unit = (head_down * last_cols(silu_gate)).astype(bf16).T
    own_term = jnp.sum(tokens[rows - 1].astype(f32) * reward_head.astype(f32))
    terms = jnp.sum(last_cols(hidden) * head_down, axis=0)
    terms = terms + jnp.where(jnp.arange(n_yl) == lax.axis_index("yl"), own_term, 0.0)
    unit_rows = jnp.concatenate(
        [jnp.pad(gate_unit, ((0, 0), (0, 128 - own))), jnp.pad(up_unit, ((0, 0), (0, half - 128 - own)))], axis=1
    )
    term_rows = jnp.pad(pieces(terms).reshape(1, -1), ((0, 7 - n_yl), (0, half - 3 * n_yl)))
    mine = jnp.concatenate([gate_grad, up_grad, hidden, unit_rows, term_rows], axis=0)
    everyone = to_all(mine, GZ, n_gz)
    gate_g, up_g, hid = (
        everyone[:, i * own : (i + 1) * own].reshape(2 * units, half) for i in range(3)
    )
    units_at = everyone[:, 3 * own : 3 * own + n_yl].transpose(1, 0, 2)
    gate_u, up_u = (
        units_at[:, :, i * 128 : i * 128 + own].reshape(n_yl, 2 * units) for i in range(2)
    )
    core_terms = jnp.sum(
        everyone[:, 3 * own + n_yl, : 3 * n_yl].astype(f32).reshape(n_gz * 3, n_yl), axis=0
    )
    pair_terms = jnp.stack([core_terms, lax.ppermute(core_terms, "co", SWAP)])

    token_part = dot(gate_g, gate_w, 0, 0) + dot(up_g, up_w, 0, 0)
    token_part = token_part.astype(bf16).reshape(n_yl, rows, n_gy, cols).transpose(0, 2, 1, 3)
    unit_part = (dot(gate_u, gate_w, 1, 0) + dot(up_u, up_w, 1, 0)).astype(bf16)
    term_row = jnp.pad(pieces(pair_terms).reshape(1, 1, -1), ((0, 0), (0, 0), (0, cols - 6 * n_yl)))
    extra = jnp.concatenate(
        [unit_part.reshape(n_plane, 1, cols), jnp.broadcast_to(term_row, (n_plane, 1, cols))], axis=1
    )
    sent = jnp.concatenate(
        [token_part.reshape(n_plane, rows, cols), jnp.pad(extra, ((0, 0), (0, 6), (0, 0)))], axis=1
    )
    token_sum = jnp.sum(exchange(sent, PLANE).astype(f32), axis=0)

    both = jnp.sum(token_sum[rows + 1, : 6 * n_yl].reshape(3, 2, n_yl), axis=0)
    sequence = jnp.arange(2 * n_yl, dtype=jnp.int32)
    rewards = jnp.where(sequence % 2 == core, jnp.repeat(both[0], 2), jnp.repeat(both[1], 2))
    chosen_hot = (pair_index[:, 0:1] == sequence[None, :]).astype(f32)
    rejected_hot = (pair_index[:, 1:2] == sequence[None, :]).astype(f32)
    margin = jnp.sum((chosen_hot - rejected_hot) * rewards[None, :], axis=1)
    pair_weight = jax.nn.sigmoid(-margin)
    scaled = reward_weight * jnp.sum((rejected_hot - chosen_hot) * pair_weight[:, None], axis=0)
    by_core = scaled.reshape(n_yl, 2)
    core_coefs = jnp.where(core == 0, by_core[:, 0], by_core[:, 1])
    sib_coefs = jnp.where(core == 0, by_core[:, 1], by_core[:, 0])
    coefs = jnp.concatenate([core_coefs, sib_coefs])
    my_coef = jnp.sum(jnp.where(sequence == my_seq, scaled, 0.0))

    row = jnp.arange(rows)[:, None]
    head_term = my_coef * (reward_head.astype(f32) + token_sum[rows])
    grad_tokens = lm_grad + token_sum[:rows] + jnp.where(row == rows - 1, head_term[None, :], 0.0)

    loss_scale = 1.0 / jnp.sqrt(f32(rows * 2 * n_yl))
    tok_sib = lax.ppermute(tok_half, "co", SWAP)
    low_sib = lax.ppermute(low_half, "co", SWAP)
    unit_swap = lax.ppermute(jnp.concatenate([gate_u[:, units:], up_u[:, units:]], axis=0), "co", SWAP)
    gate_u8 = jnp.concatenate([gate_u[:, :units], unit_swap[:n_yl]], axis=0)
    up_u8 = jnp.concatenate([up_u[:, :units], unit_swap[n_yl:]], axis=0)

    def last_rows(value):
        return value.reshape(n_yl, rows, width)[:, rows - 1]

    last_tok = jnp.concatenate([last_rows(tok_half), last_rows(tok_sib)], axis=0).astype(f32)
    last_tok = (last_tok * coefs[:, None]).astype(bf16)
    head_term8 = (coefs[:, None] * head_vec.astype(f32)).astype(bf16)

    def weight_grad(full, own_right, sib_right, last_left, last_right):
        from_sib = lax.ppermute(full[units:], "co", SWAP)
        total = lax.optimization_barrier(
            (dot(full[:units], own_right, 1, 0) + dot(from_sib, sib_right, 1, 0)) * loss_scale
        )
        if last_left is None:
            ends = [v.reshape(units, n_yl, rows)[:, :, rows - 1] for v in (full[:units], from_sib)]
            last_left = jnp.concatenate(ends, axis=1).T
        return total + dot(last_left, last_right, 0, 0) * loss_scale

    grad_gate = weight_grad(gate_g, tok_half, tok_sib, gate_u8, last_tok)
    grad_up = weight_grad(up_g, tok_half, tok_sib, up_u8, last_tok)
    grad_down = weight_grad(hid, low_half, low_sib, None, head_term8)
    return grad_tokens, grad_gate, grad_up, grad_down, rewards


def solution(mesh):
    fine = Mesh(mesh.devices.reshape(4, 2, 8, 2, 4), FINE)
    gx, gz = ("yl", "co"), GZ
    weight = P(("gy",) + gx, gz)
    act = P(gx, gz + ("gy",))
    return jax.shard_map(
        body,
        mesh=fine,
        in_specs=(act, weight, weight, weight, P(gz + ("gy",)), act, P()),
        out_specs=(act, weight, weight, weight, P()),
        check_vma=False,
    )
```

```python
import jax
import jax.numpy as jnp
from jax import lax
from jax.experimental import pallas as pl
from jax.experimental.pallas import tpu as pltpu
from jax.sharding import Mesh, PartitionSpec as P

SEQ_LEN = 128
reward_weight = 64.0
FINE = ("yl", "co", "gy", "yh", "xx")
PLANE = ("yl", "gy")
GZ = ("yh", "xx")
SWAP = [(0, 1), (1, 0)]
f32, bf16 = jnp.float32, jnp.bfloat16


def exchange(pieces, axes):
    return lax.all_to_all(pieces, axes, 0, 0)


def to_all(value, axes, count):
    return exchange(jnp.broadcast_to(value[None], (count,) + value.shape), axes)


def dot(left, right, left_dim, right_dim):
    return lax.dot_general(
        left, right, (((left_dim,), (right_dim,)), ((), ())), preferred_element_type=f32
    )


def pieces(value):
    high = lax.reduce_precision(value, 8, 7)
    middle = lax.reduce_precision(value - high, 8, 7)
    return jnp.stack([high, middle, value - high - middle]).astype(bf16)


def first_products(tok_got, low_got, *refs):
    weights, (parts, tok, low, head, wide_head) = refs[:6], refs[6:]
    n_gy, n_yl, rows, cols = low_got.shape
    units, half = weights[0].shape[0], n_yl * rows
    for z in range(n_gy):
        at = slice(z * cols, (z + 1) * cols)
        for y in range(n_yl):
            tok[y * rows : (y + 1) * rows, at] = tok_got[y * n_gy + z, :rows]
            low[y * rows : (y + 1) * rows, at] = low_got[z, y]
        head[:, at] = tok_got[z, rows:]
        for r in range(0, 128, 16):
            wide_head[r : r + 16, at] = tok_got[z, rows:]
    for c in range(2):
        here = slice(c * units, (c + 1) * units)
        gate_w, up_w, down_w = (weights[2 * i + c][...] for i in range(3))
        parts[here, :half] = dot(gate_w, tok[...], 1, 1).astype(bf16)
        parts[here, half : 2 * half] = dot(up_w, tok[...], 1, 1).astype(bf16)
        parts[here, 2 * half : 3 * half] = dot(down_w, low[...], 1, 1).astype(bf16)
        v = dot(down_w, wide_head[...], 1, 1)
        high = v.astype(bf16).astype(f32)
        lane = lax.broadcasted_iota(jnp.int32, v.shape, 1)
        v = jnp.where(lane == 0, high, jnp.where(lane == 1, v - high, 0.0))
        parts[here, 3 * half :] = v.astype(bf16)


def body(tokens, gate_weight, up_weight, down_weight, reward_head, lm_grad, pair_index):
    n_yl, n_gy = lax.axis_size("yl"), lax.axis_size("gy")
    n_plane, n_gz = n_yl * n_gy, lax.axis_size(GZ)
    rows, cols = tokens.shape
    units, width = gate_weight.shape
    my_seq = lax.axis_index(("yl", "co"))
    core = lax.axis_index("co")

    def chip_block(weight):
        return weight, lax.ppermute(weight, "co", SWAP)

    gate_ws, up_ws, down_ws = chip_block(gate_weight), chip_block(up_weight), chip_block(down_weight)
    gate_w, up_w = jnp.concatenate(gate_ws, axis=0), jnp.concatenate(up_ws, axis=0)

    head_rows = jnp.broadcast_to(reward_head[None, :], (16, cols))
    low_got = to_all(lm_grad.astype(bf16), "yl", n_yl)
    tok_block, low_got = lax.optimization_barrier(
        (jnp.concatenate([tokens, head_rows], axis=0), low_got)
    )
    low_got = lax.all_gather(low_got, "gy")
    tok_got = to_all(tok_block, PLANE, n_plane)

    half = n_yl * rows
    whole = pl.BlockSpec(memory_space=pltpu.VMEM)
    parts, tok_half, low_half, head_vec = pl.pallas_call(
        first_products,
        out_shape=(
            jax.ShapeDtypeStruct((2 * units, 3 * half + 128), bf16),
            jax.ShapeDtypeStruct((half, width), bf16),
            jax.ShapeDtypeStruct((half, width), bf16),
            jax.ShapeDtypeStruct((16, width), bf16),
        ),
        in_specs=[whole] * 8,
        out_specs=(whole,) * 4,
        scratch_shapes=[pltpu.VMEM((128, width), bf16)],
        compiler_params=pltpu.CompilerParams(vmem_limit_bytes=40 * 2**20),
        cost_estimate=pl.CostEstimate(
            flops=2 * 2 * units * width * (3 * half + 128), bytes_accessed=12 * 2**20, transcendentals=0
        ),
        name="first_products",
    )(tok_got, low_got, *gate_ws, *up_ws, *down_ws)
    head_vec = head_vec[:1]
    own = 2 * units // n_gz
    sums = jnp.sum(exchange(parts.reshape(n_gz, own, 3 * half + 128), GZ).astype(f32), axis=0)
    gate_sum, up_sum, hidden_grad = (sums[:, i * half : (i + 1) * half] for i in range(3))
    head_down = sums[:, 3 * half : 3 * half + 1] + sums[:, 3 * half + 1 : 3 * half + 2]

    gate_sigmoid = jax.nn.sigmoid(gate_sum)
    silu_gate = gate_sum * gate_sigmoid
    hidden = (silu_gate * up_sum).astype(bf16)

    gate_slope = up_sum * gate_sigmoid * (1.0 + gate_sum * (1.0 - gate_sigmoid))
    up_grad = (hidden_grad * silu_gate).astype(bf16)
    gate_grad = (hidden_grad * gate_slope).astype(bf16)

    def last_cols(value):
        return value.reshape(own, n_yl, rows)[:, :, rows - 1].astype(f32)

    gate_unit = (head_down * last_cols(gate_slope)).astype(bf16).T
    up_unit = (head_down * last_cols(silu_gate)).astype(bf16).T
    own_term = jnp.sum(tokens[rows - 1].astype(f32) * reward_head.astype(f32))
    terms = jnp.sum(last_cols(hidden) * head_down, axis=0)
    terms = terms + jnp.where(jnp.arange(n_yl) == lax.axis_index("yl"), own_term, 0.0)
    unit_rows = jnp.concatenate(
        [jnp.pad(gate_unit, ((0, 0), (0, 128 - own))), jnp.pad(up_unit, ((0, 0), (0, half - 128 - own)))], axis=1
    )
    term_rows = jnp.pad(pieces(terms).reshape(1, -1), ((0, 7 - n_yl), (0, half - 3 * n_yl)))
    mine = jnp.concatenate([gate_grad, up_grad, hidden, unit_rows, term_rows], axis=0)
    everyone = to_all(mine, GZ, n_gz)
    gate_g, up_g, hid = (
        everyone[:, i * own : (i + 1) * own].reshape(2 * units, half) for i in range(3)
    )
    units_at = everyone[:, 3 * own : 3 * own + n_yl].transpose(1, 0, 2)
    gate_u, up_u = (
        units_at[:, :, i * 128 : i * 128 + own].reshape(n_yl, 2 * units) for i in range(2)
    )
    core_terms = jnp.sum(
        everyone[:, 3 * own + n_yl, : 3 * n_yl].astype(f32).reshape(n_gz * 3, n_yl), axis=0
    )
    pair_terms = jnp.stack([core_terms, lax.ppermute(core_terms, "co", SWAP)])

    token_part = dot(gate_g, gate_w, 0, 0) + dot(up_g, up_w, 0, 0)
    token_part = token_part.astype(bf16).reshape(n_yl, rows, n_gy, cols).transpose(0, 2, 1, 3)
    unit_part = (dot(gate_u, gate_w, 1, 0) + dot(up_u, up_w, 1, 0)).astype(bf16)
    term_row = jnp.pad(pieces(pair_terms).reshape(1, 1, -1), ((0, 0), (0, 0), (0, cols - 6 * n_yl)))
    extra = jnp.concatenate(
        [unit_part.reshape(n_plane, 1, cols), jnp.broadcast_to(term_row, (n_plane, 1, cols))], axis=1
    )
    sent = jnp.concatenate(
        [token_part.reshape(n_plane, rows, cols), jnp.pad(extra, ((0, 0), (0, 6), (0, 0)))], axis=1
    )
    token_sum = jnp.sum(exchange(sent, PLANE).astype(f32), axis=0)

    both = jnp.sum(token_sum[rows + 1, : 6 * n_yl].reshape(3, 2, n_yl), axis=0)
    sequence = jnp.arange(2 * n_yl, dtype=jnp.int32)
    rewards = jnp.where(sequence % 2 == core, jnp.repeat(both[0], 2), jnp.repeat(both[1], 2))
    chosen_hot = (pair_index[:, 0:1] == sequence[None, :]).astype(f32)
    rejected_hot = (pair_index[:, 1:2] == sequence[None, :]).astype(f32)
    margin = jnp.sum((chosen_hot - rejected_hot) * rewards[None, :], axis=1)
    pair_weight = jax.nn.sigmoid(-margin)
    scaled = reward_weight * jnp.sum((rejected_hot - chosen_hot) * pair_weight[:, None], axis=0)
    by_core = scaled.reshape(n_yl, 2)
    core_coefs = jnp.where(core == 0, by_core[:, 0], by_core[:, 1])
    sib_coefs = jnp.where(core == 0, by_core[:, 1], by_core[:, 0])
    coefs = jnp.concatenate([core_coefs, sib_coefs])
    my_coef = jnp.sum(jnp.where(sequence == my_seq, scaled, 0.0))

    row = jnp.arange(rows)[:, None]
    head_term = my_coef * (reward_head.astype(f32) + token_sum[rows])
    grad_tokens = lm_grad + token_sum[:rows] + jnp.where(row == rows - 1, head_term[None, :], 0.0)

    loss_scale = 1.0 / jnp.sqrt(f32(rows * 2 * n_yl))
    tok_sib = lax.ppermute(tok_half, "co", SWAP)
    low_sib = lax.ppermute(low_half, "co", SWAP)
    unit_swap = lax.ppermute(jnp.concatenate([gate_u[:, units:], up_u[:, units:]], axis=0), "co", SWAP)
    gate_u8 = jnp.concatenate([gate_u[:, :units], unit_swap[:n_yl]], axis=0)
    up_u8 = jnp.concatenate([up_u[:, :units], unit_swap[n_yl:]], axis=0)

    def last_rows(value):
        return value.reshape(n_yl, rows, width)[:, rows - 1]

    last_tok = jnp.concatenate([last_rows(tok_half), last_rows(tok_sib)], axis=0).astype(f32)
    last_tok = (last_tok * coefs[:, None]).astype(bf16)
    head_term8 = (coefs[:, None] * head_vec.astype(f32)).astype(bf16)

    def weight_grad(full, own_right, sib_right, last_left, last_right):
        from_sib = lax.ppermute(full[units:], "co", SWAP)
        total = lax.optimization_barrier(
            (dot(full[:units], own_right, 1, 0) + dot(from_sib, sib_right, 1, 0)) * loss_scale
        )
        if last_left is None:
            ends = [v.reshape(units, n_yl, rows)[:, :, rows - 1] for v in (full[:units], from_sib)]
            last_left = jnp.concatenate(ends, axis=1).T
        return total + dot(last_left, last_right, 0, 0) * loss_scale

    grad_gate = weight_grad(gate_g, tok_half, tok_sib, gate_u8, last_tok)
    grad_up = weight_grad(up_g, tok_half, tok_sib, up_u8, last_tok)
    grad_down = weight_grad(hid, low_half, low_sib, None, head_term8)
    return grad_tokens, grad_gate, grad_up, grad_down, rewards


def solution(mesh):
    fine = Mesh(mesh.devices.reshape(4, 2, 8, 2, 4), FINE)
    gx, gz = ("yl", "co"), GZ
    weight = P(("gy",) + gx, gz)
    act = P(gx, gz + ("gy",))
    return jax.shard_map(
        body,
        mesh=fine,
        in_specs=(act, weight, weight, weight, P(gz + ("gy",)), act, P()),
        out_specs=(act, weight, weight, weight, P()),
        check_vma=False,
    )
```

```python
import jax
import jax.numpy as jnp
from jax import lax
from jax.experimental import pallas as pl
from jax.experimental.pallas import tpu as pltpu
from jax.sharding import Mesh, PartitionSpec as P

SEQ_LEN = 128
reward_weight = 64.0
FINE = ("yl", "co", "gy", "yh", "xx")
PLANE = ("yl", "gy")
GZ = ("yh", "xx")
SWAP = [(0, 1), (1, 0)]
f32, bf16 = jnp.float32, jnp.bfloat16


def exchange(pieces, axes):
    return lax.all_to_all(pieces, axes, 0, 0)


def to_all(value, axes, count):
    return exchange(jnp.broadcast_to(value[None], (count,) + value.shape), axes)


def dot(left, right, left_dim, right_dim):
    return lax.dot_general(
        left, right, (((left_dim,), (right_dim,)), ((), ())), preferred_element_type=f32
    )


def pieces(value):
    high = lax.reduce_precision(value, 8, 7)
    middle = lax.reduce_precision(value - high, 8, 7)
    return jnp.stack([high, middle, value - high - middle]).astype(bf16)


def load(sources, held, sems):
    copies = [pltpu.make_async_copy(src, held.at[i], sems.at[i]) for i, src in enumerate(sources)]
    for copy in copies:
        copy.start()
    return copies


def token_products(tok_got, *refs):
    weights, (parts, tok, head, held, wide_head, sems) = refs[:6], refs[6:]
    copies = load(weights, held, sems)
    width, cols = tok.shape[1], tok_got.shape[2]
    n_gy = width // cols
    n_yl = tok_got.shape[0] // n_gy
    rows = tok.shape[0] // n_yl
    units, half = weights[0].shape[0], tok.shape[0]
    for z in range(n_gy):
        at = slice(z * cols, (z + 1) * cols)
        for y in range(n_yl):
            tok[y * rows : (y + 1) * rows, at] = tok_got[y * n_gy + z, :rows]
        head[:, at] = tok_got[z, rows:]
        for r in range(0, 128, 16):
            wide_head[r : r + 16, at] = tok_got[z, rows:]
    for i in range(6):
        copies[i].wait()
        here = slice(i % 2 * units, (i % 2 + 1) * units)
        if i < 4:
            at = slice(i // 2 * half, (i // 2 + 1) * half)
            parts[here, at] = dot(held[i], tok[...], 1, 1).astype(bf16)
        else:
            v = dot(held[i], wide_head[...], 1, 1)
            high = v.astype(bf16).astype(f32)
            lane = lax.broadcasted_iota(jnp.int32, v.shape, 1)
            v = jnp.where(lane == 0, high, jnp.where(lane == 1, v - high, 0.0))
            parts[here, 2 * half :] = v.astype(bf16)


def cotangent_products(at_yl, low_got, *refs):
    weights, (parts, low, held, low_held, sems) = refs[:2], refs[2:]
    copies = load(weights, held, sems)
    arrival = pltpu.make_async_copy(low_got, low_held, sems.at[2])
    arrival.start()
    arrival.wait()
    n_gy, n_yl, rows, cols = low_held.shape
    units = weights[0].shape[0]
    for shift in range(n_yl):
        first = pl.multiple_of(lax.rem(at_yl[0] + (n_yl - shift), n_yl) * rows, rows)
        for z in range(n_gy):
            low[pl.ds(first, rows), z * cols : (z + 1) * cols] = low_held[z, shift]
    for i in range(2):
        copies[i].wait()
        parts[i * units : (i + 1) * units, :] = dot(held[i], low[...], 1, 1).astype(bf16)


def body(tokens, gate_weight, up_weight, down_weight, reward_head, lm_grad, pair_index):
    n_yl, n_gy = lax.axis_size("yl"), lax.axis_size("gy")
    n_plane, n_gz = n_yl * n_gy, lax.axis_size(GZ)
    rows, cols = tokens.shape
    units, width = gate_weight.shape
    my_seq = lax.axis_index(("yl", "co"))
    core = lax.axis_index("co")

    def chip_block(weight):
        return weight, lax.ppermute(weight, "co", SWAP)

    gate_ws, up_ws, down_ws = chip_block(gate_weight), chip_block(up_weight), chip_block(down_weight)
    gate_w, up_w = jnp.concatenate(gate_ws, axis=0), jnp.concatenate(up_ws, axis=0)

    low = lm_grad.astype(bf16)
    low_rows = [low]
    for shift in range(1, n_yl):
        low_rows.append(lax.ppermute(low, "yl", [(k, (k + shift) % n_yl) for k in range(n_yl)]))
    low_got = lax.all_gather(jnp.stack(low_rows), "gy")
    head_rows = jnp.broadcast_to(reward_head[None, :], (16, cols))
    tok_got = to_all(jnp.concatenate([tokens, head_rows], axis=0), PLANE, n_plane)

    half, own = n_yl * rows, 2 * units // n_gz
    whole, apart = pl.BlockSpec(memory_space=pltpu.VMEM), pl.BlockSpec(memory_space=pl.ANY)
    grant = pltpu.CompilerParams(vmem_limit_bytes=40 * 2**20)
    parts, tok_half, head_vec = pl.pallas_call(
        token_products,
        out_shape=(
            jax.ShapeDtypeStruct((2 * units, 2 * half + 128), bf16),
            jax.ShapeDtypeStruct((half, width), bf16),
            jax.ShapeDtypeStruct((16, width), bf16),
        ),
        in_specs=[whole] + [apart] * 6,
        out_specs=(whole,) * 3,
        scratch_shapes=[
            pltpu.VMEM((6, units, width), bf16),
            pltpu.VMEM((128, width), bf16),
            pltpu.SemaphoreType.DMA((6,)),
        ],
        compiler_params=grant,
        cost_estimate=pl.CostEstimate(
            flops=4 * units * width * (2 * half + 128), bytes_accessed=8 * 2**20, transcendentals=0
        ),
        name="token_products",
    )(tok_got, *gate_ws, *up_ws, *down_ws)
    head_vec = head_vec[:1]
    first = exchange(parts.reshape(n_gz, own, 2 * half + 128), GZ)

    back_parts, low_half = pl.pallas_call(
        cotangent_products,
        out_shape=(
            jax.ShapeDtypeStruct((2 * units, half), bf16),
            jax.ShapeDtypeStruct((half, width), bf16),
        ),
        in_specs=[pl.BlockSpec(memory_space=pltpu.SMEM)] + [apart] * 3,
        out_specs=(whole,) * 2,
        scratch_shapes=[
            pltpu.VMEM((2, units, width), bf16),
            pltpu.VMEM((n_gy, n_yl, rows, cols), bf16),
            pltpu.SemaphoreType.DMA((3,)),
        ],
        compiler_params=grant,
        cost_estimate=pl.CostEstimate(
            flops=4 * units * width * half, bytes_accessed=5 * 2**20, transcendentals=0
        ),
        name="cotangent_products",
    )(lax.axis_index("yl").astype(jnp.int32)[None], low_got, *down_ws)
    first, back_parts = lax.optimization_barrier((first, back_parts))
    second = exchange(back_parts.reshape(n_gz, own, half), GZ)

    sums = jnp.sum(first.astype(f32), axis=0)
    gate_sum, up_sum = sums[:, :half], sums[:, half : 2 * half]
    head_down = sums[:, 2 * half : 2 * half + 1] + sums[:, 2 * half + 1 : 2 * half + 2]
    gate_sigmoid = jax.nn.sigmoid(gate_sum)
    silu_gate = gate_sum * gate_sigmoid
    hidden = (silu_gate * up_sum).astype(bf16)
    gate_slope = up_sum * gate_sigmoid * (1.0 + gate_sum * (1.0 - gate_sigmoid))

    def last_cols(value):
        return value.reshape(own, n_yl, rows)[:, :, rows - 1].astype(f32)

    gate_unit = (head_down * last_cols(gate_slope)).astype(bf16).T
    up_unit = (head_down * last_cols(silu_gate)).astype(bf16).T
    own_term = jnp.sum(tokens[rows - 1].astype(f32) * reward_head.astype(f32))
    terms = jnp.sum(last_cols(hidden) * head_down, axis=0)
    terms = terms + jnp.where(jnp.arange(n_yl) == lax.axis_index("yl"), own_term, 0.0)
    unit_rows = jnp.concatenate(
        [jnp.pad(gate_unit, ((0, 0), (0, 128 - own))), jnp.pad(up_unit, ((0, 0), (0, half - 128 - own)))], axis=1
    )
    term_rows = jnp.pad(pieces(terms).reshape(1, -1), ((0, 7 - n_yl), (0, half - 3 * n_yl)))
    silu_gate, gate_slope, early, second = lax.optimization_barrier(
        (silu_gate, gate_slope, jnp.concatenate([hidden, unit_rows, term_rows], axis=0), second)
    )
    hidden_grad = jnp.sum(second.astype(f32), axis=0)
    up_grad = (hidden_grad * silu_gate).astype(bf16)
    gate_grad = (hidden_grad * gate_slope).astype(bf16)
    mine = jnp.concatenate([gate_grad, up_grad, early], axis=0)
    everyone = to_all(mine, GZ, n_gz)
    gate_g, up_g, hid = (
        everyone[:, i * own : (i + 1) * own].reshape(2 * units, half) for i in range(3)
    )
    units_at = everyone[:, 3 * own : 3 * own + n_yl].transpose(1, 0, 2)
    gate_u, up_u = (
        units_at[:, :, i * 128 : i * 128 + own].reshape(n_yl, 2 * units) for i in range(2)
    )
    core_terms = jnp.sum(
        everyone[:, 3 * own + n_yl, : 3 * n_yl].astype(f32).reshape(n_gz * 3, n_yl), axis=0
    )
    pair_terms = jnp.stack([core_terms, lax.ppermute(core_terms, "co", SWAP)])

    token_part = dot(gate_g, gate_w, 0, 0) + dot(up_g, up_w, 0, 0)
    token_part = token_part.astype(bf16).reshape(n_yl, rows, n_gy, cols).transpose(0, 2, 1, 3)
    unit_part = (dot(gate_u, gate_w, 1, 0) + dot(up_u, up_w, 1, 0)).astype(bf16)
    term_row = jnp.pad(pieces(pair_terms).reshape(1, 1, -1), ((0, 0), (0, 0), (0, cols - 6 * n_yl)))
    extra = jnp.concatenate(
        [unit_part.reshape(n_plane, 1, cols), jnp.broadcast_to(term_row, (n_plane, 1, cols))], axis=1
    )
    sent = jnp.concatenate(
        [token_part.reshape(n_plane, rows, cols), jnp.pad(extra, ((0, 0), (0, 6), (0, 0)))], axis=1
    )
    sent, gate_g, up_g, hid, gate_u, up_u = lax.optimization_barrier(
        (sent, gate_g, up_g, hid, gate_u, up_u)
    )
    token_sum = jnp.sum(exchange(sent, PLANE).astype(f32), axis=0)

    both = jnp.sum(token_sum[rows + 1, : 6 * n_yl].reshape(3, 2, n_yl), axis=0)
    sequence = jnp.arange(2 * n_yl, dtype=jnp.int32)
    rewards = jnp.where(sequence % 2 == core, jnp.repeat(both[0], 2), jnp.repeat(both[1], 2))
    chosen_hot = (pair_index[:, 0:1] == sequence[None, :]).astype(f32)
    rejected_hot = (pair_index[:, 1:2] == sequence[None, :]).astype(f32)
    margin = jnp.sum((chosen_hot - rejected_hot) * rewards[None, :], axis=1)
    pair_weight = jax.nn.sigmoid(-margin)
    scaled = reward_weight * jnp.sum((rejected_hot - chosen_hot) * pair_weight[:, None], axis=0)
    by_core = scaled.reshape(n_yl, 2)
    core_coefs = jnp.where(core == 0, by_core[:, 0], by_core[:, 1])
    sib_coefs = jnp.where(core == 0, by_core[:, 1], by_core[:, 0])
    coefs = jnp.concatenate([core_coefs, sib_coefs])
    my_coef = jnp.sum(jnp.where(sequence == my_seq, scaled, 0.0))

    row = jnp.arange(rows)[:, None]
    head_term = my_coef * (reward_head.astype(f32) + token_sum[rows])
    grad_tokens = lm_grad + token_sum[:rows] + jnp.where(row == rows - 1, head_term[None, :], 0.0)

    loss_scale = 1.0 / jnp.sqrt(f32(rows * 2 * n_yl))
    tok_sib = lax.ppermute(tok_half, "co", SWAP)
    low_sib = lax.ppermute(low_half, "co", SWAP)
    unit_swap = lax.ppermute(jnp.concatenate([gate_u[:, units:], up_u[:, units:]], axis=0), "co", SWAP)
    gate_u8 = jnp.concatenate([gate_u[:, :units], unit_swap[:n_yl]], axis=0)
    up_u8 = jnp.concatenate([up_u[:, :units], unit_swap[n_yl:]], axis=0)

    def last_rows(value):
        return value.reshape(n_yl, rows, width)[:, rows - 1]

    last_tok = jnp.concatenate([last_rows(tok_half), last_rows(tok_sib)], axis=0).astype(f32)
    last_tok = (last_tok * coefs[:, None]).astype(bf16)
    head_term8 = (coefs[:, None] * head_vec.astype(f32)).astype(bf16)

    def weight_grad(full, own_right, sib_right, last_left, last_right):
        from_sib = lax.ppermute(full[units:], "co", SWAP)
        total = lax.optimization_barrier(
            (dot(full[:units], own_right, 1, 0) + dot(from_sib, sib_right, 1, 0)) * loss_scale
        )
        if last_left is None:
            ends = [v.reshape(units, n_yl, rows)[:, :, rows - 1] for v in (full[:units], from_sib)]
            last_left = jnp.concatenate(ends, axis=1).T
        return total + dot(last_left, last_right, 0, 0) * loss_scale

    grad_gate = weight_grad(gate_g, tok_half, tok_sib, gate_u8, last_tok)
    grad_up = weight_grad(up_g, tok_half, tok_sib, up_u8, last_tok)
    grad_down = weight_grad(hid, low_half, low_sib, None, head_term8)
    return grad_tokens, grad_gate, grad_up, grad_down, rewards


def solution(mesh):
    fine = Mesh(mesh.devices.reshape(4, 2, 8, 2, 4), FINE)
    gx, gz = ("yl", "co"), GZ
    weight = P(("gy",) + gx, gz)
    act = P(gx, gz + ("gy",))
    return jax.shard_map(
        body,
        mesh=fine,
        in_specs=(act, weight, weight, weight, P(gz + ("gy",)), act, P()),
        out_specs=(act, weight, weight, weight, P()),
        check_vma=False,
    )
```

```python
import jax
import jax.numpy as jnp
from jax import lax
from jax.experimental import pallas as pl
from jax.experimental.pallas import tpu as pltpu
from jax.sharding import Mesh, PartitionSpec as P

SEQ_LEN = 128
reward_weight = 64.0
FINE = ("yl", "co", "gy", "yh", "xx")
PLANE = ("yl", "gy")
GZ = ("yh", "xx")
SWAP = [(0, 1), (1, 0)]
f32, bf16 = jnp.float32, jnp.bfloat16


def exchange(pieces, axes):
    return lax.all_to_all(pieces, axes, 0, 0)


def to_all(value, axes, count):
    return exchange(jnp.broadcast_to(value[None], (count,) + value.shape), axes)


def dot(left, right, left_dim, right_dim):
    return lax.dot_general(
        left, right, (((left_dim,), (right_dim,)), ((), ())), preferred_element_type=f32
    )


def pieces(value):
    high = lax.reduce_precision(value, 8, 7)
    middle = lax.reduce_precision(value - high, 8, 7)
    return jnp.stack([high, middle, value - high - middle]).astype(bf16)


def token_products(tok_got, gate_w, up_w, down_w, parts, tok, head, wide_head):
    width, cols = tok.shape[1], tok_got.shape[2]
    n_gy = width // cols
    n_yl = tok_got.shape[0] // n_gy
    rows = tok.shape[0] // n_yl
    chip_units, half = down_w.shape[0], tok.shape[0]
    for z in range(n_gy):
        at = slice(z * cols, (z + 1) * cols)
        for y in range(n_yl):
            tok[y * rows : (y + 1) * rows, at] = tok_got[y * n_gy + z, :rows]
        head[:, at] = tok_got[z, rows:]
        for r in range(0, 128, 16):
            wide_head[r : r + 16, at] = tok_got[z, rows:]
    parts[:, :half] = dot(gate_w[:chip_units], tok[...], 1, 1).astype(bf16)
    parts[:, half : 2 * half] = dot(up_w[:chip_units], tok[...], 1, 1).astype(bf16)
    v = dot(down_w[...], wide_head[...], 1, 1)
    high = v.astype(bf16).astype(f32)
    lane = lax.broadcasted_iota(jnp.int32, v.shape, 1)
    v = jnp.where(lane == 0, high, jnp.where(lane == 1, v - high, 0.0))
    parts[:, 2 * half :] = v.astype(bf16)


def cotangent_products(low_got, down_w, parts, low):
    n_gy, n_yl, rows, cols = low_got.shape
    for y in range(n_yl):
        for z in range(n_gy):
            low[y * rows : (y + 1) * rows, z * cols : (z + 1) * cols] = low_got[z, y]
    parts[...] = dot(down_w[...], low[...], 1, 1).astype(bf16)


def token_gradients(everyone, gate_w, up_w, sent, full):
    width = gate_w.shape[1]
    n_gz, n_rows, half = everyone.shape
    own = (n_rows - 8) // 3
    n_plane, piece_rows, cols = sent.shape
    n_gy, rows = width // cols, piece_rows - 16
    unit = jnp.zeros((8, half), f32)
    for j in range(n_gz):
        block = everyone[j].astype(f32)
        for i in range(2):
            full[i, j * own : (j + 1) * own] = block[i * own : (i + 1) * own]
        unit += block[3 * own :]
    for i in range(2):
        full[i, n_gz * own :] = jnp.zeros((full.shape[1] - n_gz * own, half), f32)
    unit = unit.astype(bf16)
    gate_t, up_t = (full[i].T.astype(bf16) for i in range(2))
    step = 2 * cols
    for c in range(0, width, step):
        part = dot(gate_t, gate_w[:, c : c + step], 1, 0) + dot(up_t, up_w[:, c : c + step], 1, 0)
        units_here = (
            dot(unit, gate_w[:, c : c + step], 1, 0)[:4] + dot(unit, up_w[:, c : c + step], 1, 0)[4:]
        )
        for z in range(c // cols, (c + step) // cols):
            at = slice(z * cols - c, (z + 1) * cols - c)
            for y in range(n_plane // n_gy):
                piece = y * n_gy + z
                sent[piece, :rows] = part[y * rows : (y + 1) * rows, at].astype(bf16)
                row = lax.broadcasted_iota(jnp.int32, (16, cols), 0)
                sent[piece, rows:] = jnp.where(row == 0, units_here[y : y + 1, at], 0.0).astype(bf16)


def body(tokens, gate_weight, up_weight, down_weight, reward_head, lm_grad, pair_index):
    n_yl, n_gy = lax.axis_size("yl"), lax.axis_size("gy")
    n_plane, n_gz = n_yl * n_gy, lax.axis_size(GZ)
    rows, cols = tokens.shape
    units, width = gate_weight.shape
    my_seq = lax.axis_index(("yl", "co"))
    core = lax.axis_index("co")

    def chip_block(weight, padding):
        parts = [weight, lax.ppermute(weight, "co", SWAP), jnp.zeros((padding, width), bf16)]
        return jnp.concatenate(parts, axis=0)

    padding = -2 * units % 128
    gate_w, up_w = chip_block(gate_weight, padding), chip_block(up_weight, padding)
    down_w = chip_block(down_weight, 0)

    low_got = to_all(lm_grad.astype(bf16), "yl", n_yl)
    head_rows = jnp.broadcast_to(reward_head[None, :], (16, cols))
    tok_block = jnp.concatenate([tokens, head_rows], axis=0)
    low_got, tok_block = lax.optimization_barrier((low_got, tok_block))
    low_got = lax.all_gather(low_got, "gy")
    tok_got = to_all(tok_block, PLANE, n_plane)

    half, own = n_yl * rows, 2 * units // n_gz
    whole = pl.BlockSpec(memory_space=pltpu.VMEM)
    grant = pltpu.CompilerParams(vmem_limit_bytes=40 * 2**20)
    parts, tok_half, head_vec = pl.pallas_call(
        token_products,
        out_shape=(
            jax.ShapeDtypeStruct((2 * units, 2 * half + 128), bf16),
            jax.ShapeDtypeStruct((half, width), bf16),
            jax.ShapeDtypeStruct((16, width), bf16),
        ),
        in_specs=[whole] * 4,
        out_specs=(whole,) * 3,
        scratch_shapes=[pltpu.VMEM((128, width), bf16)],
        compiler_params=grant,
        cost_estimate=pl.CostEstimate(
            flops=4 * units * width * (2 * half + 128), bytes_accessed=8 * 2**20, transcendentals=0
        ),
        name="token_products",
    )(tok_got, gate_w, up_w, down_w)
    head_vec = head_vec[:1]
    first = exchange(parts.reshape(n_gz, own, 2 * half + 128), GZ)

    back_parts, low_half = pl.pallas_call(
        cotangent_products,
        out_shape=(
            jax.ShapeDtypeStruct((2 * units, half), bf16),
            jax.ShapeDtypeStruct((half, width), bf16),
        ),
        in_specs=[whole] * 2,
        out_specs=(whole,) * 2,
        compiler_params=grant,
        cost_estimate=pl.CostEstimate(
            flops=4 * units * width * half, bytes_accessed=5 * 2**20, transcendentals=0
        ),
        name="cotangent_products",
    )(low_got, down_w)
    first, back_parts = lax.optimization_barrier((first, back_parts))
    second = exchange(back_parts.reshape(n_gz, own, half), GZ)

    sums = jnp.sum(first.astype(f32), axis=0)
    gate_sum, up_sum = sums[:, :half], sums[:, half : 2 * half]
    head_down = sums[:, 2 * half : 2 * half + 1] + sums[:, 2 * half + 1 : 2 * half + 2]
    gate_sigmoid = jax.nn.sigmoid(gate_sum)
    silu_gate = gate_sum * gate_sigmoid
    hidden = (silu_gate * up_sum).astype(bf16)
    gate_slope = up_sum * gate_sigmoid * (1.0 + gate_sum * (1.0 - gate_sigmoid))

    def last_cols(value):
        return value.reshape(own, n_yl, rows)[:, :, rows - 1].astype(f32)

    gate_unit = (head_down * last_cols(gate_slope)).astype(bf16).T
    up_unit = (head_down * last_cols(silu_gate)).astype(bf16).T
    own_term = jnp.sum(tokens[rows - 1].astype(f32) * reward_head.astype(f32))
    terms = jnp.sum(last_cols(hidden) * head_down, axis=0)
    terms = terms + jnp.where(jnp.arange(n_yl) == lax.axis_index("yl"), own_term, 0.0)
    unit_rows = lax.dynamic_update_slice(
        jnp.zeros((2 * n_yl, half), bf16),
        jnp.concatenate([gate_unit, up_unit], axis=0),
        (0, lax.axis_index(GZ) * own),
    )
    term_rows = pieces(terms).reshape(1, -1)
    unit_rows = lax.dynamic_update_slice(unit_rows, term_rows, (0, 2 * units))
    silu_gate, gate_slope, early, second = lax.optimization_barrier(
        (silu_gate, gate_slope, jnp.concatenate([hidden, unit_rows], axis=0), second)
    )
    hidden_grad = jnp.sum(second.astype(f32), axis=0)
    up_grad = (hidden_grad * silu_gate).astype(bf16)
    gate_grad = (hidden_grad * gate_slope).astype(bf16)
    mine = jnp.concatenate([gate_grad, up_grad, early], axis=0)
    everyone = to_all(mine, GZ, n_gz)
    core_terms = jnp.sum(
        everyone[:, 3 * own, 2 * units : 2 * units + 3 * n_yl].astype(f32).reshape(n_gz * 3, n_yl), axis=0
    )
    pair_terms = jnp.stack([core_terms, lax.ppermute(core_terms, "co", SWAP)])
    sent = pl.pallas_call(
        token_gradients,
        out_shape=jax.ShapeDtypeStruct((n_plane, rows + 16, cols), bf16),
        in_specs=[whole] * 3,
        out_specs=whole,
        scratch_shapes=[pltpu.VMEM((2, 2 * units + padding, half), f32)],
        compiler_params=grant,
        cost_estimate=pl.CostEstimate(
            flops=8 * units * width * half, bytes_accessed=5 * 2**20, transcendentals=0
        ),
        name="token_gradients",
    )(everyone, gate_w, up_w)
    term_row = pieces(pair_terms).reshape(1, 1, 6 * n_yl)
    sent = lax.dynamic_update_slice(
        sent, jnp.broadcast_to(term_row, (n_plane, 1, 6 * n_yl)), (0, rows + 1, 0)
    )
    sent, everyone = lax.optimization_barrier((sent, everyone))
    gate_g, up_g, hid = (
        everyone[:, i * own : (i + 1) * own].reshape(2 * units, half) for i in range(3)
    )
    units_at = jnp.sum(everyone[:, 3 * own :, : 2 * units].astype(f32), axis=0).astype(bf16)
    gate_u, up_u = units_at[:n_yl], units_at[n_yl:]
    token_sum = jnp.sum(exchange(sent, PLANE).astype(f32), axis=0)

    both = jnp.sum(token_sum[rows + 1, : 6 * n_yl].reshape(3, 2, n_yl), axis=0)
    sequence = jnp.arange(2 * n_yl, dtype=jnp.int32)
    rewards = jnp.where(sequence % 2 == core, jnp.repeat(both[0], 2), jnp.repeat(both[1], 2))
    chosen_hot = (pair_index[:, 0:1] == sequence[None, :]).astype(f32)
    rejected_hot = (pair_index[:, 1:2] == sequence[None, :]).astype(f32)
    margin = jnp.sum((chosen_hot - rejected_hot) * rewards[None, :], axis=1)
    pair_weight = jax.nn.sigmoid(-margin)
    scaled = reward_weight * jnp.sum((rejected_hot - chosen_hot) * pair_weight[:, None], axis=0)
    by_core = scaled.reshape(n_yl, 2)
    core_coefs = jnp.where(core == 0, by_core[:, 0], by_core[:, 1])
    sib_coefs = jnp.where(core == 0, by_core[:, 1], by_core[:, 0])
    coefs = jnp.concatenate([core_coefs, sib_coefs])
    my_coef = jnp.sum(jnp.where(sequence == my_seq, scaled, 0.0))

    row = jnp.arange(rows)[:, None]
    head_term = my_coef * (reward_head.astype(f32) + token_sum[rows])
    grad_tokens = lm_grad + token_sum[:rows] + jnp.where(row == rows - 1, head_term[None, :], 0.0)

    loss_scale = 1.0 / jnp.sqrt(f32(rows * 2 * n_yl))
    tok_sib = lax.ppermute(tok_half, "co", SWAP)
    low_sib = lax.ppermute(low_half, "co", SWAP)
    unit_swap = lax.ppermute(jnp.concatenate([gate_u[:, units:], up_u[:, units:]], axis=0), "co", SWAP)
    gate_u8 = jnp.concatenate([gate_u[:, :units], unit_swap[:n_yl]], axis=0)
    up_u8 = jnp.concatenate([up_u[:, :units], unit_swap[n_yl:]], axis=0)

    def last_rows(value):
        return value.reshape(n_yl, rows, width)[:, rows - 1]

    last_tok = jnp.concatenate([last_rows(tok_half), last_rows(tok_sib)], axis=0).astype(f32)
    last_tok = (last_tok * coefs[:, None]).astype(bf16)
    head_term8 = (coefs[:, None] * head_vec.astype(f32)).astype(bf16)

    def weight_grad(full, own_right, sib_right, last_left, last_right):
        from_sib = lax.ppermute(full[units:], "co", SWAP)
        total = lax.optimization_barrier(
            (dot(full[:units], own_right, 1, 0) + dot(from_sib, sib_right, 1, 0)) * loss_scale
        )
        if last_left is None:
            ends = [v.reshape(units, n_yl, rows)[:, :, rows - 1] for v in (full[:units], from_sib)]
            last_left = jnp.concatenate(ends, axis=1).T
        return total + dot(last_left, last_right, 0, 0) * loss_scale

    grad_gate = weight_grad(gate_g, tok_half, tok_sib, gate_u8, last_tok)
    grad_up = weight_grad(up_g, tok_half, tok_sib, up_u8, last_tok)
    grad_down = weight_grad(hid, low_half, low_sib, None, head_term8)
    return grad_tokens, grad_gate, grad_up, grad_down, rewards


def solution(mesh):
    fine = Mesh(mesh.devices.reshape(4, 2, 8, 2, 4), FINE)
    gx, gz = ("yl", "co"), GZ
    weight = P(("gy",) + gx, gz)
    act = P(gx, gz + ("gy",))
    return jax.shard_map(
        body,
        mesh=fine,
        in_specs=(act, weight, weight, weight, P(gz + ("gy",)), act, P()),
        out_specs=(act, weight, weight, weight, P()),
        check_vma=False,
    )
```

```python
import jax
import jax.numpy as jnp
from jax import lax
from jax.experimental import pallas as pl
from jax.experimental.pallas import tpu as pltpu
from jax.sharding import Mesh, PartitionSpec as P

SEQ_LEN = 128
reward_weight = 64.0
FINE = ("yl", "co", "gy", "yh", "xx")
PLANE = ("yl", "gy")
GZ = ("yh", "xx")
SWAP = [(0, 1), (1, 0)]
f32, bf16 = jnp.float32, jnp.bfloat16


def exchange(pieces, axes):
    return lax.all_to_all(pieces, axes, 0, 0)


def to_all(value, axes, count):
    return exchange(jnp.broadcast_to(value[None], (count,) + value.shape), axes)


def dot(left, right, left_dim, right_dim):
    return lax.dot_general(
        left, right, (((left_dim,), (right_dim,)), ((), ())), preferred_element_type=f32
    )


def pieces(value):
    high = lax.reduce_precision(value, 8, 7)
    middle = lax.reduce_precision(value - high, 8, 7)
    return jnp.stack([high, middle, value - high - middle]).astype(bf16)


def first_products(got, gate_w, up_w, down_w, parts, tok, low, head, wide_head):
    width, cols = tok.shape[1], got.shape[2]
    n_gy = width // cols
    n_yl = got.shape[0] // n_gy
    half = tok.shape[0]
    rows = half // n_yl
    chip_units = down_w.shape[0]
    for z in range(n_gy):
        at = slice(z * cols, (z + 1) * cols)
        for y in range(n_yl):
            tok[y * rows : (y + 1) * rows, at] = got[y * n_gy + z, :rows]
            low[y * rows : (y + 1) * rows, at] = got[y * n_gy + z, rows : 2 * rows]
        head[:, at] = got[z, 2 * rows :]
        for r in range(0, 128, 16):
            wide_head[r : r + 16, at] = got[z, 2 * rows :]
    parts[:, :half] = dot(gate_w[:chip_units], tok[...], 1, 1).astype(bf16)
    parts[:, half : 2 * half] = dot(up_w[:chip_units], tok[...], 1, 1).astype(bf16)
    parts[:, 2 * half : 3 * half] = dot(down_w[...], low[...], 1, 1).astype(bf16)
    v = dot(down_w[...], wide_head[...], 1, 1)
    high = v.astype(bf16).astype(f32)
    lane = lax.broadcasted_iota(jnp.int32, v.shape, 1)
    v = jnp.where(lane == 0, high, jnp.where(lane == 1, v - high, 0.0))
    parts[:, 3 * half :] = v.astype(bf16)


def hidden_units(place, got, own_terms, sent):
    n_gz, own, lanes = got.shape
    half = sent.shape[2]
    n_seq = half // SEQ_LEN
    sums = got[0].astype(f32)
    for j in range(1, n_gz):
        sums += got[j].astype(f32)
    gate_sum, up_sum, hidden_grad = (sums[:, i * half : (i + 1) * half] for i in range(3))
    head_down = sums[:, 3 * half : 3 * half + 1] + sums[:, 3 * half + 1 : 3 * half + 2]
    gate_sigmoid = jax.nn.sigmoid(gate_sum)
    silu_gate = gate_sum * gate_sigmoid
    hidden = (silu_gate * up_sum).astype(bf16).astype(f32)
    gate_slope = up_sum * gate_sigmoid * (1.0 + gate_sum * (1.0 - gate_sigmoid))

    row = lax.broadcasted_iota(jnp.int32, (8, half), 0)
    lane = lax.broadcasted_iota(jnp.int32, (8, half), 1)
    blank = jnp.zeros((128 - own, half), f32)

    def picked(value, first):
        pick = (lane == (row - first) * SEQ_LEN + SEQ_LEN - 1) & (row >= first) & (row < first + n_seq)
        value = jnp.concatenate([value * head_down, blank], axis=0).astype(bf16)
        return dot(jnp.where(pick, 1.0, 0.0).astype(bf16), value, 1, 1)

    unit = picked(gate_slope, 0) + picked(silu_gate, n_seq)
    unit = jnp.concatenate([unit, jnp.zeros((8, half - 128), f32)], axis=1)
    unit = pltpu.roll(unit, place[0], 1)

    terms = jnp.sum(hidden * head_down, axis=0, keepdims=True) + own_terms[...]
    for s in range(n_seq):
        rest = jnp.sum(jnp.where(lane[:1] == s * SEQ_LEN + SEQ_LEN - 1, terms, 0.0), axis=1, keepdims=True)
        for i in range(3):
            piece = rest.astype(bf16).astype(f32)
            unit += jnp.where((row == 0) & (lane == n_gz * own + i * n_seq + s), piece, 0.0)
            rest = rest - piece
    mine = jnp.concatenate([hidden_grad * gate_slope, hidden_grad * silu_gate, hidden, unit], axis=0)
    mine = mine.astype(bf16)
    for j in range(n_gz):
        sent[j] = mine


def token_gradients(everyone, gate_w, up_w, sent, full):
    width = gate_w.shape[1]
    n_gz, n_rows, half = everyone.shape
    own = (n_rows - 8) // 3
    n_plane, piece_rows, cols = sent.shape
    n_gy, rows = width // cols, piece_rows - 16
    unit = jnp.zeros((8, half), f32)
    for j in range(n_gz):
        block = everyone[j].astype(f32)
        for i in range(2):
            full[i, j * own : (j + 1) * own] = block[i * own : (i + 1) * own]
        unit += block[3 * own :]
    for i in range(2):
        full[i, n_gz * own :] = jnp.zeros((full.shape[1] - n_gz * own, half), f32)
    unit = unit.astype(bf16)
    gate_t, up_t = (full[i].T.astype(bf16) for i in range(2))
    step = 2 * cols
    for c in range(0, width, step):
        part = dot(gate_t, gate_w[:, c : c + step], 1, 0) + dot(up_t, up_w[:, c : c + step], 1, 0)
        units_here = (
            dot(unit, gate_w[:, c : c + step], 1, 0)[:4] + dot(unit, up_w[:, c : c + step], 1, 0)[4:]
        )
        for z in range(c // cols, (c + step) // cols):
            at = slice(z * cols - c, (z + 1) * cols - c)
            for y in range(n_plane // n_gy):
                piece = y * n_gy + z
                sent[piece, :rows] = part[y * rows : (y + 1) * rows, at].astype(bf16)
                row = lax.broadcasted_iota(jnp.int32, (16, cols), 0)
                sent[piece, rows:] = jnp.where(row == 0, units_here[y : y + 1, at], 0.0).astype(bf16)


def body(tokens, gate_weight, up_weight, down_weight, reward_head, lm_grad, pair_index):
    n_yl, n_gy = lax.axis_size("yl"), lax.axis_size("gy")
    n_plane, n_gz = n_yl * n_gy, lax.axis_size(GZ)
    rows, cols = tokens.shape
    units, width = gate_weight.shape
    my_seq = lax.axis_index(("yl", "co"))
    core = lax.axis_index("co")

    def chip_block(weight, padding):
        parts = [weight, lax.ppermute(weight, "co", SWAP), jnp.zeros((padding, width), bf16)]
        return jnp.concatenate(parts, axis=0)

    padding = -2 * units % 128
    gate_w, up_w = chip_block(gate_weight, padding), chip_block(up_weight, padding)
    down_w = chip_block(down_weight, 0)

    head_rows = jnp.broadcast_to(reward_head[None, :], (16, cols))
    got = to_all(jnp.concatenate([tokens, lm_grad.astype(bf16), head_rows], axis=0), PLANE, n_plane)

    half, own = n_yl * rows, 2 * units // n_gz
    whole = pl.BlockSpec(memory_space=pltpu.VMEM)
    grant = pltpu.CompilerParams(vmem_limit_bytes=40 * 2**20)
    parts, tok_half, low_half, head_vec = pl.pallas_call(
        first_products,
        out_shape=(
            jax.ShapeDtypeStruct((2 * units, 3 * half + 128), bf16),
            jax.ShapeDtypeStruct((half, width), bf16),
            jax.ShapeDtypeStruct((half, width), bf16),
            jax.ShapeDtypeStruct((16, width), bf16),
        ),
        in_specs=[whole] * 4,
        out_specs=(whole,) * 4,
        scratch_shapes=[pltpu.VMEM((128, width), bf16)],
        compiler_params=grant,
        cost_estimate=pl.CostEstimate(
            flops=4 * units * width * (3 * half + 128), bytes_accessed=12 * 2**20, transcendentals=0
        ),
        name="first_products",
    )(got, gate_w, up_w, down_w)
    head_vec = head_vec[:1]
    sums_got = exchange(parts.reshape(n_gz, own, 3 * half + 128), GZ)

    own_term = jnp.sum(tokens[rows - 1].astype(f32) * reward_head.astype(f32))
    spot = lax.axis_index("yl") * rows + rows - 1
    own_terms = jnp.where(jnp.arange(half)[None, :] == spot, own_term, 0.0)
    to_send = pl.pallas_call(
        hidden_units,
        out_shape=jax.ShapeDtypeStruct((n_gz, 3 * own + 8, half), bf16),
        in_specs=[pl.BlockSpec(memory_space=pltpu.SMEM), whole, whole],
        out_specs=whole,
        compiler_params=grant,
        cost_estimate=pl.CostEstimate(
            flops=40 * own * half, bytes_accessed=4 * 2**20, transcendentals=own * half
        ),
        name="hidden_units",
    )((lax.axis_index(GZ) * own).astype(jnp.int32)[None], sums_got, own_terms)
    everyone = exchange(to_send, GZ)
    core_terms = jnp.sum(
        everyone[:, 3 * own, 2 * units : 2 * units + 3 * n_yl].astype(f32).reshape(n_gz * 3, n_yl), axis=0
    )
    pair_terms = jnp.stack([core_terms, lax.ppermute(core_terms, "co", SWAP)])
    sent = pl.pallas_call(
        token_gradients,
        out_shape=jax.ShapeDtypeStruct((n_plane, rows + 16, cols), bf16),
        in_specs=[whole] * 3,
        out_specs=whole,
        scratch_shapes=[pltpu.VMEM((2, 2 * units + padding, half), f32)],
        compiler_params=grant,
        cost_estimate=pl.CostEstimate(
            flops=8 * units * width * half, bytes_accessed=5 * 2**20, transcendentals=0
        ),
        name="token_gradients",
    )(everyone, gate_w, up_w)
    term_row = pieces(pair_terms).reshape(1, 1, 6 * n_yl)
    sent = lax.dynamic_update_slice(
        sent, jnp.broadcast_to(term_row, (n_plane, 1, 6 * n_yl)), (0, rows + 1, 0)
    )
    sent, everyone = lax.optimization_barrier((sent, everyone))
    gate_g, up_g, hid = (
        everyone[:, i * own : (i + 1) * own].reshape(2 * units, half) for i in range(3)
    )
    units_at = jnp.sum(everyone[:, 3 * own :, : 2 * units].astype(f32), axis=0).astype(bf16)
    gate_u, up_u = units_at[:n_yl], units_at[n_yl:]
    token_sum = jnp.sum(exchange(sent, PLANE).astype(f32), axis=0)

    both = jnp.sum(token_sum[rows + 1, : 6 * n_yl].reshape(3, 2, n_yl), axis=0)
    sequence = jnp.arange(2 * n_yl, dtype=jnp.int32)
    rewards = jnp.where(sequence % 2 == core, jnp.repeat(both[0], 2), jnp.repeat(both[1], 2))
    chosen_hot = (pair_index[:, 0:1] == sequence[None, :]).astype(f32)
    rejected_hot = (pair_index[:, 1:2] == sequence[None, :]).astype(f32)
    margin = jnp.sum((chosen_hot - rejected_hot) * rewards[None, :], axis=1)
    pair_weight = jax.nn.sigmoid(-margin)
    scaled = reward_weight * jnp.sum((rejected_hot - chosen_hot) * pair_weight[:, None], axis=0)
    by_core = scaled.reshape(n_yl, 2)
    core_coefs = jnp.where(core == 0, by_core[:, 0], by_core[:, 1])
    sib_coefs = jnp.where(core == 0, by_core[:, 1], by_core[:, 0])
    coefs = jnp.concatenate([core_coefs, sib_coefs])
    my_coef = jnp.sum(jnp.where(sequence == my_seq, scaled, 0.0))

    row = jnp.arange(rows)[:, None]
    head_term = my_coef * (reward_head.astype(f32) + token_sum[rows])
    grad_tokens = lm_grad + token_sum[:rows] + jnp.where(row == rows - 1, head_term[None, :], 0.0)

    loss_scale = 1.0 / jnp.sqrt(f32(rows * 2 * n_yl))
    tok_sib = lax.ppermute(tok_half, "co", SWAP)
    low_sib = lax.ppermute(low_half, "co", SWAP)
    unit_swap = lax.ppermute(jnp.concatenate([gate_u[:, units:], up_u[:, units:]], axis=0), "co", SWAP)
    gate_u8 = jnp.concatenate([gate_u[:, :units], unit_swap[:n_yl]], axis=0)
    up_u8 = jnp.concatenate([up_u[:, :units], unit_swap[n_yl:]], axis=0)

    def last_rows(value):
        return value.reshape(n_yl, rows, width)[:, rows - 1]

    last_tok = jnp.concatenate([last_rows(tok_half), last_rows(tok_sib)], axis=0).astype(f32)
    last_tok = (last_tok * coefs[:, None]).astype(bf16)
    head_term8 = (coefs[:, None] * head_vec.astype(f32)).astype(bf16)

    def weight_grad(full, own_right, sib_right, last_left, last_right):
        from_sib = lax.ppermute(full[units:], "co", SWAP)
        total = lax.optimization_barrier(
            (dot(full[:units], own_right, 1, 0) + dot(from_sib, sib_right, 1, 0)) * loss_scale
        )
        if last_left is None:
            ends = [v.reshape(units, n_yl, rows)[:, :, rows - 1] for v in (full[:units], from_sib)]
            last_left = jnp.concatenate(ends, axis=1).T
        return total + dot(last_left, last_right, 0, 0) * loss_scale

    grad_gate = weight_grad(gate_g, tok_half, tok_sib, gate_u8, last_tok)
    grad_up = weight_grad(up_g, tok_half, tok_sib, up_u8, last_tok)
    grad_down = weight_grad(hid, low_half, low_sib, None, head_term8)
    return grad_tokens, grad_gate, grad_up, grad_down, rewards


def solution(mesh):
    fine = Mesh(mesh.devices.reshape(4, 2, 8, 2, 4), FINE)
    gx, gz = ("yl", "co"), GZ
    weight = P(("gy",) + gx, gz)
    act = P(gx, gz + ("gy",))
    return jax.shard_map(
        body,
        mesh=fine,
        in_specs=(act, weight, weight, weight, P(gz + ("gy",)), act, P()),
        out_specs=(act, weight, weight, weight, P()),
        check_vma=False,
    )
```

```python
import functools

import jax
import jax.numpy as jnp
from jax import lax
from jax.experimental import pallas as pl
from jax.experimental.pallas import tpu as pltpu
from jax.sharding import Mesh, PartitionSpec as P

SEQ_LEN = 128
reward_weight = 64.0
FINE = ("yl", "co", "gy", "yh", "xx")
PLANE = ("yl", "gy")
GZ = ("yh", "xx")
SWAP = [(0, 1), (1, 0)]
f32, bf16 = jnp.float32, jnp.bfloat16


def exchange(pieces, axes):
    return lax.all_to_all(pieces, axes, 0, 0)


def to_all(value, axes, count):
    return exchange(jnp.broadcast_to(value[None], (count,) + value.shape), axes)


def dot(left, right, left_dim, right_dim):
    return lax.dot_general(
        left, right, (((left_dim,), (right_dim,)), ((), ())), preferred_element_type=f32
    )


def pieces(value):
    high = lax.reduce_precision(value, 8, 7)
    middle = lax.reduce_precision(value - high, 8, 7)
    return jnp.stack([high, middle, value - high - middle]).astype(bf16)


def token_products(tok_got, gate_w, up_w, down_w, parts, tok, head, wide_head):
    width, cols = tok.shape[1], tok_got.shape[2]
    n_gy = width // cols
    n_yl = tok_got.shape[0] // n_gy
    rows = tok.shape[0] // n_yl
    chip_units, half = down_w.shape[0], tok.shape[0]
    for z in range(n_gy):
        at = slice(z * cols, (z + 1) * cols)
        for y in range(n_yl):
            tok[y * rows : (y + 1) * rows, at] = tok_got[y * n_gy + z, :rows]
        head[:, at] = tok_got[z, rows:]
        for r in range(0, 128, 16):
            wide_head[r : r + 16, at] = tok_got[z, rows:]
    parts[:, :half] = dot(gate_w[:chip_units], tok[...], 1, 1).astype(bf16)
    parts[:, half : 2 * half] = dot(up_w[:chip_units], tok[...], 1, 1).astype(bf16)
    v = dot(down_w[...], wide_head[...], 1, 1)
    high = v.astype(bf16).astype(f32)
    lane = lax.broadcasted_iota(jnp.int32, v.shape, 1)
    v = jnp.where(lane == 0, high, jnp.where(lane == 1, v - high, 0.0))
    parts[:, 2 * half :] = v.astype(bf16)


def cotangent_products(low_got, down_w, parts, low):
    n_gy, n_yl, rows, cols = low_got.shape
    for y in range(n_yl):
        for z in range(n_gy):
            low[y * rows : (y + 1) * rows, z * cols : (z + 1) * cols] = low_got[z, y]
    parts[...] = dot(down_w[...], low[...], 1, 1).astype(bf16)


def split_sums(in_two, place, got, keep, give, total):
    own = keep.shape[0]
    sums = got[0].astype(f32)
    for j in range(1, got.shape[0]):
        sums += got[j].astype(f32)
    total[...] = sums
    keep[...] = total[pl.ds(pl.multiple_of(place[0] * own, 8), own), :]
    away = total[pl.ds(pl.multiple_of((1 - place[0]) * own, 8), own), :]
    give[...] = away.astype(bf16)
    if in_two:
        ends = away[:, -128:]
        lost = pltpu.roll(ends - ends.astype(bf16).astype(f32), 1, 1)
        lane = lax.broadcasted_iota(jnp.int32, ends.shape, 1)
        give[:, -128:] = jnp.where(lane == 1, ends + lost, ends).astype(bf16)


def hidden_units(chip_units, place, keep, got, back_keep, back_got, own_terms, mine):
    own, half = back_keep.shape
    n_seq = half // SEQ_LEN
    sums = keep[...] + got[...].astype(f32)
    hidden_grad = back_keep[...] + back_got[...].astype(f32)
    gate_sum, up_sum = sums[:, :half], sums[:, half : 2 * half]
    head_down = sums[:, 2 * half : 2 * half + 1] + sums[:, 2 * half + 1 : 2 * half + 2]
    gate_sigmoid = jax.nn.sigmoid(gate_sum)
    silu_gate = gate_sum * gate_sigmoid
    hidden = (silu_gate * up_sum).astype(bf16).astype(f32)
    gate_slope = up_sum * gate_sigmoid * (1.0 + gate_sum * (1.0 - gate_sigmoid))

    row = lax.broadcasted_iota(jnp.int32, (8, half), 0)
    lane = lax.broadcasted_iota(jnp.int32, (8, half), 1)
    blank = jnp.zeros((128 - own, half), f32)

    def picked(value, first):
        pick = (lane == (row - first) * SEQ_LEN + SEQ_LEN - 1) & (row >= first) & (row < first + n_seq)
        value = jnp.concatenate([value * head_down, blank], axis=0).astype(bf16)
        return dot(jnp.where(pick, 1.0, 0.0).astype(bf16), value, 1, 1)

    unit = picked(gate_slope, 0) + picked(silu_gate, n_seq)
    unit = jnp.concatenate([unit, jnp.zeros((8, half - 128), f32)], axis=1)
    unit = pltpu.roll(unit, place[0], 1)

    terms = jnp.sum(hidden * head_down, axis=0, keepdims=True) + own_terms[...]
    for s in range(n_seq):
        rest = jnp.sum(jnp.where(lane[:1] == s * SEQ_LEN + SEQ_LEN - 1, terms, 0.0), axis=1, keepdims=True)
        for i in range(3):
            piece = rest.astype(bf16).astype(f32)
            unit += jnp.where((row == 0) & (lane == chip_units + i * n_seq + s), piece, 0.0)
            rest = rest - piece
    rows = jnp.concatenate([hidden_grad * gate_slope, hidden_grad * silu_gate, hidden, unit], axis=0)
    mine[...] = rows.astype(bf16)


def token_gradients(everyone, gate_w, up_w, sent, full):
    width = gate_w.shape[1]
    n_gz, n_rows, half = everyone.shape
    own = (n_rows - 8) // 3
    n_plane, piece_rows, cols = sent.shape
    n_gy, rows = width // cols, piece_rows - 16
    unit = jnp.zeros((8, half), f32)
    for j in range(n_gz):
        block = everyone[j].astype(f32)
        for i in range(2):
            full[i, j * own : (j + 1) * own] = block[i * own : (i + 1) * own]
        unit += block[3 * own :]
    for i in range(2):
        full[i, n_gz * own :] = jnp.zeros((full.shape[1] - n_gz * own, half), f32)
    unit = unit.astype(bf16)
    gate_t, up_t = (full[i].T.astype(bf16) for i in range(2))
    step = 2 * cols
    for c in range(0, width, step):
        part = dot(gate_t, gate_w[:, c : c + step], 1, 0) + dot(up_t, up_w[:, c : c + step], 1, 0)
        units_here = (
            dot(unit, gate_w[:, c : c + step], 1, 0)[:4] + dot(unit, up_w[:, c : c + step], 1, 0)[4:]
        )
        for z in range(c // cols, (c + step) // cols):
            at = slice(z * cols - c, (z + 1) * cols - c)
            for y in range(n_plane // n_gy):
                piece = y * n_gy + z
                sent[piece, :rows] = part[y * rows : (y + 1) * rows, at].astype(bf16)
                row = lax.broadcasted_iota(jnp.int32, (16, cols), 0)
                sent[piece, rows:] = jnp.where(row == 0, units_here[y : y + 1, at], 0.0).astype(bf16)


def body(tokens, gate_weight, up_weight, down_weight, reward_head, lm_grad, pair_index):
    n_yl, n_gy = lax.axis_size("yl"), lax.axis_size("gy")
    n_plane, n_gz = n_yl * n_gy, lax.axis_size(GZ)
    rows, cols = tokens.shape
    units, width = gate_weight.shape
    my_seq = lax.axis_index(("yl", "co"))
    core = lax.axis_index("co")

    def chip_block(weight, padding):
        parts = [weight, lax.ppermute(weight, "co", SWAP), jnp.zeros((padding, width), bf16)]
        return jnp.concatenate(parts, axis=0)

    padding = -2 * units % 128
    gate_w, up_w = chip_block(gate_weight, padding), chip_block(up_weight, padding)
    down_w = chip_block(down_weight, 0)

    low_got = to_all(lm_grad.astype(bf16), "yl", n_yl)
    head_rows = jnp.broadcast_to(reward_head[None, :], (16, cols))
    tok_block = jnp.concatenate([tokens, head_rows], axis=0)
    low_got, tok_block = lax.optimization_barrier((low_got, tok_block))
    low_got = lax.all_gather(low_got, "gy")
    tok_got = to_all(tok_block, PLANE, n_plane)

    half, own = n_yl * rows, 2 * units // n_gz
    whole = pl.BlockSpec(memory_space=pltpu.VMEM)
    grant = pltpu.CompilerParams(vmem_limit_bytes=40 * 2**20)
    parts, tok_half, head_vec = pl.pallas_call(
        token_products,
        out_shape=(
            jax.ShapeDtypeStruct((2 * units, 2 * half + 128), bf16),
            jax.ShapeDtypeStruct((half, width), bf16),
            jax.ShapeDtypeStruct((16, width), bf16),
        ),
        in_specs=[whole] * 4,
        out_specs=(whole,) * 3,
        scratch_shapes=[pltpu.VMEM((128, width), bf16)],
        compiler_params=grant,
        cost_estimate=pl.CostEstimate(
            flops=4 * units * width * (2 * half + 128), bytes_accessed=8 * 2**20, transcendentals=0
        ),
        name="token_products",
    )(tok_got, gate_w, up_w, down_w)
    head_vec = head_vec[:1]
    n_xx = lax.axis_size("xx")
    first = exchange(parts.reshape(n_xx, 2 * own, 2 * half + 128), "xx")
    y_half = lax.axis_index("yh").astype(jnp.int32)[None]
    scalar = pl.BlockSpec(memory_space=pltpu.SMEM)

    def halves(got, in_two):
        lanes = got.shape[2]
        keep, give = pl.pallas_call(
            functools.partial(split_sums, in_two),
            out_shape=(jax.ShapeDtypeStruct((own, lanes), f32), jax.ShapeDtypeStruct((own, lanes), bf16)),
            in_specs=[scalar, whole],
            out_specs=(whole,) * 2,
            scratch_shapes=[pltpu.VMEM((2 * own, lanes), f32)],
            compiler_params=grant,
            cost_estimate=pl.CostEstimate(flops=8 * own * lanes, bytes_accessed=22 * own * lanes, transcendentals=0),
            name="split_sums",
        )(y_half, got)
        return keep, lax.ppermute(give, "yh", SWAP)

    back_parts, low_half = pl.pallas_call(
        cotangent_products,
        out_shape=(
            jax.ShapeDtypeStruct((2 * units, half), bf16),
            jax.ShapeDtypeStruct((half, width), bf16),
        ),
        in_specs=[whole] * 2,
        out_specs=(whole,) * 2,
        compiler_params=grant,
        cost_estimate=pl.CostEstimate(
            flops=4 * units * width * half, bytes_accessed=5 * 2**20, transcendentals=0
        ),
        name="cotangent_products",
    )(low_got, down_w)
    first, back_parts = lax.optimization_barrier((first, back_parts))
    second = exchange(back_parts.reshape(n_xx, 2 * own, half), "xx")
    sums, sums_got = halves(first, True)
    back, back_got = halves(second, False)

    own_term = jnp.sum(tokens[rows - 1].astype(f32) * reward_head.astype(f32))
    spot = lax.axis_index("yl") * rows + rows - 1
    own_terms = jnp.where(jnp.arange(half)[None, :] == spot, own_term, 0.0)
    place = (lax.axis_index(("xx", "yh")) * own).astype(jnp.int32)[None]
    mine = pl.pallas_call(
        functools.partial(hidden_units, 2 * units),
        out_shape=jax.ShapeDtypeStruct((3 * own + 8, half), bf16),
        in_specs=[scalar] + [whole] * 5,
        out_specs=whole,
        compiler_params=grant,
        cost_estimate=pl.CostEstimate(
            flops=40 * own * half, bytes_accessed=12 * own * half, transcendentals=own * half
        ),
        name="hidden_units",
    )(place, sums, sums_got, back, back_got, own_terms)
    other = lax.ppermute(mine, "yh", SWAP)
    pair = jnp.stack([jnp.where(y_half == 0, mine, other), jnp.where(y_half == 0, other, mine)])
    everyone = to_all(pair, "xx", n_xx).reshape(n_gz, 3 * own + 8, half)
    core_terms = jnp.sum(
        everyone[:, 3 * own, 2 * units : 2 * units + 3 * n_yl].astype(f32).reshape(n_gz * 3, n_yl), axis=0
    )
    pair_terms = jnp.stack([core_terms, lax.ppermute(core_terms, "co", SWAP)])
    sent = pl.pallas_call(
        token_gradients,
        out_shape=jax.ShapeDtypeStruct((n_plane, rows + 16, cols), bf16),
        in_specs=[whole] * 3,
        out_specs=whole,
        scratch_shapes=[pltpu.VMEM((2, 2 * units + padding, half), f32)],
        compiler_params=grant,
        cost_estimate=pl.CostEstimate(
            flops=8 * units * width * half, bytes_accessed=5 * 2**20, transcendentals=0
        ),
        name="token_gradients",
    )(everyone, gate_w, up_w)
    term_row = pieces(pair_terms).reshape(1, 1, 6 * n_yl)
    sent = lax.dynamic_update_slice(
        sent, jnp.broadcast_to(term_row, (n_plane, 1, 6 * n_yl)), (0, rows + 1, 0)
    )
    sent, everyone = lax.optimization_barrier((sent, everyone))
    gate_g, up_g, hid = (
        everyone[:, i * own : (i + 1) * own].reshape(2 * units, half) for i in range(3)
    )
    units_at = jnp.sum(everyone[:, 3 * own :, : 2 * units].astype(f32), axis=0).astype(bf16)
    gate_u, up_u = units_at[:n_yl], units_at[n_yl:]
    token_sum = jnp.sum(exchange(sent, PLANE).astype(f32), axis=0)

    both = jnp.sum(token_sum[rows + 1, : 6 * n_yl].reshape(3, 2, n_yl), axis=0)
    sequence = jnp.arange(2 * n_yl, dtype=jnp.int32)
    rewards = jnp.where(sequence % 2 == core, jnp.repeat(both[0], 2), jnp.repeat(both[1], 2))
    chosen_hot = (pair_index[:, 0:1] == sequence[None, :]).astype(f32)
    rejected_hot = (pair_index[:, 1:2] == sequence[None, :]).astype(f32)
    margin = jnp.sum((chosen_hot - rejected_hot) * rewards[None, :], axis=1)
    pair_weight = jax.nn.sigmoid(-margin)
    scaled = reward_weight * jnp.sum((rejected_hot - chosen_hot) * pair_weight[:, None], axis=0)
    by_core = scaled.reshape(n_yl, 2)
    core_coefs = jnp.where(core == 0, by_core[:, 0], by_core[:, 1])
    sib_coefs = jnp.where(core == 0, by_core[:, 1], by_core[:, 0])
    coefs = jnp.concatenate([core_coefs, sib_coefs])
    my_coef = jnp.sum(jnp.where(sequence == my_seq, scaled, 0.0))

    row = jnp.arange(rows)[:, None]
    head_term = my_coef * (reward_head.astype(f32) + token_sum[rows])
    grad_tokens = lm_grad + token_sum[:rows] + jnp.where(row == rows - 1, head_term[None, :], 0.0)

    loss_scale = 1.0 / jnp.sqrt(f32(rows * 2 * n_yl))
    tok_sib = lax.ppermute(tok_half, "co", SWAP)
    low_sib = lax.ppermute(low_half, "co", SWAP)
    unit_swap = lax.ppermute(jnp.concatenate([gate_u[:, units:], up_u[:, units:]], axis=0), "co", SWAP)
    gate_u8 = jnp.concatenate([gate_u[:, :units], unit_swap[:n_yl]], axis=0)
    up_u8 = jnp.concatenate([up_u[:, :units], unit_swap[n_yl:]], axis=0)

    def last_rows(value):
        return value.reshape(n_yl, rows, width)[:, rows - 1]

    last_tok = jnp.concatenate([last_rows(tok_half), last_rows(tok_sib)], axis=0).astype(f32)
    last_tok = (last_tok * coefs[:, None]).astype(bf16)
    head_term8 = (coefs[:, None] * head_vec.astype(f32)).astype(bf16)

    def weight_grad(full, own_right, sib_right, last_left, last_right):
        from_sib = lax.ppermute(full[units:], "co", SWAP)
        total = lax.optimization_barrier(
            (dot(full[:units], own_right, 1, 0) + dot(from_sib, sib_right, 1, 0)) * loss_scale
        )
        if last_left is None:
            ends = [v.reshape(units, n_yl, rows)[:, :, rows - 1] for v in (full[:units], from_sib)]
            last_left = jnp.concatenate(ends, axis=1).T
        return total + dot(last_left, last_right, 0, 0) * loss_scale

    grad_gate = weight_grad(gate_g, tok_half, tok_sib, gate_u8, last_tok)
    grad_up = weight_grad(up_g, tok_half, tok_sib, up_u8, last_tok)
    grad_down = weight_grad(hid, low_half, low_sib, None, head_term8)
    return grad_tokens, grad_gate, grad_up, grad_down, rewards


def solution(mesh):
    fine = Mesh(mesh.devices.reshape(4, 2, 8, 2, 4), FINE)
    gx, gz = ("yl", "co"), GZ
    weight = P(("gy",) + gx, gz)
    act = P(gx, gz + ("gy",))
    return jax.shard_map(
        body,
        mesh=fine,
        in_specs=(act, weight, weight, weight, P(gz + ("gy",)), act, P()),
        out_specs=(act, weight, weight, weight, P()),
        check_vma=False,
    )
```

```python
import functools

import jax
import jax.numpy as jnp
from jax import lax
from jax.experimental import pallas as pl
from jax.experimental.pallas import tpu as pltpu
from jax.sharding import Mesh, PartitionSpec as P

SEQ_LEN = 128
reward_weight = 64.0
FINE = ("yl", "co", "gy", "yh", "xx")
PLANE = ("yl", "gy")
GZ = ("yh", "xx")
SWAP = [(0, 1), (1, 0)]
f32, bf16 = jnp.float32, jnp.bfloat16


def exchange(pieces, axes):
    return lax.all_to_all(pieces, axes, 0, 0)


def to_all(value, axes, count):
    return exchange(jnp.broadcast_to(value[None], (count,) + value.shape), axes)


def dot(left, right, left_dim, right_dim):
    return lax.dot_general(
        left, right, (((left_dim,), (right_dim,)), ((), ())), preferred_element_type=f32
    )


def token_products(tok_got, gate_w, up_w, parts, tok):
    n_plane, rows, cols = tok_got.shape
    half, width = tok.shape
    n_gy, n_yl = width // cols, half // rows
    chip_units = parts.shape[0]
    for y in range(n_yl):
        for z in range(n_gy):
            tok[y * rows : (y + 1) * rows, z * cols : (z + 1) * cols] = tok_got[y * n_gy + z]
    parts[:, :half] = dot(gate_w[:chip_units], tok[...], 1, 1).astype(bf16)
    parts[:, half:] = dot(up_w[:chip_units], tok[...], 1, 1).astype(bf16)


def cotangent_products(core, low_got, tok, tok_sib, gate_w, up_w, down_w, parts, low, head, wide):
    n_gy, _, cols = low_got.shape
    half, width = low.shape
    n_yl = half // SEQ_LEN
    chip_units = down_w.shape[0]
    for z in range(n_gy):
        at = slice(z * cols, (z + 1) * cols)
        low[:, at] = low_got[z, :half]
        head[:, at] = low_got[z, half:]
    ends = [
        [ref[(y + 1) * SEQ_LEN - 16 : (y + 1) * SEQ_LEN].astype(f32)[15:] for y in range(n_yl)]
        for ref in (tok, tok_sib)
    ]
    here, there = (jnp.concatenate(rows, axis=0) for rows in ends)
    ends = [jnp.where(core[0] == 0, here, there), jnp.where(core[0] == 0, there, here)]
    wide[:16] = head[...]
    wide[16:32] = jnp.concatenate(ends + [jnp.zeros((16 - 2 * n_yl, width), f32)], axis=0).astype(bf16)
    wide[32:] = jnp.zeros((96, width), bf16)
    parts[:, :half] = dot(down_w[...], low[...], 1, 1).astype(bf16)
    v = dot(down_w[...], wide[...], 1, 1)
    gate = dot(gate_w[:chip_units], wide[...], 1, 1)
    up = pltpu.roll(dot(up_w[:chip_units], wide[...], 1, 1), 16, 1)
    high = v.astype(bf16).astype(f32)
    lane = lax.broadcasted_iota(jnp.int32, v.shape, 1)
    more = jnp.where(lane == 0, high, jnp.where(lane == 1, v - high, 0.0))
    more = jnp.where((lane >= 16) & (lane < 32), gate, jnp.where((lane >= 32) & (lane < 48), up, more))
    parts[:, half:] = more.astype(bf16)


def split_sums(in_two, place, got, keep, give, total):
    own = keep.shape[0]
    sums = got[0].astype(f32)
    for j in range(1, got.shape[0]):
        sums += got[j].astype(f32)
    total[...] = sums
    keep[...] = total[pl.ds(pl.multiple_of(place[0] * own, 8), own), :]
    away = total[pl.ds(pl.multiple_of((1 - place[0]) * own, 8), own), :]
    give[...] = away.astype(bf16)
    if in_two:
        ends = away[:, -128:]
        lost = pltpu.roll(ends - ends.astype(bf16).astype(f32), 1, 1)
        lane = lax.broadcasted_iota(jnp.int32, ends.shape, 1)
        give[:, -128:] = jnp.where(lane == 1, ends + lost, ends).astype(bf16)


def hidden_units(chip_units, place, keep, got, back_keep, back_got, tok_terms, mine):
    own, half = keep.shape[0], keep.shape[1] // 2
    n_seq = half // SEQ_LEN
    sums = keep[...] + got[...].astype(f32)
    back = back_keep[...] + back_got[...].astype(f32)
    gate_sum, up_sum, hidden_grad = sums[:, :half], sums[:, half:], back[:, :half]
    more = back[:, half:]
    head_down = more[:, 0:1] + more[:, 1:2]
    gate_sigmoid = jax.nn.sigmoid(gate_sum)
    silu_gate = gate_sum * gate_sigmoid
    hidden = (silu_gate * up_sum).astype(bf16).astype(f32)
    gate_slope = up_sum * gate_sigmoid * (1.0 + gate_sum * (1.0 - gate_sigmoid))

    row = lax.broadcasted_iota(jnp.int32, (8, half), 0)
    lane = lax.broadcasted_iota(jnp.int32, (8, half), 1)
    blank = jnp.zeros((128 - own, half), f32)

    def picked(value, first):
        pick = (lane == (row - first) * SEQ_LEN + SEQ_LEN - 1) & (row >= first) & (row < first + n_seq)
        value = jnp.concatenate([value * head_down, blank], axis=0).astype(bf16)
        return dot(jnp.where(pick, 1.0, 0.0).astype(bf16), value, 1, 1)

    unit = picked(gate_slope, 0) + picked(silu_gate, n_seq)
    unit = jnp.concatenate([unit, jnp.zeros((8, half - 128), f32)], axis=1)
    unit = pltpu.roll(unit, place[0], 1)

    last_hidden = (more * jax.nn.sigmoid(more) * pltpu.roll(more, 128 - 16, 1)).astype(bf16).astype(f32)
    terms = jnp.sum(last_hidden * head_down, axis=0, keepdims=True) + tok_terms[...]
    for s in range(2 * n_seq):
        rest = jnp.sum(jnp.where(lane[:1, :128] == 16 + s, terms, 0.0), axis=1, keepdims=True)
        for i in range(3):
            piece = rest.astype(bf16).astype(f32)
            unit += jnp.where((row == 0) & (lane == chip_units + 2 * i * n_seq + s), piece, 0.0)
            rest = rest - piece
    rows = jnp.concatenate([hidden_grad * gate_slope, hidden_grad * silu_gate, hidden, unit], axis=0)
    mine[...] = rows.astype(bf16)


def token_gradients(everyone, gate_w, up_w, sent, full):
    width = gate_w.shape[1]
    n_gz, n_rows, half = everyone.shape
    own = (n_rows - 8) // 3
    n_plane, piece_rows, cols = sent.shape
    n_gy, rows = width // cols, piece_rows - 16
    unit = jnp.zeros((8, half), f32)
    for j in range(n_gz):
        block = everyone[j].astype(f32)
        for i in range(2):
            full[i, j * own : (j + 1) * own] = block[i * own : (i + 1) * own]
        unit += block[3 * own :]
    terms = unit + pltpu.roll(unit, half - 8, 1) + pltpu.roll(unit, half - 16, 1)
    terms = pltpu.roll(terms, half - n_gz * own, 1)[:, :cols]
    lane = lax.broadcasted_iota(jnp.int32, terms.shape, 1)
    high = terms.astype(bf16).astype(f32)
    middle = (terms - high).astype(bf16).astype(f32)
    terms = jnp.where(
        lane < 8,
        high,
        jnp.where(lane < 16, pltpu.roll(middle, 8, 1), pltpu.roll(terms - high - middle, 16, 1)),
    )
    terms = jnp.where(lane < 24, terms, 0.0)[:1]
    for i in range(2):
        full[i, n_gz * own :] = jnp.zeros((full.shape[1] - n_gz * own, half), f32)
    unit = unit.astype(bf16)
    gate_t, up_t = (full[i].T.astype(bf16) for i in range(2))
    step = 2 * cols
    for c in range(0, width, step):
        part = dot(gate_t, gate_w[:, c : c + step], 1, 0) + dot(up_t, up_w[:, c : c + step], 1, 0)
        units_here = (
            dot(unit, gate_w[:, c : c + step], 1, 0)[:4] + dot(unit, up_w[:, c : c + step], 1, 0)[4:]
        )
        for z in range(c // cols, (c + step) // cols):
            at = slice(z * cols - c, (z + 1) * cols - c)
            for y in range(n_plane // n_gy):
                piece = y * n_gy + z
                sent[piece, :rows] = part[y * rows : (y + 1) * rows, at].astype(bf16)
                row = lax.broadcasted_iota(jnp.int32, (16, cols), 0)
                extra = jnp.where(row == 0, units_here[y : y + 1, at], jnp.where(row == 1, terms, 0.0))
                sent[piece, rows:] = extra.astype(bf16)


def body(tokens, gate_weight, up_weight, down_weight, reward_head, lm_grad, pair_index):
    n_yl, n_gy = lax.axis_size("yl"), lax.axis_size("gy")
    n_plane, n_gz = n_yl * n_gy, lax.axis_size(GZ)
    rows, cols = tokens.shape
    units, width = gate_weight.shape
    my_seq = lax.axis_index(("yl", "co"))
    core = lax.axis_index("co")

    def core_order(here, there):
        return [jnp.where(core == 0, here, there), jnp.where(core == 0, there, here)]

    def chip_block(weight, padding):
        parts = core_order(weight, lax.ppermute(weight, "co", SWAP))
        return jnp.concatenate(parts + [jnp.zeros((padding, width), bf16)], axis=0)

    padding = -2 * units % 128
    gate_w, up_w = chip_block(gate_weight, padding), chip_block(up_weight, padding)
    down_w = chip_block(down_weight, 0)

    half = n_yl * rows
    low_got = to_all(lm_grad.astype(bf16), "yl", n_yl).reshape(half, cols)
    low_got, tok_block = lax.optimization_barrier((low_got, tokens))
    head_rows = jnp.broadcast_to(reward_head[None, :], (16, cols))
    low_got = lax.all_gather(jnp.concatenate([low_got, head_rows], axis=0), "gy")
    tok_got = to_all(tok_block, PLANE, n_plane)

    own = 2 * units // n_gz
    whole, scalar = pl.BlockSpec(memory_space=pltpu.VMEM), pl.BlockSpec(memory_space=pltpu.SMEM)
    grant = pltpu.CompilerParams(vmem_limit_bytes=40 * 2**20)
    parts, tok_half = pl.pallas_call(
        token_products,
        out_shape=(
            jax.ShapeDtypeStruct((2 * units, 2 * half), bf16),
            jax.ShapeDtypeStruct((half, width), bf16),
        ),
        in_specs=[whole] * 3,
        out_specs=(whole,) * 2,
        compiler_params=grant,
        cost_estimate=pl.CostEstimate(
            flops=8 * units * width * half, bytes_accessed=8 * 2**20, transcendentals=0
        ),
        name="token_products",
    )(tok_got, gate_w, up_w)
    tok_sib = lax.ppermute(tok_half, "co", SWAP)

    n_xx = lax.axis_size("xx")
    first = exchange(parts.reshape(n_xx, 2 * own, 2 * half), "xx")
    y_half = lax.axis_index("yh").astype(jnp.int32)[None]

    def halves(got, in_two):
        lanes = got.shape[2]
        keep, give = pl.pallas_call(
            functools.partial(split_sums, in_two),
            out_shape=(jax.ShapeDtypeStruct((own, lanes), f32), jax.ShapeDtypeStruct((own, lanes), bf16)),
            in_specs=[scalar, whole],
            out_specs=(whole,) * 2,
            scratch_shapes=[pltpu.VMEM((2 * own, lanes), f32)],
            compiler_params=grant,
            cost_estimate=pl.CostEstimate(flops=8 * own * lanes, bytes_accessed=22 * own * lanes, transcendentals=0),
            name="split_sums",
        )(y_half, got)
        return keep, lax.ppermute(give, "yh", SWAP)

    back_parts, low_half, head_vec = pl.pallas_call(
        cotangent_products,
        out_shape=(
            jax.ShapeDtypeStruct((2 * units, half + 128), bf16),
            jax.ShapeDtypeStruct((half, width), bf16),
            jax.ShapeDtypeStruct((16, width), bf16),
        ),
        in_specs=[scalar] + [whole] * 6,
        out_specs=(whole,) * 3,
        scratch_shapes=[pltpu.VMEM((128, width), bf16)],
        compiler_params=grant,
        cost_estimate=pl.CostEstimate(
            flops=4 * units * width * (half + 384), bytes_accessed=5 * 2**20, transcendentals=0
        ),
        name="cotangent_products",
    )(core.astype(jnp.int32)[None], low_got, tok_half, tok_sib, gate_w, up_w, down_w)
    head_vec = head_vec[:1]
    first, back_parts = lax.optimization_barrier((first, back_parts))
    second = exchange(back_parts.reshape(n_xx, 2 * own, half + 128), "xx")
    sums, sums_got = halves(first, False)
    back, back_got = halves(second, True)

    own_term = jnp.sum(tokens[rows - 1].astype(f32) * reward_head.astype(f32))
    sib_term = lax.ppermute(own_term[None], "co", SWAP)[0]
    spot = jnp.arange(128)[None, :] - 16 - lax.axis_index("yl")
    first_term, second_term = core_order(own_term, sib_term)
    tok_terms = jnp.where(spot == 0, first_term, jnp.where(spot == n_yl, second_term, 0.0))
    place = (lax.axis_index(("xx", "yh")) * own).astype(jnp.int32)[None]
    mine = pl.pallas_call(
        functools.partial(hidden_units, 2 * units),
        out_shape=jax.ShapeDtypeStruct((3 * own + 8, half), bf16),
        in_specs=[scalar] + [whole] * 5,
        out_specs=whole,
        compiler_params=grant,
        cost_estimate=pl.CostEstimate(
            flops=40 * own * half, bytes_accessed=12 * own * half, transcendentals=own * half
        ),
        name="hidden_units",
    )(place, sums, sums_got, back, back_got, tok_terms)
    other = lax.ppermute(mine, "yh", SWAP)
    pair = jnp.stack([jnp.where(y_half == 0, mine, other), jnp.where(y_half == 0, other, mine)])
    everyone = to_all(pair, "xx", n_xx).reshape(n_gz, 3 * own + 8, half)
    sent = pl.pallas_call(
        token_gradients,
        out_shape=jax.ShapeDtypeStruct((n_plane, rows + 16, cols), bf16),
        in_specs=[whole] * 3,
        out_specs=whole,
        scratch_shapes=[pltpu.VMEM((2, 2 * units + padding, half), f32)],
        compiler_params=grant,
        cost_estimate=pl.CostEstimate(
            flops=8 * units * width * half, bytes_accessed=5 * 2**20, transcendentals=0
        ),
        name="token_gradients",
    )(everyone, gate_w, up_w)
    sent, everyone = lax.optimization_barrier((sent, everyone))
    gate_g, up_g, hid = (
        everyone[:, i * own : (i + 1) * own].reshape(2 * units, half) for i in range(3)
    )
    units_at = jnp.sum(everyone[:, 3 * own :, : 2 * units].astype(f32), axis=0).astype(bf16)
    token_sum = jnp.sum(exchange(sent, PLANE).astype(f32), axis=0)

    both = jnp.sum(token_sum[rows + 1, : 6 * n_yl].reshape(3, 2, n_yl), axis=0)
    sequence = jnp.arange(2 * n_yl, dtype=jnp.int32)
    rewards = both.T.reshape(2 * n_yl)
    chosen_hot = (pair_index[:, 0:1] == sequence[None, :]).astype(f32)
    rejected_hot = (pair_index[:, 1:2] == sequence[None, :]).astype(f32)
    margin = jnp.sum((chosen_hot - rejected_hot) * rewards[None, :], axis=1)
    pair_weight = jax.nn.sigmoid(-margin)
    scaled = reward_weight * jnp.sum((rejected_hot - chosen_hot) * pair_weight[:, None], axis=0)
    by_core = scaled.reshape(n_yl, 2)
    core_coefs = jnp.where(core == 0, by_core[:, 0], by_core[:, 1])
    sib_coefs = jnp.where(core == 0, by_core[:, 1], by_core[:, 0])
    coefs = jnp.concatenate([core_coefs, sib_coefs])
    my_coef = jnp.sum(jnp.where(sequence == my_seq, scaled, 0.0))

    row = jnp.arange(rows)[:, None]
    head_term = my_coef * (reward_head.astype(f32) + token_sum[rows])
    grad_tokens = lm_grad + token_sum[:rows] + jnp.where(row == rows - 1, head_term[None, :], 0.0)

    loss_scale = 1.0 / jnp.sqrt(f32(rows * 2 * n_yl))
    low_sib = lax.ppermute(low_half, "co", SWAP)

    def core_parts(value, axis):
        return [
            lax.dynamic_slice_in_dim(value, which * units, units, axis) for which in (core, 1 - core)
        ]

    unit_here, unit_there = core_parts(units_at, 1)
    unit_swap = lax.ppermute(unit_there, "co", SWAP)
    gate_u8 = jnp.concatenate([unit_here[:n_yl], unit_swap[:n_yl]], axis=0)
    up_u8 = jnp.concatenate([unit_here[n_yl:], unit_swap[n_yl:]], axis=0)

    def last_rows(value):
        return value.reshape(n_yl, rows, width)[:, rows - 1]

    last_tok = jnp.concatenate([last_rows(tok_half), last_rows(tok_sib)], axis=0).astype(f32)
    last_tok = (last_tok * coefs[:, None]).astype(bf16)
    head_term8 = (coefs[:, None] * head_vec.astype(f32)).astype(bf16)

    def weight_grad(full, own_right, sib_right, last_left, last_right):
        here, there = core_parts(full, 0)
        from_sib = lax.ppermute(there, "co", SWAP)
        total = lax.optimization_barrier(
            (dot(here, own_right, 1, 0) + dot(from_sib, sib_right, 1, 0)) * loss_scale
        )
        if last_left is None:
            ends = [v.reshape(units, n_yl, rows)[:, :, rows - 1] for v in (here, from_sib)]
            last_left = jnp.concatenate(ends, axis=1).T
        return total + dot(last_left, last_right, 0, 0) * loss_scale

    grad_gate = weight_grad(gate_g, tok_half, tok_sib, gate_u8, last_tok)
    grad_up = weight_grad(up_g, tok_half, tok_sib, up_u8, last_tok)
    grad_down = weight_grad(hid, low_half, low_sib, None, head_term8)
    return grad_tokens, grad_gate, grad_up, grad_down, rewards


def solution(mesh):
    fine = Mesh(mesh.devices.reshape(4, 2, 8, 2, 4), FINE)
    gx, gz = ("yl", "co"), GZ
    weight = P(("gy",) + gx, gz)
    act = P(gx, gz + ("gy",))
    return jax.shard_map(
        body,
        mesh=fine,
        in_specs=(act, weight, weight, weight, P(gz + ("gy",)), act, P()),
        out_specs=(act, weight, weight, weight, P()),
        check_vma=False,
    )
```

```python
import functools

import jax
import jax.numpy as jnp
from jax import lax
from jax.experimental import pallas as pl
from jax.experimental.pallas import tpu as pltpu
from jax.sharding import Mesh, PartitionSpec as P

SEQ_LEN = 128
reward_weight = 64.0
FINE = ("yl", "co", "gy", "yh", "xx")
PLANE = ("yl", "gy")
GZ = ("yh", "xx")
SWAP = [(0, 1), (1, 0)]
f32, bf16 = jnp.float32, jnp.bfloat16


def exchange(pieces, axes):
    return lax.all_to_all(pieces, axes, 0, 0)


def to_all(value, axes, count):
    return exchange(jnp.broadcast_to(value[None], (count,) + value.shape), axes)


def dot(left, right, left_dim, right_dim):
    return lax.dot_general(
        left, right, (((left_dim,), (right_dim,)), ((), ())), preferred_element_type=f32
    )


def token_products(tok_got, gate_w, up_w, parts, tok, ends):
    n_plane, rows, cols = tok_got.shape
    half, width = tok.shape
    n_gy, n_yl = width // cols, half // rows
    chip_units = parts.shape[0]
    for y in range(n_yl):
        for z in range(n_gy):
            tok[y * rows : (y + 1) * rows, z * cols : (z + 1) * cols] = tok_got[y * n_gy + z]
    last = [tok[(y + 1) * rows - 16 : (y + 1) * rows].astype(f32)[15:] for y in range(n_yl)]
    ends[...] = jnp.concatenate(last + [jnp.zeros((16 - n_yl, width), f32)], axis=0).astype(bf16)
    parts[:, :half] = dot(gate_w[:chip_units], tok[...], 1, 1).astype(bf16)
    parts[:, half:] = dot(up_w[:chip_units], tok[...], 1, 1).astype(bf16)


def cotangent_products(core, low_got, ends, ends_sib, gate_w, up_w, down_w, parts, low, head, wide):
    n_gy, _, cols = low_got.shape
    half, width = low.shape
    n_yl = half // SEQ_LEN
    chip_units = down_w.shape[0]
    for z in range(n_gy):
        at = slice(z * cols, (z + 1) * cols)
        low[:, at] = low_got[z, :half]
        head[:, at] = low_got[z, half:]
    here, there = (ref[...].astype(f32)[:n_yl] for ref in (ends, ends_sib))
    last = [jnp.where(core[0] == 0, here, there), jnp.where(core[0] == 0, there, here)]
    wide[:16] = head[...]
    wide[16:32] = jnp.concatenate(last + [jnp.zeros((16 - 2 * n_yl, width), f32)], axis=0).astype(bf16)
    wide[32:] = jnp.zeros((96, width), bf16)
    parts[:, :half] = dot(down_w[...], low[...], 1, 1).astype(bf16)
    v = dot(down_w[...], wide[...], 1, 1)
    gate = dot(gate_w[:chip_units], wide[...], 1, 1)
    up = pltpu.roll(dot(up_w[:chip_units], wide[...], 1, 1), 16, 1)
    high = v.astype(bf16).astype(f32)
    lane = lax.broadcasted_iota(jnp.int32, v.shape, 1)
    more = jnp.where(lane == 0, high, jnp.where(lane == 1, v - high, 0.0))
    more = jnp.where((lane >= 16) & (lane < 32), gate, jnp.where((lane >= 32) & (lane < 48), up, more))
    parts[:, half:] = more.astype(bf16)


def split_sums(in_two, place, got, keep, give, total):
    own = keep.shape[0]
    sums = got[0].astype(f32)
    for j in range(1, got.shape[0]):
        sums += got[j].astype(f32)
    total[...] = sums
    keep[...] = total[pl.ds(pl.multiple_of(place[0] * own, 8), own), :]
    away = total[pl.ds(pl.multiple_of((1 - place[0]) * own, 8), own), :]
    give[...] = away.astype(bf16)
    if in_two:
        ends = away[:, -128:]
        lost = pltpu.roll(ends - ends.astype(bf16).astype(f32), 1, 1)
        lane = lax.broadcasted_iota(jnp.int32, ends.shape, 1)
        give[:, -128:] = jnp.where(lane == 1, ends + lost, ends).astype(bf16)


def hidden_units(chip_units, place, keep, got, back_keep, back_got, tok_terms, mine):
    own, half = keep.shape[0], keep.shape[1] // 2
    n_seq = half // SEQ_LEN
    sums = keep[...] + got[...].astype(f32)
    back = back_keep[...] + back_got[...].astype(f32)
    gate_sum, up_sum, hidden_grad = sums[:, :half], sums[:, half:], back[:, :half]
    more = back[:, half:]
    head_down = more[:, 0:1] + more[:, 1:2]
    gate_sigmoid = jax.nn.sigmoid(gate_sum)
    silu_gate = gate_sum * gate_sigmoid
    hidden = (silu_gate * up_sum).astype(bf16).astype(f32)
    gate_slope = up_sum * gate_sigmoid * (1.0 + gate_sum * (1.0 - gate_sigmoid))

    row = lax.broadcasted_iota(jnp.int32, (8, half), 0)
    lane = lax.broadcasted_iota(jnp.int32, (8, half), 1)
    blank = jnp.zeros((128 - own, half), f32)

    def picked(value, first):
        pick = (lane == (row - first) * SEQ_LEN + SEQ_LEN - 1) & (row >= first) & (row < first + n_seq)
        value = jnp.concatenate([value * head_down, blank], axis=0).astype(bf16)
        return dot(jnp.where(pick, 1.0, 0.0).astype(bf16), value, 1, 1)

    unit = picked(gate_slope, 0) + picked(silu_gate, n_seq)
    unit = jnp.concatenate([unit, jnp.zeros((8, half - 128), f32)], axis=1)
    unit = pltpu.roll(unit, place[0], 1)

    last_hidden = (more * jax.nn.sigmoid(more) * pltpu.roll(more, 128 - 16, 1)).astype(bf16).astype(f32)
    terms = jnp.sum(last_hidden * head_down, axis=0, keepdims=True) + tok_terms[...]
    for s in range(2 * n_seq):
        rest = jnp.sum(jnp.where(lane[:1, :128] == 16 + s, terms, 0.0), axis=1, keepdims=True)
        for i in range(3):
            piece = rest.astype(bf16).astype(f32)
            unit += jnp.where((row == 0) & (lane == chip_units + 2 * i * n_seq + s), piece, 0.0)
            rest = rest - piece
    rows = jnp.concatenate([hidden_grad * gate_slope, hidden_grad * silu_gate, hidden, unit], axis=0)
    mine[...] = rows.astype(bf16)


def token_gradients(everyone, gate_w, up_w, sent, full):
    width = gate_w.shape[1]
    n_gz, n_rows, half = everyone.shape
    own = (n_rows - 8) // 3
    n_plane, piece_rows, cols = sent.shape
    n_gy, rows = width // cols, piece_rows - 16
    unit = jnp.zeros((8, half), f32)
    for j in range(n_gz):
        block = everyone[j].astype(f32)
        for i in range(2):
            full[i, j * own : (j + 1) * own] = block[i * own : (i + 1) * own]
        unit += block[3 * own :]
    terms = unit + pltpu.roll(unit, half - 8, 1) + pltpu.roll(unit, half - 16, 1)
    terms = pltpu.roll(terms, half - n_gz * own, 1)[:, :cols]
    lane = lax.broadcasted_iota(jnp.int32, terms.shape, 1)
    high = terms.astype(bf16).astype(f32)
    middle = (terms - high).astype(bf16).astype(f32)
    terms = jnp.where(
        lane < 8,
        high,
        jnp.where(lane < 16, pltpu.roll(middle, 8, 1), pltpu.roll(terms - high - middle, 16, 1)),
    )
    terms = jnp.where(lane < 24, terms, 0.0)[:1]
    for i in range(2):
        full[i, n_gz * own :] = jnp.zeros((full.shape[1] - n_gz * own, half), f32)
    unit = unit.astype(bf16)
    gate_t, up_t = (full[i].T.astype(bf16) for i in range(2))
    step = 2 * cols
    for c in range(0, width, step):
        part = dot(gate_t, gate_w[:, c : c + step], 1, 0) + dot(up_t, up_w[:, c : c + step], 1, 0)
        units_here = (
            dot(unit, gate_w[:, c : c + step], 1, 0)[:4] + dot(unit, up_w[:, c : c + step], 1, 0)[4:]
        )
        for z in range(c // cols, (c + step) // cols):
            at = slice(z * cols - c, (z + 1) * cols - c)
            for y in range(n_plane // n_gy):
                piece = y * n_gy + z
                sent[piece, :rows] = part[y * rows : (y + 1) * rows, at].astype(bf16)
                row = lax.broadcasted_iota(jnp.int32, (16, cols), 0)
                extra = jnp.where(row == 0, units_here[y : y + 1, at], jnp.where(row == 1, terms, 0.0))
                sent[piece, rows:] = extra.astype(bf16)


def body(tokens, gate_weight, up_weight, down_weight, reward_head, lm_grad, pair_index):
    n_yl, n_gy = lax.axis_size("yl"), lax.axis_size("gy")
    n_plane, n_gz = n_yl * n_gy, lax.axis_size(GZ)
    rows, cols = tokens.shape
    units, width = gate_weight.shape
    my_seq = lax.axis_index(("yl", "co"))
    core = lax.axis_index("co")

    def core_order(here, there):
        return [jnp.where(core == 0, here, there), jnp.where(core == 0, there, here)]

    def chip_block(weight, padding):
        parts = core_order(weight, lax.ppermute(weight, "co", SWAP))
        return jnp.concatenate(parts + [jnp.zeros((padding, width), bf16)], axis=0)

    padding = -2 * units % 128
    gate_w, up_w = chip_block(gate_weight, padding), chip_block(up_weight, padding)
    down_w = chip_block(down_weight, 0)

    half = n_yl * rows
    low_got = to_all(lm_grad.astype(bf16), "yl", n_yl).reshape(half, cols)
    low_got, tok_block = lax.optimization_barrier((low_got, tokens))
    head_rows = jnp.broadcast_to(reward_head[None, :], (16, cols))
    low_got = lax.all_gather(jnp.concatenate([low_got, head_rows], axis=0), "gy")
    tok_got = to_all(tok_block, PLANE, n_plane)

    own_term = jnp.sum(tokens[rows - 1].astype(f32) * reward_head.astype(f32))
    sib_term = lax.ppermute(own_term[None], "co", SWAP)[0]
    spot = jnp.arange(128)[None, :] - 16 - lax.axis_index("yl")
    first_term, second_term = core_order(own_term, sib_term)
    tok_terms = jnp.where(spot == 0, first_term, jnp.where(spot == n_yl, second_term, 0.0))
    gate_w, up_w, down_w, tok_terms = lax.optimization_barrier((gate_w, up_w, down_w, tok_terms))

    own = 2 * units // n_gz
    whole, scalar = pl.BlockSpec(memory_space=pltpu.VMEM), pl.BlockSpec(memory_space=pltpu.SMEM)
    grant = pltpu.CompilerParams(vmem_limit_bytes=16 * 2**20)
    parts, tok_half, ends = pl.pallas_call(
        token_products,
        out_shape=(
            jax.ShapeDtypeStruct((2 * units, 2 * half), bf16),
            jax.ShapeDtypeStruct((half, width), bf16),
            jax.ShapeDtypeStruct((16, width), bf16),
        ),
        in_specs=[whole] * 3,
        out_specs=(whole,) * 3,
        compiler_params=grant,
        cost_estimate=pl.CostEstimate(
            flops=8 * units * width * half, bytes_accessed=8 * 2**20, transcendentals=0
        ),
        name="token_products",
    )(tok_got, gate_w, up_w)
    ends_sib = lax.ppermute(ends, "co", SWAP)

    n_xx = lax.axis_size("xx")
    first = exchange(parts.reshape(n_xx, 2 * own, 2 * half), "xx")
    y_half = lax.axis_index("yh").astype(jnp.int32)[None]

    def halves(got, in_two):
        lanes = got.shape[2]
        keep, give = pl.pallas_call(
            functools.partial(split_sums, in_two),
            out_shape=(jax.ShapeDtypeStruct((own, lanes), f32), jax.ShapeDtypeStruct((own, lanes), bf16)),
            in_specs=[scalar, whole],
            out_specs=(whole,) * 2,
            scratch_shapes=[pltpu.VMEM((2 * own, lanes), f32)],
            compiler_params=grant,
            cost_estimate=pl.CostEstimate(flops=8 * own * lanes, bytes_accessed=22 * own * lanes, transcendentals=0),
            name="split_sums",
        )(y_half, got)
        return keep, lax.ppermute(give, "yh", SWAP)

    back_parts, low_half, head_vec = pl.pallas_call(
        cotangent_products,
        out_shape=(
            jax.ShapeDtypeStruct((2 * units, half + 128), bf16),
            jax.ShapeDtypeStruct((half, width), bf16),
            jax.ShapeDtypeStruct((16, width), bf16),
        ),
        in_specs=[scalar] + [whole] * 6,
        out_specs=(whole,) * 3,
        scratch_shapes=[pltpu.VMEM((128, width), bf16)],
        compiler_params=grant,
        cost_estimate=pl.CostEstimate(
            flops=4 * units * width * (half + 384), bytes_accessed=5 * 2**20, transcendentals=0
        ),
        name="cotangent_products",
    )(core.astype(jnp.int32)[None], low_got, ends, ends_sib, gate_w, up_w, down_w)
    head_vec = head_vec[:1]
    first, back_parts = lax.optimization_barrier((first, back_parts))
    second = exchange(back_parts.reshape(n_xx, 2 * own, half + 128), "xx")
    sums, sums_got = halves(first, False)
    back, back_got = halves(second, True)

    place = (lax.axis_index(("xx", "yh")) * own).astype(jnp.int32)[None]
    mine = pl.pallas_call(
        functools.partial(hidden_units, 2 * units),
        out_shape=jax.ShapeDtypeStruct((3 * own + 8, half), bf16),
        in_specs=[scalar] + [whole] * 5,
        out_specs=whole,
        compiler_params=grant,
        cost_estimate=pl.CostEstimate(
            flops=40 * own * half, bytes_accessed=12 * own * half, transcendentals=own * half
        ),
        name="hidden_units",
    )(place, sums, sums_got, back, back_got, tok_terms)
    other = lax.ppermute(mine, "yh", SWAP)
    pair = jnp.stack([jnp.where(y_half == 0, mine, other), jnp.where(y_half == 0, other, mine)])
    everyone = to_all(pair, "xx", n_xx).reshape(n_gz, 3 * own + 8, half)
    sent = pl.pallas_call(
        token_gradients,
        out_shape=jax.ShapeDtypeStruct((n_plane, rows + 16, cols), bf16),
        in_specs=[whole] * 3,
        out_specs=whole,
        scratch_shapes=[pltpu.VMEM((2, 2 * units + padding, half), f32)],
        compiler_params=grant,
        cost_estimate=pl.CostEstimate(
            flops=8 * units * width * half, bytes_accessed=5 * 2**20, transcendentals=0
        ),
        name="token_gradients",
    )(everyone, gate_w, up_w)
    sent, everyone = lax.optimization_barrier((sent, everyone))
    gate_g, up_g, hid = (
        everyone[:, i * own : (i + 1) * own].reshape(2 * units, half) for i in range(3)
    )
    units_at = jnp.sum(everyone[:, 3 * own :, : 2 * units].astype(f32), axis=0).astype(bf16)
    token_sum = jnp.sum(exchange(sent, PLANE).astype(f32), axis=0)

    both = jnp.sum(token_sum[rows + 1, : 6 * n_yl].reshape(3, 2, n_yl), axis=0)
    sequence = jnp.arange(2 * n_yl, dtype=jnp.int32)
    rewards = both.T.reshape(2 * n_yl)
    chosen_hot = (pair_index[:, 0:1] == sequence[None, :]).astype(f32)
    rejected_hot = (pair_index[:, 1:2] == sequence[None, :]).astype(f32)
    margin = jnp.sum((chosen_hot - rejected_hot) * rewards[None, :], axis=1)
    pair_weight = jax.nn.sigmoid(-margin)
    scaled = reward_weight * jnp.sum((rejected_hot - chosen_hot) * pair_weight[:, None], axis=0)
    by_core = scaled.reshape(n_yl, 2)
    core_coefs = jnp.where(core == 0, by_core[:, 0], by_core[:, 1])
    sib_coefs = jnp.where(core == 0, by_core[:, 1], by_core[:, 0])
    coefs = jnp.concatenate([core_coefs, sib_coefs])
    my_coef = jnp.sum(jnp.where(sequence == my_seq, scaled, 0.0))

    row = jnp.arange(rows)[:, None]
    head_term = my_coef * (reward_head.astype(f32) + token_sum[rows])
    grad_tokens = lm_grad + token_sum[:rows] + jnp.where(row == rows - 1, head_term[None, :], 0.0)

    loss_scale = 1.0 / jnp.sqrt(f32(rows * 2 * n_yl))
    tok_sib = lax.ppermute(tok_half, "co", SWAP)
    low_sib = lax.ppermute(low_half, "co", SWAP)

    def core_parts(value, axis):
        return [
            lax.dynamic_slice_in_dim(value, which * units, units, axis) for which in (core, 1 - core)
        ]

    unit_here, unit_there = core_parts(units_at, 1)
    unit_swap = lax.ppermute(unit_there, "co", SWAP)
    gate_u8 = jnp.concatenate([unit_here[:n_yl], unit_swap[:n_yl]], axis=0)
    up_u8 = jnp.concatenate([unit_here[n_yl:], unit_swap[n_yl:]], axis=0)

    def last_rows(value):
        return value.reshape(n_yl, rows, width)[:, rows - 1]

    last_tok = jnp.concatenate([last_rows(tok_half), last_rows(tok_sib)], axis=0).astype(f32)
    last_tok = (last_tok * coefs[:, None]).astype(bf16)
    head_term8 = (coefs[:, None] * head_vec.astype(f32)).astype(bf16)

    def weight_grad(full, own_right, sib_right, last_left, last_right):
        here, there = core_parts(full, 0)
        from_sib = lax.ppermute(there, "co", SWAP)
        total = lax.optimization_barrier(
            (dot(here, own_right, 1, 0) + dot(from_sib, sib_right, 1, 0)) * loss_scale
        )
        if last_left is None:
            ends = [v.reshape(units, n_yl, rows)[:, :, rows - 1] for v in (here, from_sib)]
            last_left = jnp.concatenate(ends, axis=1).T
        return total + dot(last_left, last_right, 0, 0) * loss_scale

    grad_gate = weight_grad(gate_g, tok_half, tok_sib, gate_u8, last_tok)
    grad_up = weight_grad(up_g, tok_half, tok_sib, up_u8, last_tok)
    grad_down = weight_grad(hid, low_half, low_sib, None, head_term8)
    return grad_tokens, grad_gate, grad_up, grad_down, rewards


def solution(mesh):
    fine = Mesh(mesh.devices.reshape(4, 2, 8, 2, 4), FINE)
    gx, gz = ("yl", "co"), GZ
    weight = P(("gy",) + gx, gz)
    act = P(gx, gz + ("gy",))
    return jax.shard_map(
        body,
        mesh=fine,
        in_specs=(act, weight, weight, weight, P(gz + ("gy",)), act, P()),
        out_specs=(act, weight, weight, weight, P()),
        check_vma=False,
    )
```

```python
import functools

import jax
import jax.numpy as jnp
from jax import lax
from jax.experimental import pallas as pl
from jax.experimental.pallas import tpu as pltpu
from jax.sharding import Mesh, PartitionSpec as P

SEQ_LEN = 128
reward_weight = 64.0
FINE = ("yl", "co", "gy", "yh", "xx")
PLANE = ("yl", "gy")
GZ = ("yh", "xx")
SWAP = [(0, 1), (1, 0)]
f32, bf16 = jnp.float32, jnp.bfloat16


def exchange(pieces, axes):
    return lax.all_to_all(pieces, axes, 0, 0)


def to_all(value, axes, count):
    return exchange(jnp.broadcast_to(value[None], (count,) + value.shape), axes)


def dot(left, right, left_dim, right_dim):
    return lax.dot_general(
        left, right, (((left_dim,), (right_dim,)), ((), ())), preferred_element_type=f32
    )


def token_products(tok_got, gate_w, up_w, parts, tok, ends):
    n_plane, rows, cols = tok_got.shape
    half, width = tok.shape
    n_gy, n_yl = width // cols, half // rows
    chip_units = parts.shape[0]
    for y in range(n_yl):
        for z in range(n_gy):
            tok[y * rows : (y + 1) * rows, z * cols : (z + 1) * cols] = tok_got[y * n_gy + z]
    last = [tok[(y + 1) * rows - 16 : (y + 1) * rows].astype(f32)[15:] for y in range(n_yl)]
    ends[...] = jnp.concatenate(last + [jnp.zeros((16 - n_yl, width), f32)], axis=0).astype(bf16)
    parts[:, :half] = dot(gate_w[:chip_units], tok[...], 1, 1).astype(bf16)
    parts[:, half:] = dot(up_w[:chip_units], tok[...], 1, 1).astype(bf16)


def cotangent_products(core, low_got, ends, ends_sib, gate_w, up_w, down_w, parts, low, head, wide):
    n_gy, _, cols = low_got.shape
    half, width = low.shape
    n_yl = half // SEQ_LEN
    chip_units = down_w.shape[0]
    for z in range(n_gy):
        at = slice(z * cols, (z + 1) * cols)
        low[:, at] = low_got[z, :half]
        head[:, at] = low_got[z, half:]
    here, there = (ref[...].astype(f32)[:n_yl] for ref in (ends, ends_sib))
    last = [jnp.where(core[0] == 0, here, there), jnp.where(core[0] == 0, there, here)]
    wide[:16] = head[...]
    wide[16:32] = jnp.concatenate(last + [jnp.zeros((16 - 2 * n_yl, width), f32)], axis=0).astype(bf16)
    wide[32:] = jnp.zeros((96, width), bf16)
    parts[:, :half] = dot(down_w[...], low[...], 1, 1).astype(bf16)
    v = dot(down_w[...], wide[...], 1, 1)
    gate = dot(gate_w[:chip_units], wide[...], 1, 1)
    up = pltpu.roll(dot(up_w[:chip_units], wide[...], 1, 1), 16, 1)
    high = v.astype(bf16).astype(f32)
    lane = lax.broadcasted_iota(jnp.int32, v.shape, 1)
    more = jnp.where(lane == 0, high, jnp.where(lane == 1, v - high, 0.0))
    more = jnp.where((lane >= 16) & (lane < 32), gate, jnp.where((lane >= 32) & (lane < 48), up, more))
    parts[:, half:] = more.astype(bf16)


def split_sums(in_two, place, got, keep, give, total):
    own = keep.shape[0]
    sums = got[0].astype(f32)
    for j in range(1, got.shape[0]):
        sums += got[j].astype(f32)
    total[...] = sums
    keep[...] = total[pl.ds(pl.multiple_of(place[0] * own, 8), own), :]
    away = total[pl.ds(pl.multiple_of((1 - place[0]) * own, 8), own), :]
    give[...] = away.astype(bf16)
    if in_two:
        ends = away[:, -128:]
        lost = pltpu.roll(ends - ends.astype(bf16).astype(f32), 1, 1)
        lane = lax.broadcasted_iota(jnp.int32, ends.shape, 1)
        give[:, -128:] = jnp.where(lane == 1, ends + lost, ends).astype(bf16)


def hidden_units(chip_units, place, keep, got, back_keep, back_got, tok_terms, mine):
    own, half = keep.shape[0], keep.shape[1] // 2
    n_seq = half // SEQ_LEN
    sums = keep[...] + got[...].astype(f32)
    back = back_keep[...] + back_got[...].astype(f32)
    gate_sum, up_sum, hidden_grad = sums[:, :half], sums[:, half:], back[:, :half]
    more = back[:, half:]
    head_down = more[:, 0:1] + more[:, 1:2]
    gate_sigmoid = jax.nn.sigmoid(gate_sum)
    silu_gate = gate_sum * gate_sigmoid
    hidden = (silu_gate * up_sum).astype(bf16).astype(f32)
    gate_slope = up_sum * gate_sigmoid * (1.0 + gate_sum * (1.0 - gate_sigmoid))

    row = lax.broadcasted_iota(jnp.int32, (8, half), 0)
    lane = lax.broadcasted_iota(jnp.int32, (8, half), 1)
    blank = jnp.zeros((128 - own, half), f32)

    def picked(value, first):
        pick = (lane == (row - first) * SEQ_LEN + SEQ_LEN - 1) & (row >= first) & (row < first + n_seq)
        value = jnp.concatenate([value * head_down, blank], axis=0).astype(bf16)
        return dot(jnp.where(pick, 1.0, 0.0).astype(bf16), value, 1, 1)

    unit = picked(gate_slope, 0) + picked(silu_gate, n_seq)
    unit = jnp.concatenate([unit, jnp.zeros((8, half - 128), f32)], axis=1)
    unit = pltpu.roll(unit, place[0], 1)

    last_hidden = (more * jax.nn.sigmoid(more) * pltpu.roll(more, 128 - 16, 1)).astype(bf16).astype(f32)
    terms = jnp.sum(last_hidden * head_down, axis=0, keepdims=True) + tok_terms[...]
    for s in range(2 * n_seq):
        rest = jnp.sum(jnp.where(lane[:1, :128] == 16 + s, terms, 0.0), axis=1, keepdims=True)
        for i in range(3):
            piece = rest.astype(bf16).astype(f32)
            unit += jnp.where((row == 0) & (lane == chip_units + 2 * i * n_seq + s), piece, 0.0)
            rest = rest - piece
    rows = jnp.concatenate([hidden_grad * gate_slope, hidden_grad * silu_gate, hidden, unit], axis=0)
    mine[...] = rows.astype(bf16)


def token_gradients(everyone, gate_w, up_w, sent, full):
    width = gate_w.shape[1]
    n_gz, n_rows, half = everyone.shape
    own = (n_rows - 8) // 3
    n_plane, piece_rows, cols = sent.shape
    n_gy, rows = width // cols, piece_rows - 16
    unit = jnp.zeros((8, half), f32)
    for j in range(n_gz):
        block = everyone[j].astype(f32)
        for i in range(2):
            full[i, j * own : (j + 1) * own] = block[i * own : (i + 1) * own]
        unit += block[3 * own :]
    terms = unit + pltpu.roll(unit, half - 8, 1) + pltpu.roll(unit, half - 16, 1)
    terms = pltpu.roll(terms, half - n_gz * own, 1)[:, :cols]
    lane = lax.broadcasted_iota(jnp.int32, terms.shape, 1)
    high = terms.astype(bf16).astype(f32)
    middle = (terms - high).astype(bf16).astype(f32)
    terms = jnp.where(
        lane < 8,
        high,
        jnp.where(lane < 16, pltpu.roll(middle, 8, 1), pltpu.roll(terms - high - middle, 16, 1)),
    )
    terms = jnp.where(lane < 24, terms, 0.0)[:1]
    for i in range(2):
        full[i, n_gz * own :] = jnp.zeros((full.shape[1] - n_gz * own, half), f32)
    unit = unit.astype(bf16)
    gate_t, up_t = (full[i].T.astype(bf16) for i in range(2))
    step = 2 * cols
    for c in range(0, width, step):
        part = dot(gate_t, gate_w[:, c : c + step], 1, 0) + dot(up_t, up_w[:, c : c + step], 1, 0)
        units_here = (
            dot(unit, gate_w[:, c : c + step], 1, 0)[:4] + dot(unit, up_w[:, c : c + step], 1, 0)[4:]
        )
        for z in range(c // cols, (c + step) // cols):
            at = slice(z * cols - c, (z + 1) * cols - c)
            for y in range(n_plane // n_gy):
                piece = y * n_gy + z
                sent[piece, :rows] = part[y * rows : (y + 1) * rows, at].astype(bf16)
                row = lax.broadcasted_iota(jnp.int32, (16, cols), 0)
                extra = jnp.where(row == 0, units_here[y : y + 1, at], jnp.where(row == 1, terms, 0.0))
                sent[piece, rows:] = extra.astype(bf16)


def body(tokens, gate_weight, up_weight, down_weight, reward_head, lm_grad, pair_index):
    n_yl, n_gy = lax.axis_size("yl"), lax.axis_size("gy")
    n_plane, n_gz = n_yl * n_gy, lax.axis_size(GZ)
    rows, cols = tokens.shape
    units, width = gate_weight.shape
    my_seq = lax.axis_index(("yl", "co"))
    core = lax.axis_index("co")

    def core_order(here, there):
        return [jnp.where(core == 0, here, there), jnp.where(core == 0, there, here)]

    def chip_block(weight, padding):
        parts = core_order(weight, lax.ppermute(weight, "co", SWAP))
        return jnp.concatenate(parts + [jnp.zeros((padding, width), bf16)], axis=0)

    padding = -2 * units % 128
    gate_w, up_w = chip_block(gate_weight, padding), chip_block(up_weight, padding)
    down_w = chip_block(down_weight, 0)

    half = n_yl * rows
    low_got = to_all(lm_grad.astype(bf16), "yl", n_yl).reshape(half, cols)
    head_rows = jnp.broadcast_to(reward_head[None, :], (16, cols))
    low_got = jnp.concatenate([low_got, head_rows], axis=0)
    low_got, tok_block = lax.optimization_barrier((low_got, tokens))
    low_got = lax.all_gather(low_got, "gy")
    tok_got = to_all(tok_block, PLANE, n_plane)

    own_term = jnp.sum(tokens[rows - 1].astype(f32) * reward_head.astype(f32))
    sib_term = lax.ppermute(own_term[None], "co", SWAP)[0]
    spot = jnp.arange(128)[None, :] - 16 - lax.axis_index("yl")
    first_term, second_term = core_order(own_term, sib_term)
    tok_terms = jnp.where(spot == 0, first_term, jnp.where(spot == n_yl, second_term, 0.0))
    gate_w, up_w, down_w, tok_terms = lax.optimization_barrier((gate_w, up_w, down_w, tok_terms))

    own = 2 * units // n_gz
    whole, scalar = pl.BlockSpec(memory_space=pltpu.VMEM), pl.BlockSpec(memory_space=pltpu.SMEM)
    grant = pltpu.CompilerParams(vmem_limit_bytes=16 * 2**20)
    parts, tok_half, ends = pl.pallas_call(
        token_products,
        out_shape=(
            jax.ShapeDtypeStruct((2 * units, 2 * half), bf16),
            jax.ShapeDtypeStruct((half, width), bf16),
            jax.ShapeDtypeStruct((16, width), bf16),
        ),
        in_specs=[whole] * 3,
        out_specs=(whole,) * 3,
        compiler_params=grant,
        cost_estimate=pl.CostEstimate(
            flops=8 * units * width * half, bytes_accessed=8 * 2**20, transcendentals=0
        ),
        name="token_products",
    )(tok_got, gate_w, up_w)
    ends_sib = lax.ppermute(ends, "co", SWAP)

    n_xx = lax.axis_size("xx")
    first = exchange(parts.reshape(n_xx, 2 * own, 2 * half), "xx")
    y_half = lax.axis_index("yh").astype(jnp.int32)[None]

    def halves(got, in_two):
        lanes = got.shape[2]
        keep, give = pl.pallas_call(
            functools.partial(split_sums, in_two),
            out_shape=(jax.ShapeDtypeStruct((own, lanes), f32), jax.ShapeDtypeStruct((own, lanes), bf16)),
            in_specs=[scalar, whole],
            out_specs=(whole,) * 2,
            scratch_shapes=[pltpu.VMEM((2 * own, lanes), f32)],
            compiler_params=grant,
            cost_estimate=pl.CostEstimate(flops=8 * own * lanes, bytes_accessed=22 * own * lanes, transcendentals=0),
            name="split_sums",
        )(y_half, got)
        return keep, lax.ppermute(give, "yh", SWAP)

    back_parts, low_half, head_vec = pl.pallas_call(
        cotangent_products,
        out_shape=(
            jax.ShapeDtypeStruct((2 * units, half + 128), bf16),
            jax.ShapeDtypeStruct((half, width), bf16),
            jax.ShapeDtypeStruct((16, width), bf16),
        ),
        in_specs=[scalar] + [whole] * 6,
        out_specs=(whole,) * 3,
        scratch_shapes=[pltpu.VMEM((128, width), bf16)],
        compiler_params=grant,
        cost_estimate=pl.CostEstimate(
            flops=4 * units * width * (half + 384), bytes_accessed=5 * 2**20, transcendentals=0
        ),
        name="cotangent_products",
    )(core.astype(jnp.int32)[None], low_got, ends, ends_sib, gate_w, up_w, down_w)
    head_vec = head_vec[:1]
    first, back_parts = lax.optimization_barrier((first, back_parts))
    second = exchange(back_parts.reshape(n_xx, 2 * own, half + 128), "xx")
    sums, sums_got = halves(first, False)
    back, back_got = halves(second, True)

    place = (lax.axis_index(("xx", "yh")) * own).astype(jnp.int32)[None]
    mine = pl.pallas_call(
        functools.partial(hidden_units, 2 * units),
        out_shape=jax.ShapeDtypeStruct((3 * own + 8, half), bf16),
        in_specs=[scalar] + [whole] * 5,
        out_specs=whole,
        compiler_params=grant,
        cost_estimate=pl.CostEstimate(
            flops=40 * own * half, bytes_accessed=12 * own * half, transcendentals=own * half
        ),
        name="hidden_units",
    )(place, sums, sums_got, back, back_got, tok_terms)
    other = lax.ppermute(mine, "yh", SWAP)
    pair = jnp.stack([jnp.where(y_half == 0, mine, other), jnp.where(y_half == 0, other, mine)])
    everyone = to_all(pair, "xx", n_xx).reshape(n_gz, 3 * own + 8, half)
    sent = pl.pallas_call(
        token_gradients,
        out_shape=jax.ShapeDtypeStruct((n_plane, rows + 16, cols), bf16),
        in_specs=[whole] * 3,
        out_specs=whole,
        scratch_shapes=[pltpu.VMEM((2, 2 * units + padding, half), f32)],
        compiler_params=grant,
        cost_estimate=pl.CostEstimate(
            flops=8 * units * width * half, bytes_accessed=5 * 2**20, transcendentals=0
        ),
        name="token_gradients",
    )(everyone, gate_w, up_w)
    sent, everyone = lax.optimization_barrier((sent, everyone))
    gate_g, up_g, hid = (
        everyone[:, i * own : (i + 1) * own].reshape(2 * units, half) for i in range(3)
    )
    units_at = jnp.sum(everyone[:, 3 * own :, : 2 * units].astype(f32), axis=0).astype(bf16)
    token_sum = jnp.sum(exchange(sent, PLANE).astype(f32), axis=0)

    both = jnp.sum(token_sum[rows + 1, : 6 * n_yl].reshape(3, 2, n_yl), axis=0)
    sequence = jnp.arange(2 * n_yl, dtype=jnp.int32)
    rewards = both.T.reshape(2 * n_yl)
    chosen_hot = (pair_index[:, 0:1] == sequence[None, :]).astype(f32)
    rejected_hot = (pair_index[:, 1:2] == sequence[None, :]).astype(f32)
    margin = jnp.sum((chosen_hot - rejected_hot) * rewards[None, :], axis=1)
    pair_weight = jax.nn.sigmoid(-margin)
    scaled = reward_weight * jnp.sum((rejected_hot - chosen_hot) * pair_weight[:, None], axis=0)
    by_core = scaled.reshape(n_yl, 2)
    core_coefs = jnp.where(core == 0, by_core[:, 0], by_core[:, 1])
    sib_coefs = jnp.where(core == 0, by_core[:, 1], by_core[:, 0])
    coefs = jnp.concatenate([core_coefs, sib_coefs])
    my_coef = jnp.sum(jnp.where(sequence == my_seq, scaled, 0.0))

    row = jnp.arange(rows)[:, None]
    head_term = my_coef * (reward_head.astype(f32) + token_sum[rows])
    grad_tokens = lm_grad + token_sum[:rows] + jnp.where(row == rows - 1, head_term[None, :], 0.0)

    loss_scale = 1.0 / jnp.sqrt(f32(rows * 2 * n_yl))
    tok_sib = lax.ppermute(tok_half, "co", SWAP)
    low_sib = lax.ppermute(low_half, "co", SWAP)

    def core_parts(value, axis):
        return [
            lax.dynamic_slice_in_dim(value, which * units, units, axis) for which in (core, 1 - core)
        ]

    unit_here, unit_there = core_parts(units_at, 1)
    unit_swap = lax.ppermute(unit_there, "co", SWAP)
    gate_u8 = jnp.concatenate([unit_here[:n_yl], unit_swap[:n_yl]], axis=0)
    up_u8 = jnp.concatenate([unit_here[n_yl:], unit_swap[n_yl:]], axis=0)

    last_tok = jnp.concatenate([ends[:n_yl], ends_sib[:n_yl]], axis=0).astype(f32)
    is_last = jnp.arange(half)[:, None] == jnp.arange(n_yl)[None, :] * rows + rows - 1
    last_tok = (last_tok * coefs[:, None]).astype(bf16)
    head_term8 = (coefs[:, None] * head_vec.astype(f32)).astype(bf16)

    def weight_grad(full, own_right, sib_right, last_left, last_right):
        here, there = core_parts(full, 0)
        from_sib = lax.ppermute(there, "co", SWAP)
        total = lax.optimization_barrier(
            (dot(here, own_right, 1, 0) + dot(from_sib, sib_right, 1, 0)) * loss_scale
        )
        if last_left is None:
            picked = [dot(is_last.astype(bf16), v, 0, 1) for v in (here, from_sib)]
            last_left = jnp.concatenate(picked, axis=0).astype(bf16)
        return total + dot(last_left, last_right, 0, 0) * loss_scale

    grad_gate = weight_grad(gate_g, tok_half, tok_sib, gate_u8, last_tok)
    grad_up = weight_grad(up_g, tok_half, tok_sib, up_u8, last_tok)
    grad_down = weight_grad(hid, low_half, low_sib, None, head_term8)
    return grad_tokens, grad_gate, grad_up, grad_down, rewards


def solution(mesh):
    fine = Mesh(mesh.devices.reshape(4, 2, 8, 2, 4), FINE)
    gx, gz = ("yl", "co"), GZ
    weight = P(("gy",) + gx, gz)
    act = P(gx, gz + ("gy",))
    return jax.shard_map(
        body,
        mesh=fine,
        in_specs=(act, weight, weight, weight, P(gz + ("gy",)), act, P()),
        out_specs=(act, weight, weight, weight, P()),
        check_vma=False,
    )
```

```python
import functools

import jax
import jax.numpy as jnp
from jax import lax
from jax.experimental import pallas as pl
from jax.experimental.pallas import tpu as pltpu
from jax.sharding import Mesh, PartitionSpec as P

SEQ_LEN = 128
reward_weight = 64.0
FINE = ("yl", "co", "gy", "yh", "xx")
PLANE = ("yl", "gy")
GZ = ("yh", "xx")
SWAP = [(0, 1), (1, 0)]
f32, bf16 = jnp.float32, jnp.bfloat16


def exchange(pieces, axes):
    return lax.all_to_all(pieces, axes, 0, 0)


def to_all(value, axes, count):
    return exchange(jnp.broadcast_to(value[None], (count,) + value.shape), axes)


def dot(left, right, left_dim, right_dim):
    return lax.dot_general(
        left, right, (((left_dim,), (right_dim,)), ((), ())), preferred_element_type=f32
    )


def token_products(tok_got, gate_w, up_w, parts, tok, ends):
    n_plane, rows, cols = tok_got.shape
    half, width = tok.shape
    n_gy, n_yl = width // cols, half // rows
    chip_units = parts.shape[0]
    for y in range(n_yl):
        for z in range(n_gy):
            tok[y * rows : (y + 1) * rows, z * cols : (z + 1) * cols] = tok_got[y * n_gy + z]
    last = [tok[(y + 1) * rows - 16 : (y + 1) * rows].astype(f32)[15:] for y in range(n_yl)]
    ends[...] = jnp.concatenate(last + [jnp.zeros((16 - n_yl, width), f32)], axis=0).astype(bf16)
    parts[:, :half] = dot(gate_w[:chip_units], tok[...], 1, 1).astype(bf16)
    parts[:, half:] = dot(up_w[:chip_units], tok[...], 1, 1).astype(bf16)


def cotangent_products(core, low_got, ends, ends_sib, gate_w, up_w, down_w, parts, low, head, wide):
    n_gy, _, cols = low_got.shape
    half, width = low.shape
    n_yl = half // SEQ_LEN
    chip_units = down_w.shape[0]
    for z in range(n_gy):
        at = slice(z * cols, (z + 1) * cols)
        low[:, at] = low_got[z, :half]
        head[:, at] = low_got[z, half:]
    here, there = (ref[...].astype(f32)[:n_yl] for ref in (ends, ends_sib))
    last = [jnp.where(core[0] == 0, here, there), jnp.where(core[0] == 0, there, here)]
    wide[:16] = head[...]
    wide[16:32] = jnp.concatenate(last + [jnp.zeros((16 - 2 * n_yl, width), f32)], axis=0).astype(bf16)
    wide[32:] = jnp.zeros((96, width), bf16)
    parts[:, :half] = dot(down_w[...], low[...], 1, 1).astype(bf16)
    v = dot(down_w[...], wide[...], 1, 1)
    gate = dot(gate_w[:chip_units], wide[...], 1, 1)
    up = pltpu.roll(dot(up_w[:chip_units], wide[...], 1, 1), 16, 1)
    high = v.astype(bf16).astype(f32)
    lane = lax.broadcasted_iota(jnp.int32, v.shape, 1)
    more = jnp.where(lane == 0, high, jnp.where(lane == 1, v - high, 0.0))
    more = jnp.where((lane >= 16) & (lane < 32), gate, jnp.where((lane >= 32) & (lane < 48), up, more))
    parts[:, half:] = more.astype(bf16)


def split_sums(in_two, place, got, keep, give, total):
    own = keep.shape[0]
    sums = got[0].astype(f32)
    for j in range(1, got.shape[0]):
        sums += got[j].astype(f32)
    total[...] = sums
    keep[...] = total[pl.ds(pl.multiple_of(place[0] * own, 8), own), :]
    away = total[pl.ds(pl.multiple_of((1 - place[0]) * own, 8), own), :]
    give[...] = away.astype(bf16)
    if in_two:
        ends = away[:, -128:]
        lost = pltpu.roll(ends - ends.astype(bf16).astype(f32), 1, 1)
        lane = lax.broadcasted_iota(jnp.int32, ends.shape, 1)
        give[:, -128:] = jnp.where(lane == 1, ends + lost, ends).astype(bf16)


def hidden_units(chip_units, place, keep, got, back_keep, back_got, tok_terms, mine):
    own, half = keep.shape[0], keep.shape[1] // 2
    n_seq = half // SEQ_LEN
    sums = keep[...] + got[...].astype(f32)
    back = back_keep[...] + back_got[...].astype(f32)
    gate_sum, up_sum, hidden_grad = sums[:, :half], sums[:, half:], back[:, :half]
    more = back[:, half:]
    head_down = more[:, 0:1] + more[:, 1:2]
    gate_sigmoid = jax.nn.sigmoid(gate_sum)
    silu_gate = gate_sum * gate_sigmoid
    hidden = (silu_gate * up_sum).astype(bf16).astype(f32)
    gate_slope = up_sum * gate_sigmoid * (1.0 + gate_sum * (1.0 - gate_sigmoid))

    row = lax.broadcasted_iota(jnp.int32, (8, half), 0)
    lane = lax.broadcasted_iota(jnp.int32, (8, half), 1)
    blank = jnp.zeros((128 - own, half), f32)

    def picked(value, first):
        pick = (lane == (row - first) * SEQ_LEN + SEQ_LEN - 1) & (row >= first) & (row < first + n_seq)
        value = jnp.concatenate([value * head_down, blank], axis=0).astype(bf16)
        return dot(jnp.where(pick, 1.0, 0.0).astype(bf16), value, 1, 1)

    unit = picked(gate_slope, 0) + picked(silu_gate, n_seq)
    unit = jnp.concatenate([unit, jnp.zeros((8, half - 128), f32)], axis=1)
    unit = pltpu.roll(unit, place[0], 1)

    last_hidden = (more * jax.nn.sigmoid(more) * pltpu.roll(more, 128 - 16, 1)).astype(bf16).astype(f32)
    terms = jnp.sum(last_hidden * head_down, axis=0, keepdims=True) + tok_terms[...]
    for s in range(2 * n_seq):
        rest = jnp.sum(jnp.where(lane[:1, :128] == 16 + s, terms, 0.0), axis=1, keepdims=True)
        for i in range(3):
            piece = rest.astype(bf16).astype(f32)
            unit += jnp.where((row == 0) & (lane == chip_units + 2 * i * n_seq + s), piece, 0.0)
            rest = rest - piece
    rows = jnp.concatenate([hidden_grad * gate_slope, hidden_grad * silu_gate, hidden, unit], axis=0)
    mine[...] = rows.astype(bf16)


def token_gradients(everyone, gate_w, up_w, sent, full):
    width = gate_w.shape[1]
    n_gz, n_rows, half = everyone.shape
    own = (n_rows - 8) // 3
    n_plane, piece_rows, cols = sent.shape
    n_gy, rows = width // cols, piece_rows - 16
    unit = jnp.zeros((8, half), f32)
    for j in range(n_gz):
        block = everyone[j].astype(f32)
        for i in range(2):
            full[i, j * own : (j + 1) * own] = block[i * own : (i + 1) * own]
        unit += block[3 * own :]
    terms = unit + pltpu.roll(unit, half - 8, 1) + pltpu.roll(unit, half - 16, 1)
    terms = pltpu.roll(terms, half - n_gz * own, 1)[:, :cols]
    lane = lax.broadcasted_iota(jnp.int32, terms.shape, 1)
    high = terms.astype(bf16).astype(f32)
    middle = (terms - high).astype(bf16).astype(f32)
    terms = jnp.where(
        lane < 8,
        high,
        jnp.where(lane < 16, pltpu.roll(middle, 8, 1), pltpu.roll(terms - high - middle, 16, 1)),
    )
    terms = jnp.where(lane < 24, terms, 0.0)[:1]
    for i in range(2):
        full[i, n_gz * own :] = jnp.zeros((full.shape[1] - n_gz * own, half), f32)
    unit = unit.astype(bf16)
    gate_t, up_t = (full[i].T.astype(bf16) for i in range(2))
    step = 2 * cols
    for c in range(0, width, step):
        part = dot(gate_t, gate_w[:, c : c + step], 1, 0) + dot(up_t, up_w[:, c : c + step], 1, 0)
        units_here = (
            dot(unit, gate_w[:, c : c + step], 1, 0)[:4] + dot(unit, up_w[:, c : c + step], 1, 0)[4:]
        )
        for z in range(c // cols, (c + step) // cols):
            at = slice(z * cols - c, (z + 1) * cols - c)
            for y in range(n_plane // n_gy):
                piece = y * n_gy + z
                sent[piece, :rows] = part[y * rows : (y + 1) * rows, at].astype(bf16)
                row = lax.broadcasted_iota(jnp.int32, (16, cols), 0)
                extra = jnp.where(row == 0, units_here[y : y + 1, at], jnp.where(row == 1, terms, 0.0))
                sent[piece, rows:] = extra.astype(bf16)


def body(tokens, gate_weight, up_weight, down_weight, reward_head, lm_grad, pair_index):
    n_yl, n_gy = lax.axis_size("yl"), lax.axis_size("gy")
    n_plane, n_gz = n_yl * n_gy, lax.axis_size(GZ)
    rows, cols = tokens.shape
    units, width = gate_weight.shape
    my_seq = lax.axis_index(("yl", "co"))
    core = lax.axis_index("co")

    def core_order(here, there):
        return [jnp.where(core == 0, here, there), jnp.where(core == 0, there, here)]

    def chip_block(weight, padding):
        parts = core_order(weight, lax.ppermute(weight, "co", SWAP))
        return jnp.concatenate(parts + [jnp.zeros((padding, width), bf16)], axis=0)

    padding = -2 * units % 128
    gate_w, up_w = chip_block(gate_weight, padding), chip_block(up_weight, padding)
    down_w = chip_block(down_weight, 0)

    half = n_yl * rows
    low_got = to_all(lm_grad.astype(bf16), "yl", n_yl).reshape(half, cols)
    head_rows = jnp.broadcast_to(reward_head[None, :], (16, cols))
    low_got = jnp.concatenate([low_got, head_rows], axis=0)
    low_got, tok_block = lax.optimization_barrier((low_got, tokens))
    low_got = lax.all_gather(low_got, "gy")
    tok_got = to_all(tok_block, PLANE, n_plane)

    gate_w, up_w, down_w = lax.optimization_barrier((gate_w, up_w, down_w))

    own = 2 * units // n_gz
    whole, scalar = pl.BlockSpec(memory_space=pltpu.VMEM), pl.BlockSpec(memory_space=pltpu.SMEM)
    grant = pltpu.CompilerParams(vmem_limit_bytes=16 * 2**20)
    parts, tok_half, ends = pl.pallas_call(
        token_products,
        out_shape=(
            jax.ShapeDtypeStruct((2 * units, 2 * half), bf16),
            jax.ShapeDtypeStruct((half, width), bf16),
            jax.ShapeDtypeStruct((16, width), bf16),
        ),
        in_specs=[whole] * 3,
        out_specs=(whole,) * 3,
        compiler_params=grant,
        cost_estimate=pl.CostEstimate(
            flops=8 * units * width * half, bytes_accessed=8 * 2**20, transcendentals=0
        ),
        name="token_products",
    )(tok_got, gate_w, up_w)
    ends_sib = lax.ppermute(ends, "co", SWAP)

    n_xx = lax.axis_size("xx")
    first = exchange(parts.reshape(n_xx, 2 * own, 2 * half), "xx")
    y_half = lax.axis_index("yh").astype(jnp.int32)[None]

    def halves(got, in_two):
        lanes = got.shape[2]
        keep, give = pl.pallas_call(
            functools.partial(split_sums, in_two),
            out_shape=(jax.ShapeDtypeStruct((own, lanes), f32), jax.ShapeDtypeStruct((own, lanes), bf16)),
            in_specs=[scalar, whole],
            out_specs=(whole,) * 2,
            scratch_shapes=[pltpu.VMEM((2 * own, lanes), f32)],
            compiler_params=grant,
            cost_estimate=pl.CostEstimate(flops=8 * own * lanes, bytes_accessed=22 * own * lanes, transcendentals=0),
            name="split_sums",
        )(y_half, got)
        return keep, lax.ppermute(give, "yh", SWAP)

    back_parts, low_half, head_vec = pl.pallas_call(
        cotangent_products,
        out_shape=(
            jax.ShapeDtypeStruct((2 * units, half + 128), bf16),
            jax.ShapeDtypeStruct((half, width), bf16),
            jax.ShapeDtypeStruct((16, width), bf16),
        ),
        in_specs=[scalar] + [whole] * 6,
        out_specs=(whole,) * 3,
        scratch_shapes=[pltpu.VMEM((128, width), bf16)],
        compiler_params=grant,
        cost_estimate=pl.CostEstimate(
            flops=4 * units * width * (half + 384), bytes_accessed=5 * 2**20, transcendentals=0
        ),
        name="cotangent_products",
    )(core.astype(jnp.int32)[None], low_got, ends, ends_sib, gate_w, up_w, down_w)
    head_vec = head_vec[:1]
    first, back_parts = lax.optimization_barrier((first, back_parts))
    second = exchange(back_parts.reshape(n_xx, 2 * own, half + 128), "xx")
    sums, sums_got = halves(first, False)
    back, back_got = halves(second, True)

    last_rows = jnp.concatenate(core_order(ends[:n_yl], ends_sib[:n_yl]), axis=0).astype(f32)
    counted = (lax.axis_index("yl") == 0) & (lax.axis_index("gy") == 0)
    tok_terms = jnp.where(counted, jnp.sum(last_rows * head_vec.astype(f32), axis=1), 0.0)
    tok_terms = jnp.pad(tok_terms[None, :], ((0, 0), (16, 112 - 2 * n_yl)))
    place = (lax.axis_index(("xx", "yh")) * own).astype(jnp.int32)[None]
    mine = pl.pallas_call(
        functools.partial(hidden_units, 2 * units),
        out_shape=jax.ShapeDtypeStruct((3 * own + 8, half), bf16),
        in_specs=[scalar] + [whole] * 5,
        out_specs=whole,
        compiler_params=grant,
        cost_estimate=pl.CostEstimate(
            flops=40 * own * half, bytes_accessed=12 * own * half, transcendentals=own * half
        ),
        name="hidden_units",
    )(place, sums, sums_got, back, back_got, tok_terms)
    other = lax.ppermute(mine, "yh", SWAP)
    pair = jnp.stack([jnp.where(y_half == 0, mine, other), jnp.where(y_half == 0, other, mine)])
    everyone = to_all(pair, "xx", n_xx).reshape(n_gz, 3 * own + 8, half)
    sent = pl.pallas_call(
        token_gradients,
        out_shape=jax.ShapeDtypeStruct((n_plane, rows + 16, cols), bf16),
        in_specs=[whole] * 3,
        out_specs=whole,
        scratch_shapes=[pltpu.VMEM((2, 2 * units + padding, half), f32)],
        compiler_params=grant,
        cost_estimate=pl.CostEstimate(
            flops=8 * units * width * half, bytes_accessed=5 * 2**20, transcendentals=0
        ),
        name="token_gradients",
    )(everyone, gate_w, up_w)
    sent, everyone = lax.optimization_barrier((sent, everyone))
    gate_g, up_g, hid = (
        everyone[:, i * own : (i + 1) * own].reshape(2 * units, half) for i in range(3)
    )
    units_at = jnp.sum(everyone[:, 3 * own :, : 2 * units].astype(f32), axis=0).astype(bf16)
    token_sum = jnp.sum(exchange(sent, PLANE).astype(f32), axis=0)

    both = jnp.sum(token_sum[rows + 1, : 6 * n_yl].reshape(3, 2, n_yl), axis=0)
    sequence = jnp.arange(2 * n_yl, dtype=jnp.int32)
    rewards = both.T.reshape(2 * n_yl)
    chosen_hot = (pair_index[:, 0:1] == sequence[None, :]).astype(f32)
    rejected_hot = (pair_index[:, 1:2] == sequence[None, :]).astype(f32)
    margin = jnp.sum((chosen_hot - rejected_hot) * rewards[None, :], axis=1)
    pair_weight = jax.nn.sigmoid(-margin)
    scaled = reward_weight * jnp.sum((rejected_hot - chosen_hot) * pair_weight[:, None], axis=0)
    by_core = scaled.reshape(n_yl, 2)
    core_coefs = jnp.where(core == 0, by_core[:, 0], by_core[:, 1])
    sib_coefs = jnp.where(core == 0, by_core[:, 1], by_core[:, 0])
    coefs = jnp.concatenate([core_coefs, sib_coefs])
    my_coef = jnp.sum(jnp.where(sequence == my_seq, scaled, 0.0))

    row = jnp.arange(rows)[:, None]
    head_term = my_coef * (reward_head.astype(f32) + token_sum[rows])
    grad_tokens = lm_grad + token_sum[:rows] + jnp.where(row == rows - 1, head_term[None, :], 0.0)

    loss_scale = 1.0 / jnp.sqrt(f32(rows * 2 * n_yl))
    tok_sib = lax.ppermute(tok_half, "co", SWAP)
    low_sib = lax.ppermute(low_half, "co", SWAP)

    def core_parts(value, axis):
        return [
            lax.dynamic_slice_in_dim(value, which * units, units, axis) for which in (core, 1 - core)
        ]

    unit_here, unit_there = core_parts(units_at, 1)
    unit_swap = lax.ppermute(unit_there, "co", SWAP)
    gate_u8 = jnp.concatenate([unit_here[:n_yl], unit_swap[:n_yl]], axis=0)
    up_u8 = jnp.concatenate([unit_here[n_yl:], unit_swap[n_yl:]], axis=0)

    last_tok = jnp.concatenate([ends[:n_yl], ends_sib[:n_yl]], axis=0).astype(f32)
    is_last = jnp.arange(half)[:, None] == jnp.arange(n_yl)[None, :] * rows + rows - 1
    last_tok = (last_tok * coefs[:, None]).astype(bf16)
    head_term8 = (coefs[:, None] * head_vec.astype(f32)).astype(bf16)

    def weight_grad(full, own_right, sib_right, last_left, last_right):
        here, there = core_parts(full, 0)
        from_sib = lax.ppermute(there, "co", SWAP)
        total = lax.optimization_barrier(
            (dot(here, own_right, 1, 0) + dot(from_sib, sib_right, 1, 0)) * loss_scale
        )
        if last_left is None:
            picked = [dot(is_last.astype(bf16), v, 0, 1) for v in (here, from_sib)]
            last_left = jnp.concatenate(picked, axis=0).astype(bf16)
        return total + dot(last_left, last_right, 0, 0) * loss_scale

    grad_gate = weight_grad(gate_g, tok_half, tok_sib, gate_u8, last_tok)
    grad_up = weight_grad(up_g, tok_half, tok_sib, up_u8, last_tok)
    grad_down = weight_grad(hid, low_half, low_sib, None, head_term8)
    return grad_tokens, grad_gate, grad_up, grad_down, rewards


def solution(mesh):
    fine = Mesh(mesh.devices.reshape(4, 2, 8, 2, 4), FINE)
    gx, gz = ("yl", "co"), GZ
    weight = P(("gy",) + gx, gz)
    act = P(gx, gz + ("gy",))
    return jax.shard_map(
        body,
        mesh=fine,
        in_specs=(act, weight, weight, weight, P(gz + ("gy",)), act, P()),
        out_specs=(act, weight, weight, weight, P()),
        check_vma=False,
    )
```

```python
import functools

import jax
import jax.numpy as jnp
from jax import lax
from jax.experimental import pallas as pl
from jax.experimental.pallas import tpu as pltpu
from jax.sharding import Mesh, PartitionSpec as P

SEQ_LEN = 128
reward_weight = 64.0
FINE = ("yl", "co", "gy", "yh", "xx")
PLANE = ("yl", "gy")
GZ = ("yh", "xx")
SWAP = [(0, 1), (1, 0)]
f32, bf16 = jnp.float32, jnp.bfloat16


def exchange(pieces, axes):
    return lax.all_to_all(pieces, axes, 0, 0)


def to_all(value, axes, count):
    return exchange(jnp.broadcast_to(value[None], (count,) + value.shape), axes)


def dot(left, right, left_dim, right_dim):
    return lax.dot_general(
        left, right, (((left_dim,), (right_dim,)), ((), ())), preferred_element_type=f32
    )


def token_products(tok_got, gate_w, up_w, parts, tok, ends):
    n_plane, rows, cols = tok_got.shape
    half, width = tok.shape
    n_gy, n_yl = width // cols, half // rows
    chip_units = parts.shape[0]
    for y in range(n_yl):
        for z in range(n_gy):
            tok[y * rows : (y + 1) * rows, z * cols : (z + 1) * cols] = tok_got[y * n_gy + z]
    last = [tok[(y + 1) * rows - 16 : (y + 1) * rows].astype(f32)[15:] for y in range(n_yl)]
    ends[...] = jnp.concatenate(last + [jnp.zeros((16 - n_yl, width), f32)], axis=0).astype(bf16)
    parts[:, :half] = dot(gate_w[:chip_units], tok[...], 1, 1).astype(bf16)
    parts[:, half:] = dot(up_w[:chip_units], tok[...], 1, 1).astype(bf16)


def cotangent_products(core, low_got, ends, ends_sib, gate_w, up_w, down_w, parts, low, head, wide):
    n_gy, _, cols = low_got.shape
    half, width = low.shape
    n_yl = half // SEQ_LEN
    chip_units = down_w.shape[0]
    for z in range(n_gy):
        at = slice(z * cols, (z + 1) * cols)
        low[:, at] = low_got[z, :half]
        head[:, at] = low_got[z, half:]
    here, there = (ref[...].astype(f32)[:n_yl] for ref in (ends, ends_sib))
    last = [jnp.where(core[0] == 0, here, there), jnp.where(core[0] == 0, there, here)]
    wide[:16] = head[...]
    wide[16:32] = jnp.concatenate(last + [jnp.zeros((16 - 2 * n_yl, width), f32)], axis=0).astype(bf16)
    wide[32:] = jnp.zeros((96, width), bf16)
    parts[:, :half] = dot(down_w[...], low[...], 1, 1).astype(bf16)
    v = dot(down_w[...], wide[...], 1, 1)
    gate = dot(gate_w[:chip_units], wide[...], 1, 1)
    up = pltpu.roll(dot(up_w[:chip_units], wide[...], 1, 1), 16, 1)
    high = v.astype(bf16).astype(f32)
    lane = lax.broadcasted_iota(jnp.int32, v.shape, 1)
    more = jnp.where(lane == 0, high, jnp.where(lane == 1, v - high, 0.0))
    more = jnp.where((lane >= 16) & (lane < 32), gate, jnp.where((lane >= 32) & (lane < 48), up, more))
    parts[:, half:] = more.astype(bf16)


def split_sums(in_two, place, got, keep, give, total):
    own = keep.shape[0]
    sums = got[0].astype(f32)
    for j in range(1, got.shape[0]):
        sums += got[j].astype(f32)
    total[...] = sums
    keep[...] = total[pl.ds(pl.multiple_of(place[0] * own, 8), own), :]
    away = total[pl.ds(pl.multiple_of((1 - place[0]) * own, 8), own), :]
    give[...] = away.astype(bf16)
    if in_two:
        ends = away[:, -128:]
        lost = pltpu.roll(ends - ends.astype(bf16).astype(f32), 1, 1)
        lane = lax.broadcasted_iota(jnp.int32, ends.shape, 1)
        give[:, -128:] = jnp.where(lane == 1, ends + lost, ends).astype(bf16)


def hidden_units(chip_units, place, keep, got, back_keep, back_got, tok_terms, mine):
    own, half = keep.shape[0], keep.shape[1] // 2
    n_seq = half // SEQ_LEN
    sums = keep[...] + got[...].astype(f32)
    back = back_keep[...] + back_got[...].astype(f32)
    gate_sum, up_sum, hidden_grad = sums[:, :half], sums[:, half:], back[:, :half]
    more = back[:, half:]
    head_down = more[:, 0:1] + more[:, 1:2]
    gate_sigmoid = jax.nn.sigmoid(gate_sum)
    silu_gate = gate_sum * gate_sigmoid
    hidden = (silu_gate * up_sum).astype(bf16).astype(f32)
    gate_slope = up_sum * gate_sigmoid * (1.0 + gate_sum * (1.0 - gate_sigmoid))

    row = lax.broadcasted_iota(jnp.int32, (8, half), 0)
    lane = lax.broadcasted_iota(jnp.int32, (8, half), 1)
    blank = jnp.zeros((128 - own, half), f32)

    def picked(value, first):
        pick = (lane == (row - first) * SEQ_LEN + SEQ_LEN - 1) & (row >= first) & (row < first + n_seq)
        value = jnp.concatenate([value * head_down, blank], axis=0).astype(bf16)
        return dot(jnp.where(pick, 1.0, 0.0).astype(bf16), value, 1, 1)

    unit = picked(gate_slope, 0) + picked(silu_gate, n_seq)
    unit = jnp.concatenate([unit, jnp.zeros((8, half - 128), f32)], axis=1)
    unit = pltpu.roll(unit, place[0], 1)

    last_hidden = (more * jax.nn.sigmoid(more) * pltpu.roll(more, 128 - 16, 1)).astype(bf16).astype(f32)
    terms = jnp.sum(last_hidden * head_down, axis=0, keepdims=True) + tok_terms[...]
    for s in range(2 * n_seq):
        rest = jnp.sum(jnp.where(lane[:1, :128] == 16 + s, terms, 0.0), axis=1, keepdims=True)
        for i in range(3):
            piece = rest.astype(bf16).astype(f32)
            unit += jnp.where((row == 0) & (lane == chip_units + 2 * i * n_seq + s), piece, 0.0)
            rest = rest - piece
    rows = jnp.concatenate([hidden_grad * gate_slope, hidden_grad * silu_gate, hidden, unit], axis=0)
    mine[...] = rows.astype(bf16)


def token_gradients(everyone, gate_w, up_w, sent, full):
    width = gate_w.shape[1]
    n_gz, n_rows, half = everyone.shape
    own = (n_rows - 8) // 3
    n_plane, piece_rows, cols = sent.shape
    n_gy, rows = width // cols, piece_rows - 16
    unit = jnp.zeros((8, half), f32)
    for j in range(n_gz):
        block = everyone[j].astype(f32)
        for i in range(2):
            full[i, j * own : (j + 1) * own] = block[i * own : (i + 1) * own]
        unit += block[3 * own :]
    terms = unit + pltpu.roll(unit, half - 8, 1) + pltpu.roll(unit, half - 16, 1)
    terms = pltpu.roll(terms, half - n_gz * own, 1)[:, :cols]
    lane = lax.broadcasted_iota(jnp.int32, terms.shape, 1)
    high = terms.astype(bf16).astype(f32)
    middle = (terms - high).astype(bf16).astype(f32)
    terms = jnp.where(
        lane < 8,
        high,
        jnp.where(lane < 16, pltpu.roll(middle, 8, 1), pltpu.roll(terms - high - middle, 16, 1)),
    )
    terms = jnp.where(lane < 24, terms, 0.0)[:1]
    for i in range(2):
        full[i, n_gz * own :] = jnp.zeros((full.shape[1] - n_gz * own, half), f32)
    unit = unit.astype(bf16)
    gate_t, up_t = (full[i].T.astype(bf16) for i in range(2))
    step = 2 * cols
    for c in range(0, width, step):
        part = dot(gate_t, gate_w[:, c : c + step], 1, 0) + dot(up_t, up_w[:, c : c + step], 1, 0)
        units_here = (
            dot(unit, gate_w[:, c : c + step], 1, 0)[:4] + dot(unit, up_w[:, c : c + step], 1, 0)[4:]
        )
        for z in range(c // cols, (c + step) // cols):
            at = slice(z * cols - c, (z + 1) * cols - c)
            for y in range(n_plane // n_gy):
                piece = y * n_gy + z
                sent[piece, :rows] = part[y * rows : (y + 1) * rows, at].astype(bf16)
                row = lax.broadcasted_iota(jnp.int32, (16, cols), 0)
                extra = jnp.where(row == 0, units_here[y : y + 1, at], jnp.where(row == 1, terms, 0.0))
                sent[piece, rows:] = extra.astype(bf16)


def body(tokens, gate_weight, up_weight, down_weight, reward_head, lm_grad, pair_index):
    n_yl, n_gy = lax.axis_size("yl"), lax.axis_size("gy")
    n_plane, n_gz = n_yl * n_gy, lax.axis_size(GZ)
    rows, cols = tokens.shape
    units, width = gate_weight.shape
    my_seq = lax.axis_index(("yl", "co"))
    core = lax.axis_index("co")

    def core_order(here, there):
        return [jnp.where(core == 0, here, there), jnp.where(core == 0, there, here)]

    def chip_block(weight, padding):
        parts = core_order(weight, lax.ppermute(weight, "co", SWAP))
        return jnp.concatenate(parts + [jnp.zeros((padding, width), bf16)], axis=0)

    padding = -2 * units % 128
    gate_w, up_w = chip_block(gate_weight, padding), chip_block(up_weight, padding)
    down_w = chip_block(down_weight, 0)

    half = n_yl * rows
    low_got = to_all(lm_grad.astype(bf16), "yl", n_yl).reshape(half, cols)
    head_rows = jnp.broadcast_to(reward_head[None, :], (16, cols))
    low_got = jnp.concatenate([low_got, head_rows], axis=0)
    tok_sent = jnp.broadcast_to(tokens[None], (n_plane, rows, cols))
    low_got, tok_sent = lax.optimization_barrier((low_got, tok_sent))
    low_got = lax.all_gather(low_got, "gy")
    tok_got = exchange(tok_sent, PLANE)

    gate_w, up_w, down_w = lax.optimization_barrier((gate_w, up_w, down_w))

    own = 2 * units // n_gz
    whole, scalar = pl.BlockSpec(memory_space=pltpu.VMEM), pl.BlockSpec(memory_space=pltpu.SMEM)
    grant = pltpu.CompilerParams(vmem_limit_bytes=16 * 2**20)
    parts, tok_half, ends = pl.pallas_call(
        token_products,
        out_shape=(
            jax.ShapeDtypeStruct((2 * units, 2 * half), bf16),
            jax.ShapeDtypeStruct((half, width), bf16),
            jax.ShapeDtypeStruct((16, width), bf16),
        ),
        in_specs=[whole] * 3,
        out_specs=(whole,) * 3,
        compiler_params=grant,
        cost_estimate=pl.CostEstimate(
            flops=8 * units * width * half, bytes_accessed=8 * 2**20, transcendentals=0
        ),
        name="token_products",
    )(tok_got, gate_w, up_w)
    ends_sib = lax.ppermute(ends, "co", SWAP)

    n_xx = lax.axis_size("xx")
    first = exchange(parts.reshape(n_xx, 2 * own, 2 * half), "xx")
    y_half = lax.axis_index("yh").astype(jnp.int32)[None]

    def halves(got, in_two):
        lanes = got.shape[2]
        keep, give = pl.pallas_call(
            functools.partial(split_sums, in_two),
            out_shape=(jax.ShapeDtypeStruct((own, lanes), f32), jax.ShapeDtypeStruct((own, lanes), bf16)),
            in_specs=[scalar, whole],
            out_specs=(whole,) * 2,
            scratch_shapes=[pltpu.VMEM((2 * own, lanes), f32)],
            compiler_params=grant,
            cost_estimate=pl.CostEstimate(flops=8 * own * lanes, bytes_accessed=22 * own * lanes, transcendentals=0),
            name="split_sums",
        )(y_half, got)
        return keep, lax.ppermute(give, "yh", SWAP)

    back_parts, low_half, head_vec = pl.pallas_call(
        cotangent_products,
        out_shape=(
            jax.ShapeDtypeStruct((2 * units, half + 128), bf16),
            jax.ShapeDtypeStruct((half, width), bf16),
            jax.ShapeDtypeStruct((16, width), bf16),
        ),
        in_specs=[scalar] + [whole] * 6,
        out_specs=(whole,) * 3,
        scratch_shapes=[pltpu.VMEM((128, width), bf16)],
        compiler_params=grant,
        cost_estimate=pl.CostEstimate(
            flops=4 * units * width * (half + 384), bytes_accessed=5 * 2**20, transcendentals=0
        ),
        name="cotangent_products",
    )(core.astype(jnp.int32)[None], low_got, ends, ends_sib, gate_w, up_w, down_w)
    head_vec = head_vec[:1]
    first, back_parts = lax.optimization_barrier((first, back_parts))
    second = exchange(back_parts.reshape(n_xx, 2 * own, half + 128), "xx")
    sums, sums_got = halves(first, False)
    back, back_got = halves(second, True)

    last_rows = jnp.concatenate(core_order(ends[:n_yl], ends_sib[:n_yl]), axis=0).astype(f32)
    counted = (lax.axis_index("yl") == 0) & (lax.axis_index("gy") == 0)
    tok_terms = jnp.where(counted, jnp.sum(last_rows * head_vec.astype(f32), axis=1), 0.0)
    tok_terms = jnp.pad(tok_terms[None, :], ((0, 0), (16, 112 - 2 * n_yl)))
    place = (lax.axis_index(("xx", "yh")) * own).astype(jnp.int32)[None]
    mine = pl.pallas_call(
        functools.partial(hidden_units, 2 * units),
        out_shape=jax.ShapeDtypeStruct((3 * own + 8, half), bf16),
        in_specs=[scalar] + [whole] * 5,
        out_specs=whole,
        compiler_params=grant,
        cost_estimate=pl.CostEstimate(
            flops=40 * own * half, bytes_accessed=12 * own * half, transcendentals=own * half
        ),
        name="hidden_units",
    )(place, sums, sums_got, back, back_got, tok_terms)
    other = lax.ppermute(mine, "yh", SWAP)
    pair = jnp.stack([jnp.where(y_half == 0, mine, other), jnp.where(y_half == 0, other, mine)])
    everyone = to_all(pair, "xx", n_xx).reshape(n_gz, 3 * own + 8, half)
    sent = pl.pallas_call(
        token_gradients,
        out_shape=jax.ShapeDtypeStruct((n_plane, rows + 16, cols), bf16),
        in_specs=[whole] * 3,
        out_specs=whole,
        scratch_shapes=[pltpu.VMEM((2, 2 * units + padding, half), f32)],
        compiler_params=grant,
        cost_estimate=pl.CostEstimate(
            flops=8 * units * width * half, bytes_accessed=5 * 2**20, transcendentals=0
        ),
        name="token_gradients",
    )(everyone, gate_w, up_w)
    sent, everyone = lax.optimization_barrier((sent, everyone))
    gate_g, up_g, hid = (
        everyone[:, i * own : (i + 1) * own].reshape(2 * units, half) for i in range(3)
    )
    units_at = jnp.sum(everyone[:, 3 * own :, : 2 * units].astype(f32), axis=0).astype(bf16)
    token_sum = jnp.sum(exchange(sent, PLANE).astype(f32), axis=0)

    both = jnp.sum(token_sum[rows + 1, : 6 * n_yl].reshape(3, 2, n_yl), axis=0)
    sequence = jnp.arange(2 * n_yl, dtype=jnp.int32)
    rewards = both.T.reshape(2 * n_yl)
    chosen_hot = (pair_index[:, 0:1] == sequence[None, :]).astype(f32)
    rejected_hot = (pair_index[:, 1:2] == sequence[None, :]).astype(f32)
    margin = jnp.sum((chosen_hot - rejected_hot) * rewards[None, :], axis=1)
    pair_weight = jax.nn.sigmoid(-margin)
    scaled = reward_weight * jnp.sum((rejected_hot - chosen_hot) * pair_weight[:, None], axis=0)
    by_core = scaled.reshape(n_yl, 2)
    core_coefs = jnp.where(core == 0, by_core[:, 0], by_core[:, 1])
    sib_coefs = jnp.where(core == 0, by_core[:, 1], by_core[:, 0])
    coefs = jnp.concatenate([core_coefs, sib_coefs])
    my_coef = jnp.sum(jnp.where(sequence == my_seq, scaled, 0.0))

    row = jnp.arange(rows)[:, None]
    head_term = my_coef * (reward_head.astype(f32) + token_sum[rows])
    grad_tokens = lm_grad + token_sum[:rows] + jnp.where(row == rows - 1, head_term[None, :], 0.0)

    loss_scale = 1.0 / jnp.sqrt(f32(rows * 2 * n_yl))
    tok_sib = lax.ppermute(tok_half, "co", SWAP)
    low_sib = lax.ppermute(low_half, "co", SWAP)

    def core_parts(value, axis):
        return [
            lax.dynamic_slice_in_dim(value, which * units, units, axis) for which in (core, 1 - core)
        ]

    unit_here, unit_there = core_parts(units_at, 1)
    unit_swap = lax.ppermute(unit_there, "co", SWAP)
    gate_u8 = jnp.concatenate([unit_here[:n_yl], unit_swap[:n_yl]], axis=0)
    up_u8 = jnp.concatenate([unit_here[n_yl:], unit_swap[n_yl:]], axis=0)

    last_tok = jnp.concatenate([ends[:n_yl], ends_sib[:n_yl]], axis=0).astype(f32)
    is_last = jnp.arange(half)[:, None] == jnp.arange(n_yl)[None, :] * rows + rows - 1
    last_tok = (last_tok * coefs[:, None]).astype(bf16)
    head_term8 = (coefs[:, None] * head_vec.astype(f32)).astype(bf16)

    def weight_grad(full, own_right, sib_right, last_left, last_right):
        here, there = core_parts(full, 0)
        from_sib = lax.ppermute(there, "co", SWAP)
        total = lax.optimization_barrier(
            (dot(here, own_right, 1, 0) + dot(from_sib, sib_right, 1, 0)) * loss_scale
        )
        if last_left is None:
            picked = [dot(is_last.astype(bf16), v, 0, 1) for v in (here, from_sib)]
            last_left = jnp.concatenate(picked, axis=0).astype(bf16)
        return total + dot(last_left, last_right, 0, 0) * loss_scale

    grad_gate = weight_grad(gate_g, tok_half, tok_sib, gate_u8, last_tok)
    grad_up = weight_grad(up_g, tok_half, tok_sib, up_u8, last_tok)
    grad_down = weight_grad(hid, low_half, low_sib, None, head_term8)
    return grad_tokens, grad_gate, grad_up, grad_down, rewards


def solution(mesh):
    fine = Mesh(mesh.devices.reshape(4, 2, 8, 2, 4), FINE)
    gx, gz = ("yl", "co"), GZ
    weight = P(("gy",) + gx, gz)
    act = P(gx, gz + ("gy",))
    return jax.shard_map(
        body,
        mesh=fine,
        in_specs=(act, weight, weight, weight, P(gz + ("gy",)), act, P()),
        out_specs=(act, weight, weight, weight, P()),
        check_vma=False,
    )
```

```python
import functools

import jax
import jax.numpy as jnp
from jax import lax
from jax.experimental import pallas as pl
from jax.experimental.pallas import tpu as pltpu
from jax.sharding import Mesh, PartitionSpec as P

SEQ_LEN = 128
reward_weight = 64.0
FINE = ("yl", "co", "gy", "yh", "xx")
PLANE = ("yl", "gy")
GZ = ("yh", "xx")
SWAP = [(0, 1), (1, 0)]
f32, bf16 = jnp.float32, jnp.bfloat16


def exchange(pieces, axes):
    return lax.all_to_all(pieces, axes, 0, 0)


def to_all(value, axes, count):
    return exchange(jnp.broadcast_to(value[None], (count,) + value.shape), axes)


def dot(left, right, left_dim, right_dim):
    return lax.dot_general(
        left, right, (((left_dim,), (right_dim,)), ((), ())), preferred_element_type=f32
    )


def token_products(tok_got, gate_w, up_w, parts, tok, ends):
    n_plane, rows, cols = tok_got.shape
    half, width = tok.shape
    n_gy, n_yl = width // cols, half // rows
    chip_units = parts.shape[0]
    for y in range(n_yl):
        for z in range(n_gy):
            tok[y * rows : (y + 1) * rows, z * cols : (z + 1) * cols] = tok_got[y * n_gy + z]
    last = [tok[(y + 1) * rows - 16 : (y + 1) * rows].astype(f32)[15:] for y in range(n_yl)]
    ends[...] = jnp.concatenate(last + [jnp.zeros((16 - n_yl, width), f32)], axis=0).astype(bf16)
    parts[:, :half] = dot(gate_w[:chip_units], tok[...], 1, 1).astype(bf16)
    parts[:, half:] = dot(up_w[:chip_units], tok[...], 1, 1).astype(bf16)


def cotangent_products(core, low_got, ends, ends_sib, gate_w, up_w, down_w, parts, low, head, wide):
    n_gy, _, cols = low_got.shape
    half, width = low.shape
    n_yl = half // SEQ_LEN
    chip_units = down_w.shape[0]
    for z in range(n_gy):
        at = slice(z * cols, (z + 1) * cols)
        low[:, at] = low_got[z, :half]
        head[:, at] = low_got[z, half:]
    here, there = (ref[...].astype(f32)[:n_yl] for ref in (ends, ends_sib))
    last = [jnp.where(core[0] == 0, here, there), jnp.where(core[0] == 0, there, here)]
    wide[:16] = head[...]
    wide[16:32] = jnp.concatenate(last + [jnp.zeros((16 - 2 * n_yl, width), f32)], axis=0).astype(bf16)
    wide[32:] = jnp.zeros((96, width), bf16)
    parts[:, :half] = dot(down_w[...], low[...], 1, 1).astype(bf16)
    v = dot(down_w[...], wide[...], 1, 1)
    gate = dot(gate_w[:chip_units], wide[...], 1, 1)
    up = pltpu.roll(dot(up_w[:chip_units], wide[...], 1, 1), 16, 1)
    high = v.astype(bf16).astype(f32)
    lane = lax.broadcasted_iota(jnp.int32, v.shape, 1)
    more = jnp.where(lane == 0, high, jnp.where(lane == 1, v - high, 0.0))
    more = jnp.where((lane >= 16) & (lane < 32), gate, jnp.where((lane >= 32) & (lane < 48), up, more))
    parts[:, half:] = more.astype(bf16)


def split_sums(in_two, place, got, keep, give, total):
    own = keep.shape[0]
    sums = got[0].astype(f32)
    for j in range(1, got.shape[0]):
        sums += got[j].astype(f32)
    total[...] = sums
    keep[...] = total[pl.ds(pl.multiple_of(place[0] * own, 8), own), :]
    away = total[pl.ds(pl.multiple_of((1 - place[0]) * own, 8), own), :]
    give[...] = away.astype(bf16)
    if in_two:
        ends = away[:, -128:]
        lost = pltpu.roll(ends - ends.astype(bf16).astype(f32), 1, 1)
        lane = lax.broadcasted_iota(jnp.int32, ends.shape, 1)
        give[:, -128:] = jnp.where(lane == 1, ends + lost, ends).astype(bf16)


def hidden_units(chip_units, place, keep, got, back_keep, tok_terms, mine):
    own, half = keep.shape[0], keep.shape[1] // 2
    n_seq = half // SEQ_LEN
    sums = keep[...] + got[:, : 2 * half].astype(f32)
    back = back_keep[...] + got[:, 2 * half :].astype(f32)
    gate_sum, up_sum, hidden_grad = sums[:, :half], sums[:, half:], back[:, :half]
    more = back[:, half:]
    head_down = more[:, 0:1] + more[:, 1:2]
    gate_sigmoid = jax.nn.sigmoid(gate_sum)
    silu_gate = gate_sum * gate_sigmoid
    hidden = (silu_gate * up_sum).astype(bf16).astype(f32)
    gate_slope = up_sum * gate_sigmoid * (1.0 + gate_sum * (1.0 - gate_sigmoid))

    row = lax.broadcasted_iota(jnp.int32, (8, half), 0)
    lane = lax.broadcasted_iota(jnp.int32, (8, half), 1)
    blank = jnp.zeros((128 - own, half), f32)

    def picked(value, first):
        pick = (lane == (row - first) * SEQ_LEN + SEQ_LEN - 1) & (row >= first) & (row < first + n_seq)
        value = jnp.concatenate([value * head_down, blank], axis=0).astype(bf16)
        return dot(jnp.where(pick, 1.0, 0.0).astype(bf16), value, 1, 1)

    unit = picked(gate_slope, 0) + picked(silu_gate, n_seq)
    unit = jnp.concatenate([unit, jnp.zeros((8, half - 128), f32)], axis=1)
    unit = pltpu.roll(unit, place[0], 1)

    last_hidden = (more * jax.nn.sigmoid(more) * pltpu.roll(more, 128 - 16, 1)).astype(bf16).astype(f32)
    terms = jnp.sum(last_hidden * head_down, axis=0, keepdims=True) + tok_terms[...]
    for s in range(2 * n_seq):
        rest = jnp.sum(jnp.where(lane[:1, :128] == 16 + s, terms, 0.0), axis=1, keepdims=True)
        for i in range(3):
            piece = rest.astype(bf16).astype(f32)
            unit += jnp.where((row == 0) & (lane == chip_units + 2 * i * n_seq + s), piece, 0.0)
            rest = rest - piece
    rows = jnp.concatenate([hidden_grad * gate_slope, hidden_grad * silu_gate, hidden, unit], axis=0)
    mine[...] = rows.astype(bf16)


def token_gradients(everyone, gate_w, up_w, sent, full):
    width = gate_w.shape[1]
    n_gz, n_rows, half = everyone.shape
    own = (n_rows - 8) // 3
    n_plane, piece_rows, cols = sent.shape
    n_gy, rows = width // cols, piece_rows - 16
    unit = jnp.zeros((8, half), f32)
    for j in range(n_gz):
        block = everyone[j].astype(f32)
        for i in range(2):
            full[i, j * own : (j + 1) * own] = block[i * own : (i + 1) * own]
        unit += block[3 * own :]
    terms = unit + pltpu.roll(unit, half - 8, 1) + pltpu.roll(unit, half - 16, 1)
    terms = pltpu.roll(terms, half - n_gz * own, 1)[:, :cols]
    lane = lax.broadcasted_iota(jnp.int32, terms.shape, 1)
    high = terms.astype(bf16).astype(f32)
    middle = (terms - high).astype(bf16).astype(f32)
    terms = jnp.where(
        lane < 8,
        high,
        jnp.where(lane < 16, pltpu.roll(middle, 8, 1), pltpu.roll(terms - high - middle, 16, 1)),
    )
    terms = jnp.where(lane < 24, terms, 0.0)[:1]
    for i in range(2):
        full[i, n_gz * own :] = jnp.zeros((full.shape[1] - n_gz * own, half), f32)
    unit = unit.astype(bf16)
    gate_t, up_t = (full[i].T.astype(bf16) for i in range(2))
    step = 2 * cols
    for c in range(0, width, step):
        part = dot(gate_t, gate_w[:, c : c + step], 1, 0) + dot(up_t, up_w[:, c : c + step], 1, 0)
        units_here = (
            dot(unit, gate_w[:, c : c + step], 1, 0)[:4] + dot(unit, up_w[:, c : c + step], 1, 0)[4:]
        )
        for z in range(c // cols, (c + step) // cols):
            at = slice(z * cols - c, (z + 1) * cols - c)
            for y in range(n_plane // n_gy):
                piece = y * n_gy + z
                sent[piece, :rows] = part[y * rows : (y + 1) * rows, at].astype(bf16)
                row = lax.broadcasted_iota(jnp.int32, (16, cols), 0)
                extra = jnp.where(row == 0, units_here[y : y + 1, at], jnp.where(row == 1, terms, 0.0))
                sent[piece, rows:] = extra.astype(bf16)


def body(tokens, gate_weight, up_weight, down_weight, reward_head, lm_grad, pair_index):
    n_yl, n_gy = lax.axis_size("yl"), lax.axis_size("gy")
    n_plane, n_gz = n_yl * n_gy, lax.axis_size(GZ)
    rows, cols = tokens.shape
    units, width = gate_weight.shape
    my_seq = lax.axis_index(("yl", "co"))
    core = lax.axis_index("co")

    def core_order(here, there):
        return [jnp.where(core == 0, here, there), jnp.where(core == 0, there, here)]

    def chip_block(weight, padding):
        parts = core_order(weight, lax.ppermute(weight, "co", SWAP))
        return jnp.concatenate(parts + [jnp.zeros((padding, width), bf16)], axis=0)

    padding = -2 * units % 128
    gate_w, up_w = chip_block(gate_weight, padding), chip_block(up_weight, padding)
    down_w = chip_block(down_weight, 0)

    half = n_yl * rows
    low_got = to_all(lm_grad.astype(bf16), "yl", n_yl).reshape(half, cols)
    head_rows = jnp.broadcast_to(reward_head[None, :], (16, cols))
    low_got = jnp.concatenate([low_got, head_rows], axis=0)
    tok_sent = jnp.broadcast_to(tokens[None], (n_plane, rows, cols))
    low_got, tok_sent = lax.optimization_barrier((low_got, tok_sent))
    low_got = lax.all_gather(low_got, "gy")
    tok_got = exchange(tok_sent, PLANE)

    gate_w, up_w, down_w = lax.optimization_barrier((gate_w, up_w, down_w))

    own = 2 * units // n_gz
    whole, scalar = pl.BlockSpec(memory_space=pltpu.VMEM), pl.BlockSpec(memory_space=pltpu.SMEM)
    grant = pltpu.CompilerParams(vmem_limit_bytes=16 * 2**20)
    parts, tok_half, ends = pl.pallas_call(
        token_products,
        out_shape=(
            jax.ShapeDtypeStruct((2 * units, 2 * half), bf16),
            jax.ShapeDtypeStruct((half, width), bf16),
            jax.ShapeDtypeStruct((16, width), bf16),
        ),
        in_specs=[whole] * 3,
        out_specs=(whole,) * 3,
        compiler_params=grant,
        cost_estimate=pl.CostEstimate(
            flops=8 * units * width * half, bytes_accessed=8 * 2**20, transcendentals=0
        ),
        name="token_products",
    )(tok_got, gate_w, up_w)
    ends_sib = lax.ppermute(ends, "co", SWAP)

    n_xx = lax.axis_size("xx")
    first = exchange(parts.reshape(n_xx, 2 * own, 2 * half), "xx")
    y_half = lax.axis_index("yh").astype(jnp.int32)[None]

    def halves(got, in_two):
        lanes = got.shape[2]
        keep, give = pl.pallas_call(
            functools.partial(split_sums, in_two),
            out_shape=(jax.ShapeDtypeStruct((own, lanes), f32), jax.ShapeDtypeStruct((own, lanes), bf16)),
            in_specs=[scalar, whole],
            out_specs=(whole,) * 2,
            scratch_shapes=[pltpu.VMEM((2 * own, lanes), f32)],
            compiler_params=grant,
            cost_estimate=pl.CostEstimate(flops=8 * own * lanes, bytes_accessed=22 * own * lanes, transcendentals=0),
            name="split_sums",
        )(y_half, got)
        return keep, give

    back_parts, low_half, head_vec = pl.pallas_call(
        cotangent_products,
        out_shape=(
            jax.ShapeDtypeStruct((2 * units, half + 128), bf16),
            jax.ShapeDtypeStruct((half, width), bf16),
            jax.ShapeDtypeStruct((16, width), bf16),
        ),
        in_specs=[scalar] + [whole] * 6,
        out_specs=(whole,) * 3,
        scratch_shapes=[pltpu.VMEM((128, width), bf16)],
        compiler_params=grant,
        cost_estimate=pl.CostEstimate(
            flops=4 * units * width * (half + 384), bytes_accessed=5 * 2**20, transcendentals=0
        ),
        name="cotangent_products",
    )(core.astype(jnp.int32)[None], low_got, ends, ends_sib, gate_w, up_w, down_w)
    head_vec = head_vec[:1]
    first, back_parts = lax.optimization_barrier((first, back_parts))
    second = exchange(back_parts.reshape(n_xx, 2 * own, half + 128), "xx")
    sums, sums_got = halves(first, False)
    back, back_got = halves(second, True)
    both_got = lax.ppermute(jnp.concatenate([sums_got, back_got], axis=1), "yh", SWAP)

    last_rows = jnp.concatenate(core_order(ends[:n_yl], ends_sib[:n_yl]), axis=0).astype(f32)
    counted = (lax.axis_index("yl") == 0) & (lax.axis_index("gy") == 0)
    tok_terms = jnp.where(counted, jnp.sum(last_rows * head_vec.astype(f32), axis=1), 0.0)
    tok_terms = jnp.pad(tok_terms[None, :], ((0, 0), (16, 112 - 2 * n_yl)))
    place = (lax.axis_index(("xx", "yh")) * own).astype(jnp.int32)[None]
    mine = pl.pallas_call(
        functools.partial(hidden_units, 2 * units),
        out_shape=jax.ShapeDtypeStruct((3 * own + 8, half), bf16),
        in_specs=[scalar] + [whole] * 4,
        out_specs=whole,
        compiler_params=grant,
        cost_estimate=pl.CostEstimate(
            flops=40 * own * half, bytes_accessed=12 * own * half, transcendentals=own * half
        ),
        name="hidden_units",
    )(place, sums, both_got, back, tok_terms)
    other = lax.ppermute(mine, "yh", SWAP)
    pair = jnp.stack([jnp.where(y_half == 0, mine, other), jnp.where(y_half == 0, other, mine)])
    everyone = to_all(pair, "xx", n_xx).reshape(n_gz, 3 * own + 8, half)
    sent = pl.pallas_call(
        token_gradients,
        out_shape=jax.ShapeDtypeStruct((n_plane, rows + 16, cols), bf16),
        in_specs=[whole] * 3,
        out_specs=whole,
        scratch_shapes=[pltpu.VMEM((2, 2 * units + padding, half), f32)],
        compiler_params=grant,
        cost_estimate=pl.CostEstimate(
            flops=8 * units * width * half, bytes_accessed=5 * 2**20, transcendentals=0
        ),
        name="token_gradients",
    )(everyone, gate_w, up_w)
    sent, everyone = lax.optimization_barrier((sent, everyone))
    gate_g, up_g, hid = (
        everyone[:, i * own : (i + 1) * own].reshape(2 * units, half) for i in range(3)
    )
    units_at = jnp.sum(everyone[:, 3 * own :, : 2 * units].astype(f32), axis=0).astype(bf16)
    token_sum = jnp.sum(exchange(sent, PLANE).astype(f32), axis=0)

    both = jnp.sum(token_sum[rows + 1, : 6 * n_yl].reshape(3, 2, n_yl), axis=0)
    sequence = jnp.arange(2 * n_yl, dtype=jnp.int32)
    rewards = both.T.reshape(2 * n_yl)
    chosen_hot = (pair_index[:, 0:1] == sequence[None, :]).astype(f32)
    rejected_hot = (pair_index[:, 1:2] == sequence[None, :]).astype(f32)
    margin = jnp.sum((chosen_hot - rejected_hot) * rewards[None, :], axis=1)
    pair_weight = jax.nn.sigmoid(-margin)
    scaled = reward_weight * jnp.sum((rejected_hot - chosen_hot) * pair_weight[:, None], axis=0)
    by_core = scaled.reshape(n_yl, 2)
    core_coefs = jnp.where(core == 0, by_core[:, 0], by_core[:, 1])
    sib_coefs = jnp.where(core == 0, by_core[:, 1], by_core[:, 0])
    coefs = jnp.concatenate([core_coefs, sib_coefs])
    my_coef = jnp.sum(jnp.where(sequence == my_seq, scaled, 0.0))

    row = jnp.arange(rows)[:, None]
    head_term = my_coef * (reward_head.astype(f32) + token_sum[rows])
    grad_tokens = lm_grad + token_sum[:rows] + jnp.where(row == rows - 1, head_term[None, :], 0.0)

    loss_scale = 1.0 / jnp.sqrt(f32(rows * 2 * n_yl))
    tok_sib = lax.ppermute(tok_half, "co", SWAP)
    low_sib = lax.ppermute(low_half, "co", SWAP)

    def core_parts(value, axis):
        return [
            lax.dynamic_slice_in_dim(value, which * units, units, axis) for which in (core, 1 - core)
        ]

    unit_here, unit_there = core_parts(units_at, 1)
    unit_swap = lax.ppermute(unit_there, "co", SWAP)
    gate_u8 = jnp.concatenate([unit_here[:n_yl], unit_swap[:n_yl]], axis=0)
    up_u8 = jnp.concatenate([unit_here[n_yl:], unit_swap[n_yl:]], axis=0)

    last_tok = jnp.concatenate([ends[:n_yl], ends_sib[:n_yl]], axis=0).astype(f32)
    is_last = jnp.arange(half)[:, None] == jnp.arange(n_yl)[None, :] * rows + rows - 1
    last_tok = (last_tok * coefs[:, None]).astype(bf16)
    head_term8 = (coefs[:, None] * head_vec.astype(f32)).astype(bf16)

    def weight_grad(full, own_right, sib_right, last_left, last_right):
        here, there = core_parts(full, 0)
        from_sib = lax.ppermute(there, "co", SWAP)
        total = lax.optimization_barrier(
            (dot(here, own_right, 1, 0) + dot(from_sib, sib_right, 1, 0)) * loss_scale
        )
        if last_left is None:
            picked = [dot(is_last.astype(bf16), v, 0, 1) for v in (here, from_sib)]
            last_left = jnp.concatenate(picked, axis=0).astype(bf16)
        return total + dot(last_left, last_right, 0, 0) * loss_scale

    grad_gate = weight_grad(gate_g, tok_half, tok_sib, gate_u8, last_tok)
    grad_up = weight_grad(up_g, tok_half, tok_sib, up_u8, last_tok)
    grad_down = weight_grad(hid, low_half, low_sib, None, head_term8)
    return grad_tokens, grad_gate, grad_up, grad_down, rewards


def solution(mesh):
    fine = Mesh(mesh.devices.reshape(4, 2, 8, 2, 4), FINE)
    gx, gz = ("yl", "co"), GZ
    weight = P(("gy",) + gx, gz)
    act = P(gx, gz + ("gy",))
    return jax.shard_map(
        body,
        mesh=fine,
        in_specs=(act, weight, weight, weight, P(gz + ("gy",)), act, P()),
        out_specs=(act, weight, weight, weight, P()),
        check_vma=False,
    )
```
